32 devices in a mesh: cuts: 16 (over z, y, x), row: 2 (over core).
Axes of the slice: x: 2, y: 2, z: 4, core: 2. Of those that a mesh axis runs over, the one named last changes fastest.
Arguments:
- starts: float32 [16, 3, 32, 1024], P('cuts', None, 'row'), may hold values from -0.75 to 0.75
- initial: float32 [3, 32, 1024], P(None, 'row'), may hold values from -2.5 to 2.5
- encode_weight: float32 [64, 192], replicated, may hold values from -0.4375 to 0.4375
- decode_weight: float32 [192, 64], replicated, may hold values from -0.75 to 0.75
- latent_rate: float32 [64], replicated, may hold values from 0.5 to 0.995
- coupling: float32 [64, 64], replicated, may hold values from -0.0625 to 0.0625
Outputs:
- next_starts: float32 [16, 3, 32, 1024], P('cuts', None, 'row')
The draws below stay inside these ranges and needn't reach their ends.
All inputs are finite; a program needn't handle non-finite values.
Results may differ from the reference program's by a relative error of at most 0.0001.
Values sent between devices are 32-bit elements; how exact they have to be, the bound alone decides.
No kernel may reach another device: no remote copies, remote signals or barrier semaphores. Data moves between devices by JAX's collectives and lax.ppermute only.
A program may use at most 64 MiB of HBM per device.

```python
import math
import jax
import jax.numpy as jnp
from jax import lax

COLS = 1024
LAT = 64
DOWN = 8
FINE_STEPS = 2
SLICES = 16
ROWS = 32


def draw_starts(key, part):
    key = jax.random.fold_in(key, 11)
    shape = (SLICES, 3, ROWS, COLS)
    values = jnp.clip(0.3 * jax.random.normal(key, shape, jnp.float32), -0.75, 0.75)
    return values


def shard_levels(own_key, dims, split, low, high):
    def one(dim, parts):
        draws = jax.random.uniform(jax.random.fold_in(jax.random.fold_in(own_key, 6), dim), (parts,), jnp.float32, low / len(split), high / len(split))
        return jnp.repeat(jnp.exp(draws), dims[dim] // parts).reshape((-1,) + (1,) * (len(dims) - dim - 1))

    factor_of = one(*split[0])
    for cut in split[1:]:
        factor_of = factor_of * one(*cut)
    return factor_of


def centred(rng, dims, scale, limit, pieces=(), kind=jnp.bfloat16):
    result = scale * jax.random.normal(rng, dims, jnp.float32)
    if pieces:
        result = result * shard_levels(rng, dims, pieces, -0.22, 0.18)
    return jnp.clip(result, -limit, limit).astype(kind)


def setup_inputs(seed: int = 0) -> dict:
    streams_of = jax.random.split(jax.random.key(seed), 7)
    return {
        "starts": draw_starts(jax.random.fold_in(streams_of[6], 71), 0),
        "initial": centred(streams_of[1], (3, ROWS, COLS), 0.3, 2.5, ((1, 2),), jnp.float32),
        "encode_weight": centred(streams_of[2], (LAT, 3 * DOWN * DOWN), (3 * DOWN * DOWN) ** -0.5, 0.4375, (), jnp.float32),
        "decode_weight": centred(streams_of[3], (3 * DOWN * DOWN, LAT), LAT ** -0.5, 0.75, (), jnp.float32),
        "latent_rate": jnp.clip(jnp.exp(jax.random.uniform(streams_of[4], (LAT,), jnp.float32, math.log(0.5), math.log(0.995))), 0.5, 0.995),
        "coupling": centred(streams_of[5], (LAT, LAT), 0.012, 0.0625, (), jnp.float32),
    }


FCOR = 0.3
TSTEP = 0.25


def deriv_cols(field):
    return (8.0 * (jnp.roll(field, -1, -1) - jnp.roll(field, 1, -1)) - (jnp.roll(field, -2, -1) - jnp.roll(field, 2, -1))) / 12.0


def deriv_rows(field):
    return (8.0 * (field[3:-1] - field[1:-3]) - (field[4:] - field[:-4])) / 12.0


def tendency(padded):
    center = padded[:, 2:-2]
    height, along_c, along_r = center[0], center[1], center[2]
    d_height = -(deriv_cols((1.0 + height) * along_c) + deriv_rows((1.0 + padded[0]) * padded[2]))
    d_colvel = -(along_c * deriv_cols(along_c) + along_r * deriv_rows(padded[1])) + FCOR * along_r - deriv_cols(height)
    d_rowvel = -(along_c * deriv_cols(along_r) + along_r * deriv_rows(padded[2])) - FCOR * along_c - deriv_rows(padded[0])
    return jnp.stack([d_height, d_colvel, d_rowvel])


def rk_step(base, grow, shrink):
    first = shrink(base) + TSTEP * tendency(grow(base))
    second = 0.75 * shrink(shrink(base)) + 0.25 * (shrink(first) + TSTEP * tendency(grow(first)))
    third = shrink(shrink(shrink(base))) / 3.0 + (2.0 / 3.0) * (shrink(second) + TSTEP * tendency(grow(second)))
    return third


def encode(weight, state):
    lat = weight.shape[0]
    rows, cols = state.shape[1], state.shape[2]
    blocks = state.reshape(3, rows // DOWN, DOWN, cols // DOWN, DOWN)
    return jnp.einsum("cfpq,fapbq->cab", weight.reshape(lat, 3, DOWN, DOWN), blocks, precision=lax.Precision.HIGHEST)


def decode(weight, latent):
    lat = weight.shape[1]
    out = jnp.einsum("fpqc,cab->fapbq", weight.reshape(3, DOWN, DOWN, lat), latent, precision=lax.Precision.HIGHEST)
    return out.reshape(3, latent.shape[1] * DOWN, latent.shape[2] * DOWN)


def apply_coarse(matrix, latent):
    return jnp.einsum("cd,dab->cab", matrix, latent, precision=lax.Precision.HIGHEST)


def wrap_rows(state):
    return jnp.concatenate([state[:, -2:], state, state[:, :2]], axis=1)


def keep_rows(state):
    return state


def reference(starts, initial, encode_weight, decode_weight, latent_rate, coupling):
    lat = coupling.shape[0]
    coarse = latent_rate[:, None] * (jnp.eye(lat, dtype=jnp.float32) + coupling - coupling.T)

    def advance(state):
        for step in range(FINE_STEPS):
            state = rk_step(state, wrap_rows, keep_rows)
        return state

    finals = lax.map(advance, starts)

    def link(carry, pair):
        carried, previous = carry
        start_state, final_state = pair
        jump = previous - encode(encode_weight, start_state)
        carried = apply_coarse(coarse, carried + jump)
        out = final_state + decode(decode_weight, carried)
        return (carried, encode(encode_weight, final_state)), out

    first_latent = encode(encode_weight, initial)
    init = (jnp.zeros_like(first_latent), first_latent)
    final_carry, next_starts = lax.scan(link, init, (starts, finals))
    return next_starts
```

```python
import functools

import jax
import jax.numpy as jnp
from jax import lax
from jax.experimental import pallas as pl
from jax.experimental.pallas import tpu as pltpu
from jax.sharding import PartitionSpec as P

DOWN = 8
FINE_STEPS = 2
FCOR = 0.3
TSTEP = 0.25
HALO = 6 * FINE_STEPS
LANES = 128
F32 = jnp.float32
BF16 = jnp.bfloat16
VMEM = pl.BlockSpec(memory_space=pltpu.VMEM)


def halves(value):
    high = value.astype(BF16)
    return high, (value - high.astype(F32)).astype(BF16)


def dot3(left, right, contract=((1,), (0,))):
    dims = (contract, ((), ()))
    lh, ll = halves(left)
    rh, rl = halves(right)
    one = functools.partial(lax.dot_general, dimension_numbers=dims, preferred_element_type=F32)
    return one(lh, rh) + (one(lh, rl) + one(ll, rh))


def dot_full(left, right):
    return jnp.dot(left, right, precision=lax.Precision.HIGHEST, preferred_element_type=F32)


def lanes_iota():
    return lax.broadcasted_iota(jnp.int32, (8, LANES), 1)


def split_columns(chunks):
    lane = lanes_iota()
    moved = [c if j == 0 else pltpu.roll(c, j, 1) for j, c in enumerate(chunks)]
    phase = lane & 7
    out = []
    for q in range(8):
        merged = moved[0]
        for j in range(1, 8):
            merged = jnp.where(phase == (q + j) % 8, moved[j], merged)
        place = (8 * (lane & 15) + q + (lane >> 4)) & (LANES - 1)
        out.append(jnp.take_along_axis(merged, place, axis=1))
    return out


def join_columns(parts):
    lane = lanes_iota()
    phase = lane & 7
    picked = []
    for q, part in enumerate(parts):
        j = (lane - q) & 7
        place = 16 * j + (((lane - q - j) & (LANES - 1)) >> 3)
        picked.append(jnp.take_along_axis(part, place, axis=1))
    out = []
    for j in range(8):
        merged = picked[(-j) % 8]
        for q in range(8):
            if q != (-j) % 8:
                merged = jnp.where(phase == (q + j) % 8, picked[q], merged)
        out.append(merged if j == 0 else pltpu.roll(merged, LANES - j, 1))
    return out


def chunks_of(ref, field, row):
    return [ref[field, row : row + 8, LANES * j : LANES * (j + 1)] for j in range(8)]


def encode_split(weight, blocks):
    latent = dot3(weight, jnp.concatenate(blocks, axis=1))
    stacked = jnp.concatenate([latent[:, LANES * a : LANES * (a + 1)] for a in range(len(blocks))], axis=0)
    return stacked.T


def reorder(weight, column_to_row):
    size = weight.shape[1]
    source = lax.broadcasted_iota(jnp.int32, (size, size), 0)
    target = lax.broadcasted_iota(jnp.int32, (size, size), 1)
    perm = (source == column_to_row(target)).astype(F32)
    return dot_full(weight, perm)


def prepare_kernel(steps, starts, initial, enc, dec, rate, coup, own_out, t_out, enc_out, dec_out, *power_outs):
    lat = coup.shape[0]
    groups = starts.shape[1] // DOWN
    first = lax.axis_index("cuts") == 0
    keep = jnp.where(first, 1.0, 0.0).astype(F32)
    weight = reorder(enc[...], lambda k: (k // 64) * 64 + (k % 8) * 8 + (k % 64) // 8)
    enc_out[...] = weight
    blocks = [[] for _ in range(groups)]
    for f in range(3):
        for a in range(groups):
            mine = chunks_of(starts, f, 8 * a)
            given = chunks_of(initial, f, 8 * a)
            mine_split = split_columns(mine)
            for q in range(8):
                own_out[f, q, 8 * a : 8 * a + 8, :] = mine_split[q]
            diff = split_columns([keep * g - m for g, m in zip(given, mine)])
            blocks[a].extend(diff)
    blocks = [jnp.concatenate(b, axis=0) for b in blocks]
    latent = encode_split(weight, blocks)
    eye = (
        lax.broadcasted_iota(jnp.int32, (lat, lat), 0) == lax.broadcasted_iota(jnp.int32, (lat, lat), 1)
    ).astype(F32)
    coupling = coup[...]
    coarse_t = rate[...] * (eye + coupling.T - coupling)
    zero = jnp.zeros((lat, lat), F32)
    rows = []
    for a in range(groups):
        rows.append(jnp.concatenate([coarse_t if b == a else zero for b in range(groups)], axis=1))
    block = jnp.concatenate(rows, axis=0)
    t_out[...] = dot3(latent, block)
    base = block
    for k, out in enumerate(power_outs):
        out[...] = base
        if k + 1 < len(power_outs):
            base = dot_full(base, base)
    size = dec.shape[0]
    source = lax.broadcasted_iota(jnp.int32, (size, size), 1)
    target = lax.broadcasted_iota(jnp.int32, (size, size), 0)
    perm = (source == ((target % 24) // 8) * 64 + (target % 8) * 8 + target // 24).astype(F32)
    dec_out[...] = dot_full(perm, dec[...])


class Padded:
    def __init__(self, ref, reps):
        self.ref = ref
        self.reps = reps

    def put(self, field, r, q, value, rows=True, cols=True):
        ref, reps = self.ref, self.reps
        ref[field, r + 2, q + 2] = value
        if rows and r < 2:
            ref[field, r + reps + 2, q + 2] = pltpu.roll(value, 7, 0)
        if rows and r >= reps - 2:
            ref[field, r - reps + 2, q + 2] = pltpu.roll(value, 1, 0)
        if cols and q < 2:
            ref[field, r + 2, q + 10] = pltpu.roll(value, LANES - 1, 1)
        if cols and q >= 6:
            ref[field, r + 2, q - 6] = pltpu.roll(value, 1, 1)

    def put_cell(self, r, q, height, along_c, along_r):
        self.put(0, r, q, height)
        self.put(1, r, q, along_c)
        self.put(2, r, q, along_r)
        self.put(3, r, q, along_r + height * along_r, cols=False)
        self.put(4, r, q, along_c + height * along_c, rows=False)

    def cell(self, field, r, q):
        return self.ref[field, r + 2, q + 2]

    def along_cols(self, field, r, q):
        at = self.cell
        return 8.0 * (at(field, r, q + 1) - at(field, r, q - 1)) - (at(field, r, q + 2) - at(field, r, q - 2))

    def along_rows(self, field, r, q):
        at = self.cell
        return 8.0 * (at(field, r + 1, q) - at(field, r - 1, q)) - (at(field, r + 2, q) - at(field, r - 2, q))


def stage(base, now, reps, alpha, beta, gamma, put):
    for r in range(reps):
        for q in range(8):
            height, along_c, along_r = (now.cell(f, r, q) for f in range(3))
            scale = gamma / 12.0
            d_height = now.along_cols(4, r, q) + now.along_rows(3, r, q)
            d_colvel = along_c * now.along_cols(1, r, q) + along_r * now.along_rows(1, r, q) + now.along_cols(0, r, q)
            d_rowvel = along_c * now.along_cols(2, r, q) + along_r * now.along_rows(2, r, q) + now.along_rows(0, r, q)
            new = []
            turn = gamma * FCOR
            for f, (mine, d, extra) in enumerate(
                ((height, d_height, None), (along_c, d_colvel, turn * along_r), (along_r, d_rowvel, -turn * along_c))
            ):
                total = beta * mine if beta != 1.0 else mine
                if alpha:
                    total = total + alpha * base.cell(f, r, q)
                if extra is not None:
                    total = total + extra
                new.append(total - scale * d)
            put(r, q, *new)


def fine_kernel(own, other, t_in, weight, finals_out, g_out, rows_buf, buf_a, buf_b, buf_c):
    local_rows = own.shape[2]
    ext = local_rows + other.shape[1]
    reps = ext // 8
    groups = local_rows // DOWN
    for f in range(3):
        for q in range(8):
            rows_buf[f, q, 0:local_rows, :] = own[f, q, :, :]
        for tile in range(other.shape[1] // 8):
            parts = split_columns(chunks_of(other, f, 8 * tile))
            for q in range(8):
                rows_buf[f, q, local_rows + 8 * tile : local_rows + 8 * tile + 8, :] = parts[q]
    state, second, third = Padded(buf_a, reps), Padded(buf_b, reps), Padded(buf_c, reps)
    for r in range(reps):
        for q in range(8):
            state.put_cell(r, q, *(rows_buf[f, q, pl.ds(r, 8, stride=reps), :] for f in range(3)))

    def finish(r, q, *cells):
        for f in range(3):
            rows_buf[f, q, pl.ds(r, 8, stride=reps), :] = cells[f]

    for step in range(FINE_STEPS):
        stage(None, state, reps, 0.0, 1.0, TSTEP, second.put_cell)
        stage(state, second, reps, 0.75, 0.25, 0.25 * TSTEP, third.put_cell)
        last = step + 1 == FINE_STEPS
        stage(state, third, reps, 1.0 / 3.0, 2.0 / 3.0, 2.0 / 3.0 * TSTEP, finish if last else state.put_cell)
    blocks = []
    for a in range(groups):
        parts = []
        for f in range(3):
            for q in range(8):
                part = rows_buf[f, q, 8 * a : 8 * a + 8, :]
                finals_out[f, q, 8 * a : 8 * a + 8, :] = part
                parts.append(part)
        blocks.append(jnp.concatenate(parts, axis=0))
    g_out[...] = encode_split(weight[...], blocks) + t_in[...]


def delayed(value, rows):
    size = value.shape[0]
    if rows % 8 == 0:
        return jnp.concatenate([jnp.zeros((rows, value.shape[1]), F32), value[: size - rows]], axis=0)
    place = lax.broadcasted_iota(jnp.int32, value.shape, 0)
    return jnp.where(place >= rows, pltpu.roll(value, rows, 0), 0.0)


def scan_kernel(width, g_in, *rest):
    powers, out = rest[:-1], rest[-1]
    total = g_in[...]
    total = dot3(delayed(total, width), powers[0][...])
    for k, power in enumerate(powers):
        total = total + dot3(delayed(total, width << k), power[...])
    out[...] = total


def output_kernel(finals, s_in, t_in, weight, out):
    groups = finals.shape[2] // DOWN
    lat = weight.shape[1]
    carried = (s_in[...] + t_in[...]).T
    latent = jnp.concatenate([carried[lat * a : lat * (a + 1)] for a in range(groups)], axis=1)
    change = dot3(weight[...], latent)
    for a in range(groups):
        for f in range(3):
            parts = [
                finals[f, q, 8 * a : 8 * a + 8, :]
                + change[24 * q + 8 * f : 24 * q + 8 * f + 8, LANES * a : LANES * (a + 1)]
                for q in range(8)
            ]
            for j, chunk in enumerate(join_columns(parts)):
                out[0, f, 8 * a : 8 * a + 8, LANES * j : LANES * (j + 1)] = chunk


def call(kernel, shapes, inputs, scratch=(), flops=0):
    return pl.pallas_call(
        kernel,
        out_shape=[jax.ShapeDtypeStruct(s, F32) for s in shapes],
        in_specs=[VMEM] * len(inputs),
        out_specs=[VMEM] * len(shapes),
        scratch_shapes=list(scratch),
        compiler_params=pltpu.CompilerParams(vmem_limit_bytes=40 * 1024 * 1024),
        cost_estimate=pl.CostEstimate(
            flops=flops, bytes_accessed=sum(4 * x.size for x in inputs), transcendentals=0
        ),
    )(*inputs)


def neighbour_rows(state):
    count = lax.axis_size("row")
    rows = state.shape[1]
    if count == 1:
        return jnp.concatenate([state[:, :HALO], state[:, rows - HALO :]], axis=1)
    forward = [(i, (i + 1) % count) for i in range(count)]
    backward = [((i + 1) % count, i) for i in range(count)]
    if count == 2 and rows <= 2 * HALO:
        return lax.ppermute(state, "row", forward)
    below = lax.ppermute(state[:, :HALO], "row", backward)
    above = lax.ppermute(state[:, rows - HALO :], "row", forward)
    return jnp.concatenate([below, above], axis=1)


def local(starts, initial, encode_weight, decode_weight, latent_rate, coupling):
    lat = coupling.shape[0]
    state = starts[0]
    rows = state.shape[1]
    groups = rows // DOWN
    wide = groups * lat
    slices = lax.axis_size("cuts")
    steps = max(1, (slices - 1).bit_length())
    other = neighbour_rows(state)
    split = (3, 8, rows, LANES)
    own, t_part, enc, dec, *powers = call(
        functools.partial(prepare_kernel, steps),
        [split, (LANES, wide), encode_weight.shape, decode_weight.shape] + [(wide, wide)] * steps,
        [state, initial, encode_weight, decode_weight, latent_rate.reshape(1, lat), coupling],
        flops=200_000_000,
    )
    reps = (rows + other.shape[1]) // 8
    pad = pltpu.VMEM((5, reps + 4, 12, 8, LANES), F32)
    finals, g_part = call(
        fine_kernel,
        [split, (LANES, wide)],
        [own, other, t_part, enc],
        [pltpu.VMEM((3, 8, 8 * reps, LANES), F32), pad, pad, pad],
        flops=400_000_000,
    )
    width = LANES // slices
    sent = lax.all_to_all(g_part.reshape(slices, width, wide), "cuts", 0, 0)
    (sums,) = call(
        functools.partial(scan_kernel, width), [(LANES, wide)], [sent.reshape(LANES, wide), *powers], flops=50_000_000
    )
    back = lax.all_to_all(sums.reshape(slices, width, wide), "cuts", 0, 0)
    (out,) = call(
        output_kernel, [(1, 3, rows, starts.shape[3])], [finals, back.reshape(LANES, wide), t_part, dec], flops=50_000_000
    )
    return out


def solution(mesh):
    return jax.shard_map(
        local,
        mesh=mesh,
        in_specs=(P("cuts", None, "row", None), P(None, "row", None), P(), P(), P(), P()),
        out_specs=P("cuts", None, "row", None),
        check_vma=False,
    )
```

```python
import functools

import jax
import jax.numpy as jnp
from jax import lax
from jax.experimental import pallas as pl
from jax.experimental.pallas import tpu as pltpu
from jax.sharding import PartitionSpec as P

DOWN = 8
FINE_STEPS = 2
FCOR = 0.3
TSTEP = 0.25
HALO = 6 * FINE_STEPS
LANES = 128
F32 = jnp.float32
BF16 = jnp.bfloat16
VMEM = pl.BlockSpec(memory_space=pltpu.VMEM)


def halves(value):
    high = value.astype(BF16)
    return high, (value - high.astype(F32)).astype(BF16)


def dot3(left, right, contract=((1,), (0,))):
    dims = (contract, ((), ()))
    lh, ll = halves(left)
    rh, rl = halves(right)
    one = functools.partial(lax.dot_general, dimension_numbers=dims, preferred_element_type=F32)
    return one(lh, rh) + (one(lh, rl) + one(ll, rh))


def dot_full(left, right):
    return jnp.dot(left, right, precision=lax.Precision.HIGHEST, preferred_element_type=F32)


def lanes_iota():
    return lax.broadcasted_iota(jnp.int32, (8, LANES), 1)


def split_columns(chunks):
    lane = lanes_iota()
    moved = [c if j == 0 else pltpu.roll(c, j, 1) for j, c in enumerate(chunks)]
    phase = lane & 7
    out = []
    for q in range(8):
        merged = moved[0]
        for j in range(1, 8):
            merged = jnp.where(phase == (q + j) % 8, moved[j], merged)
        place = (8 * (lane & 15) + q + (lane >> 4)) & (LANES - 1)
        out.append(jnp.take_along_axis(merged, place, axis=1))
    return out


def join_columns(parts):
    lane = lanes_iota()
    phase = lane & 7
    picked = []
    for q, part in enumerate(parts):
        j = (lane - q) & 7
        place = 16 * j + (((lane - q - j) & (LANES - 1)) >> 3)
        picked.append(jnp.take_along_axis(part, place, axis=1))
    out = []
    for j in range(8):
        merged = picked[(-j) % 8]
        for q in range(8):
            if q != (-j) % 8:
                merged = jnp.where(phase == (q + j) % 8, picked[q], merged)
        out.append(merged if j == 0 else pltpu.roll(merged, LANES - j, 1))
    return out


def chunks_of(ref, field, row):
    return [ref[field, row : row + 8, LANES * j : LANES * (j + 1)] for j in range(8)]


def encode_split(weight, blocks):
    latent = dot3(weight, jnp.concatenate(blocks, axis=1))
    stacked = jnp.concatenate([latent[:, LANES * a : LANES * (a + 1)] for a in range(len(blocks))], axis=0)
    return stacked.T


def reorder(weight, column_to_row):
    size = weight.shape[1]
    source = lax.broadcasted_iota(jnp.int32, (size, size), 0)
    target = lax.broadcasted_iota(jnp.int32, (size, size), 1)
    perm = (source == column_to_row(target)).astype(F32)
    return dot_full(weight, perm)


def identity(size):
    rows = lax.broadcasted_iota(jnp.int32, (size, size), 0)
    return (rows == lax.broadcasted_iota(jnp.int32, (size, size), 1)).astype(F32)


def diagonal(block, count):
    zero = jnp.zeros_like(block)
    rows = [jnp.concatenate([block if b == a else zero for b in range(count)], axis=1) for a in range(count)]
    return jnp.concatenate(rows, axis=0)


def prepare_kernel(inner, outer, *refs):
    inputs, (own_out, t_out, enc_out, dec_out, near_out, far_out) = refs[:6], refs[6:12]
    held, sems = refs[12:18], refs[18]
    copies = [pltpu.make_async_copy(src, dst, sems.at[i]) for i, (src, dst) in enumerate(zip(inputs, held))]
    for copy in copies:
        copy.start()
    starts, initial, enc, dec, rate, coup = held
    for copy in copies:
        copy.wait()
    lat = coup.shape[0]
    groups = starts.shape[1] // DOWN
    first = lax.axis_index("cuts") == 0
    keep = jnp.where(first, 1.0, 0.0).astype(F32)
    weight = reorder(enc[...], lambda k: (k // 64) * 64 + (k % 8) * 8 + (k % 64) // 8)
    enc_out[...] = weight
    blocks = [[] for _ in range(groups)]
    for f in range(3):
        for a in range(groups):
            mine = chunks_of(starts, f, 8 * a)
            given = chunks_of(initial, f, 8 * a)
            mine_split = split_columns(mine)
            for q in range(8):
                own_out[f, q, 8 * a : 8 * a + 8, :] = mine_split[q]
            diff = split_columns([keep * g - m for g, m in zip(given, mine)])
            blocks[a].extend(diff)
    blocks = [jnp.concatenate(b, axis=0) for b in blocks]
    latent = encode_split(weight, blocks)
    coupling = coup[...]
    coarse_t = rate[...] * (identity(lat) + coupling.T - coupling)
    t_out[...] = dot3(latent, diagonal(coarse_t, groups))
    power = identity(lat)
    wide = groups * lat
    for k in range(inner):
        near_out[:, wide * k : wide * (k + 1)] = diagonal(power, groups)
        power = coarse_t if k == 0 else dot_full(power, coarse_t)
    step, power = power, coarse_t
    for k in range(max(1, outer - 1)):
        far_out[wide * k : wide * (k + 1), :] = diagonal(power, groups)
        if k + 1 < outer - 1:
            power = dot_full(power, step)
    dec_out[...] = reorder(dec[...], lambda k: ((k % 24) // 8) * 64 + (k % 8) * 8 + k // 24)


class Padded:
    def __init__(self, ref, reps):
        self.ref = ref
        self.reps = reps

    def put(self, field, r, q, value, rows=True, cols=True):
        ref, reps = self.ref, self.reps
        ref[field, r + 2, q + 2] = value
        if rows and r < 2:
            ref[field, r + reps + 2, q + 2] = pltpu.roll(value, 7, 0)
        if rows and r >= reps - 2:
            ref[field, r - reps + 2, q + 2] = pltpu.roll(value, 1, 0)
        if cols and q < 2:
            ref[field, r + 2, q + 10] = pltpu.roll(value, LANES - 1, 1)
        if cols and q >= 6:
            ref[field, r + 2, q - 6] = pltpu.roll(value, 1, 1)

    def put_cell(self, r, q, height, along_c, along_r):
        self.put(0, r, q, height)
        self.put(1, r, q, along_c)
        self.put(2, r, q, along_r)
        self.put(3, r, q, along_r + height * along_r, cols=False)
        self.put(4, r, q, along_c + height * along_c, rows=False)

    def cell(self, field, r, q):
        return self.ref[field, r + 2, q + 2]

    def along_cols(self, field, r, q):
        at = self.cell
        return 8.0 * (at(field, r, q + 1) - at(field, r, q - 1)) - (at(field, r, q + 2) - at(field, r, q - 2))

    def along_rows(self, field, r, q):
        at = self.cell
        return 8.0 * (at(field, r + 1, q) - at(field, r - 1, q)) - (at(field, r + 2, q) - at(field, r - 2, q))


def stage(base, now, reps, alpha, beta, gamma, put):
    for r in range(reps):
        for q in range(8):
            height, along_c, along_r = (now.cell(f, r, q) for f in range(3))
            scale = gamma / 12.0
            d_height = now.along_cols(4, r, q) + now.along_rows(3, r, q)
            d_colvel = along_c * now.along_cols(1, r, q) + along_r * now.along_rows(1, r, q) + now.along_cols(0, r, q)
            d_rowvel = along_c * now.along_cols(2, r, q) + along_r * now.along_rows(2, r, q) + now.along_rows(0, r, q)
            new = []
            turn = gamma * FCOR
            for f, (mine, d, extra) in enumerate(
                ((height, d_height, None), (along_c, d_colvel, turn * along_r), (along_r, d_rowvel, -turn * along_c))
            ):
                total = beta * mine if beta != 1.0 else mine
                if alpha:
                    total = total + alpha * base.cell(f, r, q)
                if extra is not None:
                    total = total + extra
                new.append(total - scale * d)
            put(r, q, *new)


def fine_kernel(own, other, t_in, weight, finals_out, g_out, rows_buf, buf_a, buf_b, buf_c):
    local_rows = own.shape[2]
    ext = local_rows + other.shape[1]
    reps = ext // 8
    groups = local_rows // DOWN
    for f in range(3):
        for q in range(8):
            rows_buf[f, q, 0:local_rows, :] = own[f, q, :, :]
        for tile in range(other.shape[1] // 8):
            parts = split_columns(chunks_of(other, f, 8 * tile))
            for q in range(8):
                rows_buf[f, q, local_rows + 8 * tile : local_rows + 8 * tile + 8, :] = parts[q]
    state, second, third = Padded(buf_a, reps), Padded(buf_b, reps), Padded(buf_c, reps)
    for r in range(reps):
        for q in range(8):
            state.put_cell(r, q, *(rows_buf[f, q, pl.ds(r, 8, stride=reps), :] for f in range(3)))

    def finish(r, q, *cells):
        for f in range(3):
            rows_buf[f, q, pl.ds(r, 8, stride=reps), :] = cells[f]

    for step in range(FINE_STEPS):
        stage(None, state, reps, 0.0, 1.0, TSTEP, second.put_cell)
        stage(state, second, reps, 0.75, 0.25, 0.25 * TSTEP, third.put_cell)
        last = step + 1 == FINE_STEPS
        stage(state, third, reps, 1.0 / 3.0, 2.0 / 3.0, 2.0 / 3.0 * TSTEP, finish if last else state.put_cell)
    blocks = []
    for a in range(groups):
        parts = []
        for f in range(3):
            for q in range(8):
                part = rows_buf[f, q, 8 * a : 8 * a + 8, :]
                finals_out[f, q, 8 * a : 8 * a + 8, :] = part
                parts.append(part)
        blocks.append(jnp.concatenate(parts, axis=0))
    g_out[...] = encode_split(weight[...], blocks) + t_in[...]


def totals_kernel(copies, g_in, near, out):
    count, width, wide = g_in.shape
    total = g_in[count - 1]
    for j in range(count - 1):
        k = count - 1 - j
        total = total + dot3(g_in[j], near[:, wide * k : wide * (k + 1)])
    for z in range(copies):
        out[z] = total


def sums_kernel(g_in, totals, near, far, out):
    count, width, wide = g_in.shape
    groups = totals.shape[0]
    group = lax.axis_index("cuts") // count
    carry = jnp.zeros((width, wide), F32)
    for k in range(groups - 1):
        earlier = group - 1 - k
        taken = totals[jnp.maximum(earlier, 0)]
        carry = carry + dot3(jnp.where(earlier >= 0, taken, 0.0), far[wide * k : wide * (k + 1), :])
    lifted = dot3(carry, near[...])
    for j in range(count):
        total = lifted[:, wide * j : wide * (j + 1)]
        for i in range(j):
            k = j - i
            total = total + dot3(g_in[i], near[:, wide * k : wide * (k + 1)])
        out[j] = total


def output_kernel(finals, s_in, t_in, weight, out):
    groups = finals.shape[2] // DOWN
    lat = weight.shape[0]
    carried = (s_in[...] + t_in[...]).T
    latent = jnp.concatenate([carried[lat * a : lat * (a + 1)] for a in range(groups)], axis=1)
    change = dot3(weight[...], latent, ((0,), (0,)))
    for a in range(groups):
        for f in range(3):
            parts = [
                finals[f, q, 8 * a : 8 * a + 8, :]
                + change[24 * q + 8 * f : 24 * q + 8 * f + 8, LANES * a : LANES * (a + 1)]
                for q in range(8)
            ]
            for j, chunk in enumerate(join_columns(parts)):
                out[0, f, 8 * a : 8 * a + 8, LANES * j : LANES * (j + 1)] = chunk


def call(kernel, shapes, inputs, scratch=(), flops=0, space=pltpu.VMEM, limit=40):
    return pl.pallas_call(
        kernel,
        out_shape=[jax.ShapeDtypeStruct(s, F32) for s in shapes],
        in_specs=[pl.BlockSpec(memory_space=space)] * len(inputs),
        out_specs=[VMEM] * len(shapes),
        scratch_shapes=list(scratch),
        compiler_params=pltpu.CompilerParams(vmem_limit_bytes=limit * 1024 * 1024),
        cost_estimate=pl.CostEstimate(
            flops=flops, bytes_accessed=sum(4 * x.size for x in inputs), transcendentals=0
        ),
    )(*inputs)


def neighbour_rows(state):
    count = lax.axis_size("row")
    rows = state.shape[1]
    if count == 1:
        return jnp.concatenate([state[:, :HALO], state[:, rows - HALO :]], axis=1)
    forward = [(i, (i + 1) % count) for i in range(count)]
    backward = [((i + 1) % count, i) for i in range(count)]
    if count == 2 and rows <= 2 * HALO:
        return lax.ppermute(state, "row", forward)
    below = lax.ppermute(state[:, :HALO], "row", backward)
    above = lax.ppermute(state[:, rows - HALO :], "row", forward)
    return jnp.concatenate([below, above], axis=1)


def local(starts, initial, encode_weight, decode_weight, latent_rate, coupling):
    lat = coupling.shape[0]
    state = starts[0]
    rows = state.shape[1]
    groups = rows // DOWN
    wide = groups * lat
    slices = lax.axis_size("cuts")
    inner = 1 << (slices.bit_length() // 2)
    outer = slices // inner
    other = neighbour_rows(state)
    split = (3, 8, rows, LANES)
    given = [state, initial, encode_weight, decode_weight.T, latent_rate.reshape(1, lat), coupling]
    own, t_part, enc, dec, near, far = call(
        functools.partial(prepare_kernel, inner, outer),
        [split, (LANES, wide), encode_weight.shape, encode_weight.shape]
        + [(wide, inner * wide), (max(1, outer - 1) * wide, wide)],
        given,
        [pltpu.VMEM(x.shape, F32) for x in given] + [pltpu.SemaphoreType.DMA((len(given),))],
        flops=200_000_000,
        space=pl.ANY,
        limit=60,
    )
    reps = (rows + other.shape[1]) // 8
    pad = pltpu.VMEM((5, reps + 4, 12, 8, LANES), F32)
    finals, g_part = call(
        fine_kernel,
        [split, (LANES, wide)],
        [own, other, t_part, enc],
        [pltpu.VMEM((3, 8, 8 * reps, LANES), F32), pad, pad, pad],
        flops=400_000_000,
    )
    width = LANES // inner
    near_groups = [[inner * z + i for i in range(inner)] for z in range(outer)]
    far_groups = [[inner * z + i for z in range(outer)] for i in range(inner)]
    mine = lax.all_to_all(g_part.reshape(inner, width, wide), "cuts", 0, 0, axis_index_groups=near_groups)
    (total,) = call(functools.partial(totals_kernel, outer), [(outer, width, wide)], [mine, near], flops=50_000_000)
    totals = lax.all_to_all(total, "cuts", 0, 0, axis_index_groups=far_groups)
    (sums,) = call(sums_kernel, [(inner, width, wide)], [mine, totals, near, far], flops=50_000_000)
    back = lax.all_to_all(sums, "cuts", 0, 0, axis_index_groups=near_groups)
    (out,) = call(
        output_kernel, [(1, 3, rows, starts.shape[3])], [finals, back.reshape(LANES, wide), t_part, dec], flops=50_000_000
    )
    return out


def solution(mesh):
    return jax.shard_map(
        local,
        mesh=mesh,
        in_specs=(P("cuts", None, "row", None), P(None, "row", None), P(), P(), P(), P()),
        out_specs=P("cuts", None, "row", None),
        check_vma=False,
    )
```

```python
import functools

import jax
import jax.numpy as jnp
from jax import lax
from jax.experimental import pallas as pl
from jax.experimental.pallas import tpu as pltpu
from jax.sharding import PartitionSpec as P

DOWN = 8
FINE_STEPS = 2
FCOR = 0.3
TSTEP = 0.25
HALO = 6 * FINE_STEPS
LANES = 128
F32 = jnp.float32
BF16 = jnp.bfloat16
VMEM = pl.BlockSpec(memory_space=pltpu.VMEM)


def halves(value):
    high = value.astype(BF16)
    return high, (value - high.astype(F32)).astype(BF16)


def dot3(left, right, contract=((1,), (0,))):
    dims = (contract, ((), ()))
    lh, ll = halves(left)
    rh, rl = halves(right)
    one = functools.partial(lax.dot_general, dimension_numbers=dims, preferred_element_type=F32)
    return one(lh, rh) + (one(lh, rl) + one(ll, rh))


def dot_full(left, right):
    return jnp.dot(left, right, precision=lax.Precision.HIGHEST, preferred_element_type=F32)


def lanes_iota():
    return lax.broadcasted_iota(jnp.int32, (8, LANES), 1)


def split_columns(chunks):
    lane = lanes_iota()
    moved = [c if j == 0 else pltpu.roll(c, j, 1) for j, c in enumerate(chunks)]
    phase = lane & 7
    out = []
    for q in range(8):
        merged = moved[0]
        for j in range(1, 8):
            merged = jnp.where(phase == (q + j) % 8, moved[j], merged)
        place = (8 * (lane & 15) + q + (lane >> 4)) & (LANES - 1)
        out.append(jnp.take_along_axis(merged, place, axis=1))
    return out


def join_columns(parts):
    lane = lanes_iota()
    phase = lane & 7
    picked = []
    for q, part in enumerate(parts):
        j = (lane - q) & 7
        place = 16 * j + (((lane - q - j) & (LANES - 1)) >> 3)
        picked.append(jnp.take_along_axis(part, place, axis=1))
    out = []
    for j in range(8):
        merged = picked[(-j) % 8]
        for q in range(8):
            if q != (-j) % 8:
                merged = jnp.where(phase == (q + j) % 8, picked[q], merged)
        out.append(merged if j == 0 else pltpu.roll(merged, LANES - j, 1))
    return out


def chunks_of(ref, field, row):
    return [ref[field, row : row + 8, LANES * j : LANES * (j + 1)] for j in range(8)]


def encode_split(weight, blocks):
    latent = dot3(weight, jnp.concatenate(blocks, axis=1))
    stacked = jnp.concatenate([latent[:, LANES * a : LANES * (a + 1)] for a in range(len(blocks))], axis=0)
    return stacked.T


def reorder(weight, column_to_row):
    size = weight.shape[1]
    source = lax.broadcasted_iota(jnp.int32, (size, size), 0)
    target = lax.broadcasted_iota(jnp.int32, (size, size), 1)
    perm = (source == column_to_row(target)).astype(F32)
    return dot_full(weight, perm)


def identity(size):
    rows = lax.broadcasted_iota(jnp.int32, (size, size), 0)
    return (rows == lax.broadcasted_iota(jnp.int32, (size, size), 1)).astype(F32)


def diagonal(block, count):
    zero = jnp.zeros_like(block)
    rows = [jnp.concatenate([block if b == a else zero for b in range(count)], axis=1) for a in range(count)]
    return jnp.concatenate(rows, axis=0)


def prepare_kernel(inner, outer, *refs):
    inside = lax.axis_index("cuts") % inner
    inputs, (own_out, t_out, enc_out, dec_out, near_out, far_out) = refs[:6], refs[6:12]
    held, sems = refs[12:18], refs[18]
    copies = [pltpu.make_async_copy(src, dst, sems.at[i]) for i, (src, dst) in enumerate(zip(inputs, held))]
    for copy in copies:
        copy.start()
    starts, initial, enc, dec, rate, coup = held
    for copy in copies:
        copy.wait()
    lat = coup.shape[0]
    groups = starts.shape[1] // DOWN
    first = lax.axis_index("cuts") == 0
    keep = jnp.where(first, 1.0, 0.0).astype(F32)
    weight = reorder(enc[...], lambda k: (k // 64) * 64 + (k % 8) * 8 + (k % 64) // 8)
    enc_out[...] = weight
    blocks = [[] for _ in range(groups)]
    for f in range(3):
        for a in range(groups):
            mine = chunks_of(starts, f, 8 * a)
            given = chunks_of(initial, f, 8 * a)
            mine_split = split_columns(mine)
            for q in range(8):
                own_out[f, q, 8 * a : 8 * a + 8, :] = mine_split[q]
            diff = split_columns([keep * g - m for g, m in zip(given, mine)])
            blocks[a].extend(diff)
    blocks = [jnp.concatenate(b, axis=0) for b in blocks]
    latent = encode_split(weight, blocks)
    coupling = coup[...]
    coarse_t = rate[...] * (identity(lat) + coupling.T - coupling)
    t_out[...] = dot3(latent, diagonal(coarse_t, groups))
    power = identity(lat)
    for k in range(inner):
        near_out[k] = diagonal(power, groups)
        power = coarse_t if k == 0 else dot_full(power, coarse_t)
    step, power = power, coarse_t
    shift = near_out[inside]
    for k in range(max(1, outer - 1)):
        far_out[k] = dot_full(shift, diagonal(power, groups))
        if k + 1 < outer - 1:
            power = dot_full(power, step)
    dec_out[...] = reorder(dec[...], lambda k: ((k % 24) // 8) * 64 + (k % 8) * 8 + k // 24)


class Padded:
    def __init__(self, ref, reps):
        self.ref = ref
        self.reps = reps

    def put(self, field, r, q, value, rows=True, cols=True):
        ref, reps = self.ref, self.reps
        ref[field, r + 2, q + 2] = value
        if rows and r < 2:
            ref[field, r + reps + 2, q + 2] = pltpu.roll(value, 7, 0)
        if rows and r >= reps - 2:
            ref[field, r - reps + 2, q + 2] = pltpu.roll(value, 1, 0)
        if cols and q < 2:
            ref[field, r + 2, q + 10] = pltpu.roll(value, LANES - 1, 1)
        if cols and q >= 6:
            ref[field, r + 2, q - 6] = pltpu.roll(value, 1, 1)

    def put_cell(self, r, q, height, along_c, along_r):
        self.put(0, r, q, height)
        self.put(1, r, q, along_c)
        self.put(2, r, q, along_r)
        self.put(3, r, q, along_r + height * along_r, cols=False)
        self.put(4, r, q, along_c + height * along_c, rows=False)

    def cell(self, field, r, q):
        return self.ref[field, r + 2, q + 2]

    def along_cols(self, field, r, q):
        at = self.cell
        return 8.0 * (at(field, r, q + 1) - at(field, r, q - 1)) - (at(field, r, q + 2) - at(field, r, q - 2))

    def along_rows(self, field, r, q):
        at = self.cell
        return 8.0 * (at(field, r + 1, q) - at(field, r - 1, q)) - (at(field, r + 2, q) - at(field, r - 2, q))


def stage(base, now, reps, alpha, beta, gamma, put):
    for r in range(reps):
        for q in range(8):
            height, along_c, along_r = (now.cell(f, r, q) for f in range(3))
            scale = gamma / 12.0
            d_height = now.along_cols(4, r, q) + now.along_rows(3, r, q)
            d_colvel = along_c * now.along_cols(1, r, q) + along_r * now.along_rows(1, r, q) + now.along_cols(0, r, q)
            d_rowvel = along_c * now.along_cols(2, r, q) + along_r * now.along_rows(2, r, q) + now.along_rows(0, r, q)
            new = []
            turn = gamma * FCOR
            for f, (mine, d, extra) in enumerate(
                ((height, d_height, None), (along_c, d_colvel, turn * along_r), (along_r, d_rowvel, -turn * along_c))
            ):
                total = beta * mine if beta != 1.0 else mine
                if alpha:
                    total = total + alpha * base.cell(f, r, q)
                if extra is not None:
                    total = total + extra
                new.append(total - scale * d)
            put(r, q, *new)


def fine_kernel(own, other, t_in, weight, finals_out, g_out, rows_buf, buf_a, buf_b, buf_c):
    local_rows = own.shape[2]
    ext = local_rows + other.shape[1]
    reps = ext // 8
    groups = local_rows // DOWN
    for f in range(3):
        for q in range(8):
            rows_buf[f, q, 0:local_rows, :] = own[f, q, :, :]
        for tile in range(other.shape[1] // 8):
            parts = split_columns(chunks_of(other, f, 8 * tile))
            for q in range(8):
                rows_buf[f, q, local_rows + 8 * tile : local_rows + 8 * tile + 8, :] = parts[q]
    state, second, third = Padded(buf_a, reps), Padded(buf_b, reps), Padded(buf_c, reps)
    for r in range(reps):
        for q in range(8):
            state.put_cell(r, q, *(rows_buf[f, q, pl.ds(r, 8, stride=reps), :] for f in range(3)))

    def finish(r, q, *cells):
        for f in range(3):
            rows_buf[f, q, pl.ds(r, 8, stride=reps), :] = cells[f]

    for step in range(FINE_STEPS):
        stage(None, state, reps, 0.0, 1.0, TSTEP, second.put_cell)
        stage(state, second, reps, 0.75, 0.25, 0.25 * TSTEP, third.put_cell)
        last = step + 1 == FINE_STEPS
        stage(state, third, reps, 1.0 / 3.0, 2.0 / 3.0, 2.0 / 3.0 * TSTEP, finish if last else state.put_cell)
    blocks = []
    for a in range(groups):
        parts = []
        for f in range(3):
            for q in range(8):
                part = rows_buf[f, q, 8 * a : 8 * a + 8, :]
                finals_out[f, q, 8 * a : 8 * a + 8, :] = part
                parts.append(part)
        blocks.append(jnp.concatenate(parts, axis=0))
    g_out[...] = encode_split(weight[...], blocks) + t_in[...]


def totals_kernel(*refs):
    parts, near, out = refs[:-2], refs[-2], refs[-1]
    count = len(parts)
    inside = lax.axis_index("cuts") % count
    total = None
    for d, part in enumerate(parts):
        term = dot3(part[...], near[count - 1 - (inside ^ d)])
        total = term if total is None else total + term
    out[...] = total


def earlier_kernel(*refs):
    parts, t_in, near, out = refs[:-3], refs[-3], refs[-2], refs[-1]
    count = len(parts)
    inside = lax.axis_index("cuts") % count
    total = t_in[...]
    for d in range(1, count):
        place = inside ^ d
        taken = jnp.where(place < inside, parts[d][...], 0.0)
        total = total + dot3(taken, near[jnp.maximum(inside - place, 0)])
    out[...] = total


def output_kernel(inner, finals, local_sum, weight, far, *refs):
    totals, out = refs[:-1], refs[-1]
    groups = finals.shape[2] // DOWN
    lat = weight.shape[0]
    group = lax.axis_index("cuts") // inner
    carried = local_sum[...]
    for d in range(1, len(totals) + 1):
        place = group ^ d
        taken = jnp.where(place < group, totals[d - 1][...], 0.0)
        carried = carried + dot3(taken, far[jnp.maximum(group - 1 - place, 0)])
    carried = carried.T
    latent = jnp.concatenate([carried[lat * a : lat * (a + 1)] for a in range(groups)], axis=1)
    change = dot3(weight[...], latent, ((0,), (0,)))
    for a in range(groups):
        for f in range(3):
            parts = [
                finals[f, q, 8 * a : 8 * a + 8, :]
                + change[24 * q + 8 * f : 24 * q + 8 * f + 8, LANES * a : LANES * (a + 1)]
                for q in range(8)
            ]
            for j, chunk in enumerate(join_columns(parts)):
                out[0, f, 8 * a : 8 * a + 8, LANES * j : LANES * (j + 1)] = chunk


def call(kernel, shapes, inputs, scratch=(), flops=0, space=pltpu.VMEM, limit=40):
    return pl.pallas_call(
        kernel,
        out_shape=[jax.ShapeDtypeStruct(s, F32) for s in shapes],
        in_specs=[pl.BlockSpec(memory_space=space)] * len(inputs),
        out_specs=[VMEM] * len(shapes),
        scratch_shapes=list(scratch),
        compiler_params=pltpu.CompilerParams(vmem_limit_bytes=limit * 1024 * 1024),
        cost_estimate=pl.CostEstimate(
            flops=flops, bytes_accessed=sum(4 * x.size for x in inputs), transcendentals=0
        ),
    )(*inputs)


def neighbour_rows(state):
    count = lax.axis_size("row")
    rows = state.shape[1]
    if count == 1:
        return jnp.concatenate([state[:, :HALO], state[:, rows - HALO :]], axis=1)
    forward = [(i, (i + 1) % count) for i in range(count)]
    backward = [((i + 1) % count, i) for i in range(count)]
    if count == 2 and rows <= 2 * HALO:
        return lax.ppermute(state, "row", forward)
    below = lax.ppermute(state[:, :HALO], "row", backward)
    above = lax.ppermute(state[:, rows - HALO :], "row", forward)
    return jnp.concatenate([below, above], axis=1)


def swapped(value, distance):
    return lax.ppermute(value, "cuts", [(i, i ^ distance) for i in range(lax.axis_size("cuts"))])


def local(starts, initial, encode_weight, decode_weight, latent_rate, coupling):
    lat = coupling.shape[0]
    state = starts[0]
    rows = state.shape[1]
    groups = rows // DOWN
    wide = groups * lat
    slices = lax.axis_size("cuts")
    inner = 1 << (slices.bit_length() // 2)
    outer = slices // inner
    other = neighbour_rows(state)
    split = (3, 8, rows, LANES)
    given = [state, initial, encode_weight, decode_weight.T, latent_rate.reshape(1, lat), coupling]
    own, t_part, enc, dec, near, far = call(
        functools.partial(prepare_kernel, inner, outer),
        [split, (LANES, wide), encode_weight.shape, encode_weight.shape]
        + [(inner, wide, wide), (max(1, outer - 1), wide, wide)],
        [pltpu.with_memory_space_constraint(x, pltpu.HBM) for x in given],
        [pltpu.VMEM(x.shape, F32) for x in given] + [pltpu.SemaphoreType.DMA((len(given),))],
        flops=200_000_000,
        space=pl.ANY,
    )
    reps = (rows + other.shape[1]) // 8
    pad = pltpu.VMEM((5, reps + 4, 12, 8, LANES), F32)
    finals, g_part = call(
        fine_kernel,
        [split, (LANES, wide)],
        [own, other, t_part, enc],
        [pltpu.VMEM((3, 8, 8 * reps, LANES), F32), pad, pad, pad],
        flops=400_000_000,
    )
    parts = [g_part] + [swapped(g_part, d) for d in range(1, inner)]
    (total,) = call(totals_kernel, [(LANES, wide)], [*parts, near], flops=50_000_000)
    totals = [swapped(total, inner * d) for d in range(1, outer)]
    (local_sum,) = call(earlier_kernel, [(LANES, wide)], [*parts, t_part, near], flops=50_000_000)
    (out,) = call(
        functools.partial(output_kernel, inner),
        [(1, 3, rows, starts.shape[3])],
        [finals, local_sum, dec, far, *totals],
        flops=50_000_000,
    )
    return out


def solution(mesh):
    return jax.shard_map(
        local,
        mesh=mesh,
        in_specs=(P("cuts", None, "row", None), P(None, "row", None), P(), P(), P(), P()),
        out_specs=P("cuts", None, "row", None),
        check_vma=False,
    )
```

```python
import functools

import jax
import jax.numpy as jnp
from jax import lax
from jax.experimental import pallas as pl
from jax.experimental.pallas import tpu as pltpu
from jax.sharding import PartitionSpec as P

DOWN = 8
FINE_STEPS = 2
FCOR = 0.3
TSTEP = 0.25
HALO = 6 * FINE_STEPS
LANES = 128
F32 = jnp.float32
BF16 = jnp.bfloat16
VMEM = pl.BlockSpec(memory_space=pltpu.VMEM)


def halves(value):
    high = value.astype(BF16)
    return high, (value - high.astype(F32)).astype(BF16)


def dot3(left, right, contract=((1,), (0,))):
    dims = (contract, ((), ()))
    lh, ll = halves(left)
    rh, rl = halves(right)
    one = functools.partial(lax.dot_general, dimension_numbers=dims, preferred_element_type=F32)
    return one(lh, rh) + (one(lh, rl) + one(ll, rh))


def dot_full(left, right):
    return jnp.dot(left, right, precision=lax.Precision.HIGHEST, preferred_element_type=F32)


def lanes_iota():
    return lax.broadcasted_iota(jnp.int32, (8, LANES), 1)


def split_columns(chunks):
    lane = lanes_iota()
    moved = [c if j == 0 else pltpu.roll(c, j, 1) for j, c in enumerate(chunks)]
    phase = lane & 7
    out = []
    for q in range(8):
        merged = moved[0]
        for j in range(1, 8):
            merged = jnp.where(phase == (q + j) % 8, moved[j], merged)
        place = (8 * (lane & 15) + q + (lane >> 4)) & (LANES - 1)
        out.append(jnp.take_along_axis(merged, place, axis=1))
    return out


def join_columns(parts):
    lane = lanes_iota()
    phase = lane & 7
    picked = []
    for q, part in enumerate(parts):
        j = (lane - q) & 7
        place = 16 * j + (((lane - q - j) & (LANES - 1)) >> 3)
        picked.append(jnp.take_along_axis(part, place, axis=1))
    out = []
    for j in range(8):
        merged = picked[(-j) % 8]
        for q in range(8):
            if q != (-j) % 8:
                merged = jnp.where(phase == (q + j) % 8, picked[q], merged)
        out.append(merged if j == 0 else pltpu.roll(merged, LANES - j, 1))
    return out


def chunks_of(ref, field, row):
    return [ref[field, row : row + 8, LANES * j : LANES * (j + 1)] for j in range(8)]


def identity(size):
    rows = lax.broadcasted_iota(jnp.int32, (size, size), 0)
    return (rows == lax.broadcasted_iota(jnp.int32, (size, size), 1)).astype(F32)


def coarse_matrix(rate, coupling):
    return (rate * (identity(coupling.shape[0]) + coupling.T - coupling)).T


def put_blocks(ref, field, group, parts):
    for q, part in enumerate(parts):
        ref[group, pl.ds(64 * field + q, 8, stride=8), :] = part


def side_by_side(ref):
    return jnp.concatenate([ref[a] for a in range(ref.shape[0])], axis=1)


def split_kernel(starts_hbm, initial_hbm, own_out, offset_out, starts, initial, sems):
    copies = [
        pltpu.make_async_copy(starts_hbm, starts, sems.at[0]),
        pltpu.make_async_copy(initial_hbm, initial, sems.at[1]),
    ]
    for copy in copies:
        copy.start()
    keep = jnp.where(lax.axis_index("cuts") == 0, 1.0, 0.0).astype(F32)
    for copy in copies:
        copy.wait()
    for f in range(3):
        for a in range(starts.shape[1] // DOWN):
            mine = chunks_of(starts, f, 8 * a)
            given = chunks_of(initial, f, 8 * a)
            for q, part in enumerate(split_columns(mine)):
                own_out[f, q, 8 * a : 8 * a + 8, :] = part
            put_blocks(offset_out, f, a, split_columns([keep * g - m for g, m in zip(given, mine)]))


def powers_kernel(inner, outer, dec, rate, coup, total_out, near_out, far_out, held):
    lat = coup.shape[0]
    inside = lax.axis_index("cuts") % inner
    coarse = coarse_matrix(rate[...], coup[...])
    powers = [identity(lat), coarse]
    for k in range(2, inner + 1):
        powers.append(dot_full(powers[k // 2], powers[k - k // 2]))
    for k, power in enumerate(powers):
        held[k] = power
    weight = dec[...].T
    decoded = [weight]
    for d in range(1, inner):
        place = inside ^ d
        part = dot_full(weight, held[jnp.maximum(inside - place, 0)])
        decoded.append(jnp.where(place < inside, part, 0.0))
    near_out[...] = jnp.concatenate(decoded, axis=1)
    total_out[...] = jnp.concatenate([held[inner - 1 - (inside ^ d)] for d in range(inner)], axis=1)
    part = dot_full(weight, held[inside + 1])
    later = [part]
    for k in range(2, outer):
        part = dot_full(part, powers[inner])
        later.append(part)
    far_out[...] = jnp.concatenate(later, axis=1)


class Padded:
    def __init__(self, ref, reps):
        self.ref = ref
        self.reps = reps

    def put(self, field, r, q, value, rows=True, cols=True):
        ref, reps = self.ref, self.reps
        ref[field, r + 2, q + 2] = value
        if rows and r < 2:
            ref[field, r + reps + 2, q + 2] = pltpu.roll(value, 7, 0)
        if rows and r >= reps - 2:
            ref[field, r - reps + 2, q + 2] = pltpu.roll(value, 1, 0)
        if cols and q < 2:
            ref[field, r + 2, q + 10] = pltpu.roll(value, LANES - 1, 1)
        if cols and q >= 6:
            ref[field, r + 2, q - 6] = pltpu.roll(value, 1, 1)

    def put_cell(self, r, q, height, along_c, along_r):
        self.put(0, r, q, height)
        self.put(1, r, q, along_c)
        self.put(2, r, q, along_r)
        self.put(3, r, q, along_r + height * along_r, cols=False)
        self.put(4, r, q, along_c + height * along_c, rows=False)

    def cell(self, field, r, q):
        return self.ref[field, r + 2, q + 2]

    def along_cols(self, field, r, q):
        at = self.cell
        return 8.0 * (at(field, r, q + 1) - at(field, r, q - 1)) - (at(field, r, q + 2) - at(field, r, q - 2))

    def along_rows(self, field, r, q):
        at = self.cell
        return 8.0 * (at(field, r + 1, q) - at(field, r - 1, q)) - (at(field, r + 2, q) - at(field, r - 2, q))


def stage(base, now, reps, alpha, beta, gamma, put):
    for r in range(reps):
        for q in range(8):
            height, along_c, along_r = (now.cell(f, r, q) for f in range(3))
            scale = gamma / 12.0
            d_height = now.along_cols(4, r, q) + now.along_rows(3, r, q)
            d_colvel = along_c * now.along_cols(1, r, q) + along_r * now.along_rows(1, r, q) + now.along_cols(0, r, q)
            d_rowvel = along_c * now.along_cols(2, r, q) + along_r * now.along_rows(2, r, q) + now.along_rows(0, r, q)
            new = []
            turn = gamma * FCOR
            for f, (mine, d, extra) in enumerate(
                ((height, d_height, None), (along_c, d_colvel, turn * along_r), (along_r, d_rowvel, -turn * along_c))
            ):
                total = beta * mine if beta != 1.0 else mine
                if alpha:
                    total = total + alpha * base.cell(f, r, q)
                if extra is not None:
                    total = total + extra
                new.append(total - scale * d)
            put(r, q, *new)


def fine_kernel(own, other, offset, enc, rate, coup, finals_out, g_out, t_out, rows_buf, buf_a, buf_b, buf_c):
    local_rows = own.shape[2]
    ext = local_rows + other.shape[1]
    reps = ext // 8
    groups = local_rows // DOWN
    for f in range(3):
        for q in range(8):
            rows_buf[f, q, 0:local_rows, :] = own[f, q, :, :]
        for tile in range(other.shape[1] // 8):
            parts = split_columns(chunks_of(other, f, 8 * tile))
            for q in range(8):
                rows_buf[f, q, local_rows + 8 * tile : local_rows + 8 * tile + 8, :] = parts[q]
    t_part = dot3(coarse_matrix(rate[...], coup[...]), dot3(enc[...], side_by_side(offset)))
    t_out[...] = t_part
    state, second, third = Padded(buf_a, reps), Padded(buf_b, reps), Padded(buf_c, reps)
    for r in range(reps):
        for q in range(8):
            state.put_cell(r, q, *(rows_buf[f, q, pl.ds(r, 8, stride=reps), :] for f in range(3)))

    def finish(r, q, *cells):
        for f in range(3):
            rows_buf[f, q, pl.ds(r, 8, stride=reps), :] = cells[f]

    for step in range(FINE_STEPS):
        stage(None, state, reps, 0.0, 1.0, TSTEP, second.put_cell)
        stage(state, second, reps, 0.75, 0.25, 0.25 * TSTEP, third.put_cell)
        last = step + 1 == FINE_STEPS
        stage(state, third, reps, 1.0 / 3.0, 2.0 / 3.0, 2.0 / 3.0 * TSTEP, finish if last else state.put_cell)
    for f in range(3):
        for a in range(groups):
            put_blocks(finals_out, f, a, [rows_buf[f, q, 8 * a : 8 * a + 8, :] for q in range(8)])
    g_out[...] = dot3(enc[...], side_by_side(finals_out)) + t_part


def weighted_kernel(*refs):
    *parts, weights, out = refs
    out[...] = dot3(weights[...], jnp.concatenate([part[...] for part in parts], axis=0))


def base_kernel(finals, *refs):
    *parts, weights, out = refs
    change = dot3(weights[...], jnp.concatenate([part[...] for part in parts], axis=0))
    for a in range(finals.shape[0]):
        out[a] = finals[a] + change[:, LANES * a : LANES * (a + 1)]


def output_kernel(base, *refs):
    *parts, weights, out, held = refs
    change = dot3(weights[...], jnp.concatenate([part[...] for part in parts], axis=0))
    for a in range(base.shape[0]):
        held[a] = base[a] + change[:, LANES * a : LANES * (a + 1)]
        for f in range(3):
            joined = join_columns([held[a, pl.ds(64 * f + q, 8, stride=8), :] for q in range(8)])
            for j, chunk in enumerate(joined):
                out[0, f, 8 * a : 8 * a + 8, LANES * j : LANES * (j + 1)] = chunk


def call(kernel, shapes, inputs, scratch=(), flops=0, space=pltpu.VMEM, limit=40):
    return pl.pallas_call(
        kernel,
        out_shape=[jax.ShapeDtypeStruct(s, F32) for s in shapes],
        in_specs=[pl.BlockSpec(memory_space=space)] * len(inputs),
        out_specs=[VMEM] * len(shapes),
        scratch_shapes=list(scratch),
        compiler_params=pltpu.CompilerParams(vmem_limit_bytes=limit * 1024 * 1024),
        cost_estimate=pl.CostEstimate(
            flops=flops, bytes_accessed=sum(4 * x.size for x in inputs), transcendentals=0
        ),
    )(*inputs)


def neighbour_rows(state):
    count = lax.axis_size("row")
    rows = state.shape[1]
    if count == 1:
        return jnp.concatenate([state[:, :HALO], state[:, rows - HALO :]], axis=1)
    forward = [(i, (i + 1) % count) for i in range(count)]
    backward = [((i + 1) % count, i) for i in range(count)]
    if count == 2 and rows <= 2 * HALO:
        return lax.ppermute(state, "row", forward)
    below = lax.ppermute(state[:, :HALO], "row", backward)
    above = lax.ppermute(state[:, rows - HALO :], "row", forward)
    return jnp.concatenate([below, above], axis=1)


def swapped(value, distance):
    return lax.ppermute(value, "cuts", [(i, i ^ distance) for i in range(lax.axis_size("cuts"))])


def later(value, distance):
    count = lax.axis_size("cuts")
    return lax.ppermute(value, "cuts", [(i, i + distance) for i in range(count - distance)])


def local(starts, initial, encode_weight, decode_weight, latent_rate, coupling):
    lat = coupling.shape[0]
    state = starts[0]
    rows = state.shape[1]
    groups = rows // DOWN
    wide = groups * LANES
    size = encode_weight.shape[1]
    slices = lax.axis_size("cuts")
    inner = 1 << (slices.bit_length() // 2)
    outer = slices // inner
    rate = latent_rate.reshape(1, lat)
    other = neighbour_rows(state)
    own, offset = call(
        split_kernel,
        [(3, 8, rows, LANES), (groups, size, LANES)],
        [pltpu.with_memory_space_constraint(x, pltpu.HBM) for x in (state, initial)],
        [pltpu.VMEM(state.shape, F32)] * 2 + [pltpu.SemaphoreType.DMA((2,))],
        flops=100_000_000,
        space=pl.ANY,
    )
    reps = (rows + other.shape[1]) // 8
    pad = pltpu.VMEM((5, reps + 4, 12, 8, LANES), F32)
    finals, g_part, t_part = call(
        fine_kernel,
        [(groups, size, LANES), (lat, wide), (lat, wide)],
        [own, other, offset, encode_weight, rate, coupling],
        [pltpu.VMEM((3, 8, 8 * reps, LANES), F32), pad, pad, pad],
        flops=400_000_000,
    )
    parts = [swapped(g_part, d) for d in range(1, inner)]
    to_total, to_near, to_far = call(
        functools.partial(powers_kernel, inner, outer),
        [(lat, inner * lat), (size, inner * lat), (size, max(1, outer - 1) * lat)],
        [decode_weight.T, rate, coupling],
        [pltpu.VMEM((inner + 1, lat, lat), F32)],
        flops=50_000_000,
    )
    (total,) = call(weighted_kernel, [(lat, wide)], [g_part, *parts, to_total], flops=50_000_000)
    totals = [later(total, inner * k) for k in range(1, outer)]
    (base,) = call(base_kernel, [(groups, size, LANES)], [finals, t_part, *parts, to_near], flops=50_000_000)
    (out,) = call(
        output_kernel,
        [(1, 3, rows, starts.shape[3])],
        [base, *totals, to_far],
        [pltpu.VMEM((groups, size, LANES), F32)],
        flops=50_000_000,
    )
    return out


def solution(mesh):
    return jax.shard_map(
        local,
        mesh=mesh,
        in_specs=(P("cuts", None, "row", None), P(None, "row", None), P(), P(), P(), P()),
        out_specs=P("cuts", None, "row", None),
        check_vma=False,
    )
```

```python
import functools

import jax
import jax.numpy as jnp
from jax import lax
from jax.experimental import pallas as pl
from jax.experimental.pallas import tpu as pltpu
from jax.sharding import PartitionSpec as P

DOWN = 8
FINE_STEPS = 2
FCOR = 0.3
TSTEP = 0.25
HALO = 6 * FINE_STEPS
LANES = 128
F32 = jnp.float32
BF16 = jnp.bfloat16
VMEM = pl.BlockSpec(memory_space=pltpu.VMEM)


def halves(value):
    high = value.astype(BF16)
    return high, (value - high.astype(F32)).astype(BF16)


def dot3(left, right, contract=((1,), (0,))):
    dims = (contract, ((), ()))
    lh, ll = halves(left)
    rh, rl = halves(right)
    one = functools.partial(lax.dot_general, dimension_numbers=dims, preferred_element_type=F32)
    return one(lh, rh) + (one(lh, rl) + one(ll, rh))


def dot_full(left, right):
    return jnp.dot(left, right, precision=lax.Precision.HIGHEST, preferred_element_type=F32)


def lanes_iota():
    return lax.broadcasted_iota(jnp.int32, (8, LANES), 1)


def split_columns(chunks):
    lane = lanes_iota()
    moved = [c if j == 0 else pltpu.roll(c, j, 1) for j, c in enumerate(chunks)]
    phase = lane & 7
    out = []
    for q in range(8):
        merged = moved[0]
        for j in range(1, 8):
            merged = jnp.where(phase == (q + j) % 8, moved[j], merged)
        place = (8 * (lane & 15) + q + (lane >> 4)) & (LANES - 1)
        out.append(jnp.take_along_axis(merged, place, axis=1))
    return out


def join_columns(parts):
    lane = lanes_iota()
    phase = lane & 7
    picked = []
    for q, part in enumerate(parts):
        j = (lane - q) & 7
        place = 16 * j + (((lane - q - j) & (LANES - 1)) >> 3)
        picked.append(jnp.take_along_axis(part, place, axis=1))
    out = []
    for j in range(8):
        merged = picked[(-j) % 8]
        for q in range(8):
            if q != (-j) % 8:
                merged = jnp.where(phase == (q + j) % 8, picked[q], merged)
        out.append(merged if j == 0 else pltpu.roll(merged, LANES - j, 1))
    return out


def chunks_of(ref, field, row):
    return [ref[field, row : row + 8, LANES * j : LANES * (j + 1)] for j in range(8)]


def identity(size):
    rows = lax.broadcasted_iota(jnp.int32, (size, size), 0)
    return (rows == lax.broadcasted_iota(jnp.int32, (size, size), 1)).astype(F32)


def coarse_matrix(rate, coupling):
    return (rate * (identity(coupling.shape[0]) + coupling.T - coupling)).T


def put_blocks(ref, field, group, parts):
    for q, part in enumerate(parts):
        ref[group, pl.ds(64 * field + q, 8, stride=8), :] = part


def side_by_side(ref):
    return jnp.concatenate([ref[a] for a in range(ref.shape[0])], axis=1)


def split_kernel(starts_hbm, initial_hbm, rate_hbm, coup_hbm, own_out, offset_out, coarse_out, *scratch):
    starts, initial, rate, coup, sems = scratch
    count = starts.shape[0]
    pieces = [(rate_hbm, rate), (coup_hbm, coup)] + [(starts_hbm.at[f], starts.at[f]) for f in range(count)]
    copies = [pltpu.make_async_copy(src, dst, sems.at[i]) for i, (src, dst) in enumerate(pieces)]
    for copy in copies[2:] + copies[:2]:
        copy.start()
    first = lax.axis_index("cuts") == 0
    given = pltpu.make_async_copy(initial_hbm, initial, sems.at[len(copies)])

    @pl.when(first)
    def _():
        given.start()

    for f in range(count):
        copies[2 + f].wait()
        for a in range(starts.shape[1] // DOWN):
            parts = split_columns(chunks_of(starts, f, 8 * a))
            for q, part in enumerate(parts):
                own_out[f, q, 8 * a : 8 * a + 8, :] = part
            put_blocks(offset_out, f, a, [-part for part in parts])
    copies[0].wait()
    copies[1].wait()
    coarse_out[...] = coarse_matrix(rate[...], coup[...])

    @pl.when(first)
    def _():
        given.wait()
        for f in range(count):
            for a in range(starts.shape[1] // DOWN):
                parts = split_columns(chunks_of(initial, f, 8 * a))
                mine = [own_out[f, q, 8 * a : 8 * a + 8, :] for q in range(8)]
                put_blocks(offset_out, f, a, [part - m for part, m in zip(parts, mine)])


def powers_kernel(inner, outer, dec, matrix, total_out, near_out, step_out, far_out, held):
    lat = matrix.shape[0]
    inside = lax.axis_index("cuts") % inner
    coarse = matrix[...]
    powers = [identity(lat), coarse]
    for k in range(2, inner + 1):
        powers.append(dot_full(powers[k // 2], powers[k - k // 2]))
    for k, power in enumerate(powers):
        held[k] = power
    weight = dec[...].T
    decoded = [weight]
    for d in range(1, inner):
        place = inside ^ d
        part = dot_full(weight, held[jnp.maximum(inside - place, 0)])
        decoded.append(jnp.where(place < inside, part, 0.0))
    near_out[...] = jnp.concatenate(decoded, axis=1)
    total_out[...] = jnp.concatenate([held[inner - 1 - (inside ^ d)] for d in range(inner)], axis=1)
    part = dot_full(weight, held[inside + 1])
    decoded, steps, step = [part], [identity(lat), powers[inner]], powers[inner]
    for k in range(1, outer // 2):
        part = dot_full(part, powers[inner])
        decoded.append(part)
        step = dot_full(step, powers[inner])
        steps.append(step)
    far_out[...] = jnp.concatenate(decoded, axis=1)
    step_out[...] = jnp.concatenate(steps, axis=1)


class Padded:
    def __init__(self, ref, reps):
        self.ref = ref
        self.reps = reps

    def put(self, field, r, q, value, rows=True, cols=True):
        ref, reps = self.ref, self.reps
        ref[field, r + 2, q + 2] = value
        if rows and r < 2:
            ref[field, r + reps + 2, q + 2] = pltpu.roll(value, 7, 0)
        if rows and r >= reps - 2:
            ref[field, r - reps + 2, q + 2] = pltpu.roll(value, 1, 0)
        if cols and q < 2:
            ref[field, r + 2, q + 10] = pltpu.roll(value, LANES - 1, 1)
        if cols and q >= 6:
            ref[field, r + 2, q - 6] = pltpu.roll(value, 1, 1)

    def put_cell(self, r, q, height, along_c, along_r):
        self.put(0, r, q, height)
        self.put(1, r, q, along_c)
        self.put(2, r, q, along_r)
        self.put(3, r, q, along_r + height * along_r, cols=False)
        self.put(4, r, q, along_c + height * along_c, rows=False)

    def cell(self, field, r, q):
        return self.ref[field, r + 2, q + 2]

    def along_cols(self, field, r, q):
        at = self.cell
        return 8.0 * (at(field, r, q + 1) - at(field, r, q - 1)) - (at(field, r, q + 2) - at(field, r, q - 2))

    def along_rows(self, field, r, q):
        at = self.cell
        return 8.0 * (at(field, r + 1, q) - at(field, r - 1, q)) - (at(field, r + 2, q) - at(field, r - 2, q))


def stage(base, now, reps, alpha, beta, gamma, put):
    for r in range(reps):
        for q in range(8):
            height, along_c, along_r = (now.cell(f, r, q) for f in range(3))
            scale = gamma / 12.0
            d_height = now.along_cols(4, r, q) + now.along_rows(3, r, q)
            d_colvel = along_c * now.along_cols(1, r, q) + along_r * now.along_rows(1, r, q) + now.along_cols(0, r, q)
            d_rowvel = along_c * now.along_cols(2, r, q) + along_r * now.along_rows(2, r, q) + now.along_rows(0, r, q)
            new = []
            turn = gamma * FCOR
            for f, (mine, d, extra) in enumerate(
                ((height, d_height, None), (along_c, d_colvel, turn * along_r), (along_r, d_rowvel, -turn * along_c))
            ):
                total = beta * mine if beta != 1.0 else mine
                if alpha:
                    total = total + alpha * base.cell(f, r, q)
                if extra is not None:
                    total = total + extra
                new.append(total - scale * d)
            put(r, q, *new)


def fine_kernel(own, other, offset, enc, coarse, finals_out, g_out, t_out, rows_buf, buf_a, buf_b, buf_c):
    local_rows = own.shape[2]
    ext = local_rows + other.shape[1]
    reps = ext // 8
    groups = local_rows // DOWN
    for f in range(3):
        for q in range(8):
            rows_buf[f, q, 0:local_rows, :] = own[f, q, :, :]
        for tile in range(other.shape[1] // 8):
            parts = split_columns(chunks_of(other, f, 8 * tile))
            for q in range(8):
                rows_buf[f, q, local_rows + 8 * tile : local_rows + 8 * tile + 8, :] = parts[q]
    t_part = dot3(coarse[...], dot3(enc[...], side_by_side(offset)))
    t_out[...] = t_part
    state, second, third = Padded(buf_a, reps), Padded(buf_b, reps), Padded(buf_c, reps)
    for r in range(reps):
        for q in range(8):
            state.put_cell(r, q, *(rows_buf[f, q, pl.ds(r, 8, stride=reps), :] for f in range(3)))

    def finish(r, q, *cells):
        for f in range(3):
            rows_buf[f, q, pl.ds(r, 8, stride=reps), :] = cells[f]

    for step in range(FINE_STEPS):
        stage(None, state, reps, 0.0, 1.0, TSTEP, second.put_cell)
        stage(state, second, reps, 0.75, 0.25, 0.25 * TSTEP, third.put_cell)
        last = step + 1 == FINE_STEPS
        stage(state, third, reps, 1.0 / 3.0, 2.0 / 3.0, 2.0 / 3.0 * TSTEP, finish if last else state.put_cell)
    for f in range(3):
        for a in range(groups):
            put_blocks(finals_out, f, a, [rows_buf[f, q, 8 * a : 8 * a + 8, :] for q in range(8)])
    g_out[...] = dot3(enc[...], side_by_side(finals_out)) + t_part


def weighted_kernel(*refs):
    *parts, weights, out = refs
    out[...] = dot3(weights[...], jnp.concatenate([part[...] for part in parts], axis=0))


def base_kernel(finals, *refs):
    *parts, weights, out = refs
    change = dot3(weights[...], jnp.concatenate([part[...] for part in parts], axis=0))
    for a in range(finals.shape[0]):
        out[a] = finals[a] + change[:, LANES * a : LANES * (a + 1)]


def stacked(sources):
    return jnp.concatenate([sum((ref[...] for ref in refs[1:]), refs[0][...]) for refs in sources], axis=0)


def running_kernel(kinds, total, *refs):
    *parts, weights, out = refs
    sources = [[total]] + [[part for part, kind in zip(parts, kinds) if kind == k] for k in range(max(kinds) + 1)]
    lat = total.shape[0]
    out[...] = dot3(weights[:, : lat * len(sources)], stacked(sources))


def output_kernel(kinds, base, *refs):
    *parts, weights, out_hbm, held, joined_out, sems = refs
    sources = [[part for part, kind in zip(parts, kinds) if kind == k] for k in range(max(kinds) + 1)]
    change = dot3(weights[...], stacked(sources))
    copies = []
    for a in range(base.shape[0]):
        held[a] = base[a] + change[:, LANES * a : LANES * (a + 1)]
        for f in range(3):
            joined = join_columns([held[a, pl.ds(64 * f + q, 8, stride=8), :] for q in range(8)])
            for j, chunk in enumerate(joined):
                joined_out[f, 8 * a : 8 * a + 8, LANES * j : LANES * (j + 1)] = chunk
            rows = pl.ds(8 * a, 8)
            copy = pltpu.make_async_copy(joined_out.at[f, rows], out_hbm.at[0, f, rows], sems.at[3 * a + f])
            copy.start()
            copies.append(copy)
    for copy in copies:
        copy.wait()


def call(kernel, shapes, inputs, scratch=(), flops=0, inside=VMEM, outside=VMEM):
    return pl.pallas_call(
        kernel,
        out_shape=[jax.ShapeDtypeStruct(s, F32) for s in shapes],
        in_specs=[inside] * len(inputs),
        out_specs=[outside] * len(shapes),
        scratch_shapes=list(scratch),
        compiler_params=pltpu.CompilerParams(vmem_limit_bytes=40 * 1024 * 1024),
        cost_estimate=pl.CostEstimate(
            flops=flops, bytes_accessed=sum(4 * x.size for x in inputs), transcendentals=0
        ),
    )(*inputs)


def neighbour_rows(state):
    count = lax.axis_size("row")
    rows = state.shape[1]
    if count == 1:
        return jnp.concatenate([state[:, :HALO], state[:, rows - HALO :]], axis=1)
    forward = [(i, (i + 1) % count) for i in range(count)]
    backward = [((i + 1) % count, i) for i in range(count)]
    if count == 2 and rows <= 2 * HALO:
        return lax.ppermute(state, "row", forward)
    below = lax.ppermute(state[:, :HALO], "row", backward)
    above = lax.ppermute(state[:, rows - HALO :], "row", forward)
    return jnp.concatenate([below, above], axis=1)


def swapped(value, distance):
    return lax.ppermute(value, "cuts", [(i, i ^ distance) for i in range(lax.axis_size("cuts"))])


def later(value, block, distance, inner):
    groups = lax.axis_size("cuts") // inner
    sources = range(block // 2 - 1, groups, block)
    pairs = [(inner * z + i, inner * (z + distance) + i) for z in sources for i in range(inner)]
    return lax.ppermute(value, "cuts", pairs)


def local(starts, initial, encode_weight, decode_weight, latent_rate, coupling):
    lat = coupling.shape[0]
    state = starts[0]
    rows = state.shape[1]
    groups = rows // DOWN
    wide = groups * LANES
    size = encode_weight.shape[1]
    slices = lax.axis_size("cuts")
    inner = 1 << (slices.bit_length() // 2)
    outer = slices // inner
    rate = latent_rate.reshape(1, lat)
    other = neighbour_rows(state)
    given = (state, initial, rate, coupling)
    own, offset, coarse = call(
        split_kernel,
        [(3, 8, rows, LANES), (groups, size, LANES), (lat, lat)],
        [pltpu.with_memory_space_constraint(x, pltpu.HBM) for x in given],
        [pltpu.VMEM(x.shape, F32) for x in given] + [pltpu.SemaphoreType.DMA((6,))],
        flops=100_000_000,
        inside=pl.BlockSpec(memory_space=pl.ANY),
    )
    reps = (rows + other.shape[1]) // 8
    pad = pltpu.VMEM((5, reps + 4, 12, 8, LANES), F32)
    finals, g_part, t_part = call(
        fine_kernel,
        [(groups, size, LANES), (lat, wide), (lat, wide)],
        [own, other, offset, encode_weight, coarse],
        [pltpu.VMEM((3, 8, 8 * reps, LANES), F32), pad, pad, pad],
        flops=400_000_000,
    )
    parts = [swapped(g_part, d) for d in range(1, inner)]
    half = outer // 2
    to_total, to_near, to_running, to_far = call(
        functools.partial(powers_kernel, inner, outer),
        [(lat, inner * lat), (size, inner * lat), (lat, (half + 1) * lat), (size, half * lat)],
        [decode_weight.T, coarse],
        [pltpu.VMEM((inner + 1, lat, lat), F32)],
        flops=50_000_000,
    )
    (total,) = call(weighted_kernel, [(lat, wide)], [g_part, *parts, to_total], flops=50_000_000)
    running, come, kinds, block = total, [], [], 2
    while block <= outer:
        if come:
            kernel = functools.partial(running_kernel, tuple(kinds))
            (running,) = call(kernel, [(lat, wide)], [total, *come, to_running], flops=50_000_000)
        for k in range(block // 2):
            come.append(later(running, block, k + 1, inner))
            kinds.append(k)
        block *= 2
    (base,) = call(base_kernel, [(groups, size, LANES)], [finals, t_part, *parts, to_near], flops=50_000_000)
    (out,) = call(
        functools.partial(output_kernel, tuple(kinds)),
        [(1, 3, rows, starts.shape[3])],
        [base, *come, to_far],
        [
            pltpu.VMEM((groups, size, LANES), F32),
            pltpu.VMEM(state.shape, F32),
            pltpu.SemaphoreType.DMA((3 * groups,)),
        ],
        flops=50_000_000,
        outside=pl.BlockSpec(memory_space=pltpu.HBM),
    )
    return out


def solution(mesh):
    return jax.shard_map(
        local,
        mesh=mesh,
        in_specs=(P("cuts", None, "row", None), P(None, "row", None), P(), P(), P(), P()),
        out_specs=P("cuts", None, "row", None),
        check_vma=False,
    )
```

```python
import functools

import jax
import jax.numpy as jnp
from jax import lax
from jax.experimental import pallas as pl
from jax.experimental.pallas import tpu as pltpu
from jax.sharding import PartitionSpec as P

DOWN = 8
FINE_STEPS = 2
FCOR = 0.3
TSTEP = 0.25
HALO = 6 * FINE_STEPS
LANES = 128
F32 = jnp.float32
BF16 = jnp.bfloat16
VMEM = pl.BlockSpec(memory_space=pltpu.VMEM)


def halves(value):
    high = value.astype(BF16)
    return high, (value - high.astype(F32)).astype(BF16)


def dot3(left, right, contract=((1,), (0,))):
    dims = (contract, ((), ()))
    lh, ll = halves(left)
    rh, rl = halves(right)
    one = functools.partial(lax.dot_general, dimension_numbers=dims, preferred_element_type=F32)
    return one(lh, rh) + (one(lh, rl) + one(ll, rh))


def dot_full(left, right):
    return jnp.dot(left, right, precision=lax.Precision.HIGHEST, preferred_element_type=F32)


def lanes_iota():
    return lax.broadcasted_iota(jnp.int32, (8, LANES), 1)


def split_columns(chunks):
    lane = lanes_iota()
    moved = [c if j == 0 else pltpu.roll(c, j, 1) for j, c in enumerate(chunks)]
    phase = lane & 7
    out = []
    for q in range(8):
        merged = moved[0]
        for j in range(1, 8):
            merged = jnp.where(phase == (q + j) % 8, moved[j], merged)
        place = (8 * (lane & 15) + q + (lane >> 4)) & (LANES - 1)
        out.append(jnp.take_along_axis(merged, place, axis=1))
    return out


def join_columns(parts):
    lane = lanes_iota()
    phase = lane & 7
    picked = []
    for q, part in enumerate(parts):
        j = (lane - q) & 7
        place = 16 * j + (((lane - q - j) & (LANES - 1)) >> 3)
        picked.append(jnp.take_along_axis(part, place, axis=1))
    out = []
    for j in range(8):
        merged = picked[(-j) % 8]
        for q in range(8):
            if q != (-j) % 8:
                merged = jnp.where(phase == (q + j) % 8, picked[q], merged)
        out.append(merged if j == 0 else pltpu.roll(merged, LANES - j, 1))
    return out


def chunks_of(ref, field, row):
    return [ref[field, row : row + 8, LANES * j : LANES * (j + 1)] for j in range(8)]


def identity(size):
    rows = lax.broadcasted_iota(jnp.int32, (size, size), 0)
    return (rows == lax.broadcasted_iota(jnp.int32, (size, size), 1)).astype(F32)


def coarse_matrix(rate, coupling):
    return (rate * (identity(coupling.shape[0]) + coupling.T - coupling)).T


def put_blocks(ref, field, group, parts):
    for q, part in enumerate(parts):
        ref[group, pl.ds(64 * field + q, 8, stride=8), :] = part


def side_by_side(ref):
    return jnp.concatenate([ref[a] for a in range(ref.shape[0])], axis=1)


def split_kernel(starts_hbm, initial_hbm, rate_hbm, coup_hbm, own_out, offset_out, coarse_out, *scratch):
    starts, initial, rate, coup, sems = scratch
    count = starts.shape[0]
    pieces = [(rate_hbm, rate), (coup_hbm, coup)] + [(starts_hbm.at[f], starts.at[f]) for f in range(count)]
    copies = [pltpu.make_async_copy(src, dst, sems.at[i]) for i, (src, dst) in enumerate(pieces)]
    for copy in copies[2:] + copies[:2]:
        copy.start()
    first = lax.axis_index("cuts") == 0
    given = pltpu.make_async_copy(initial_hbm, initial, sems.at[len(copies)])

    @pl.when(first)
    def _():
        given.start()

    for f in range(count):
        copies[2 + f].wait()
        for a in range(starts.shape[1] // DOWN):
            parts = split_columns(chunks_of(starts, f, 8 * a))
            for q, part in enumerate(parts):
                own_out[f, q, 8 * a : 8 * a + 8, :] = part
            put_blocks(offset_out, f, a, [-part for part in parts])
    copies[0].wait()
    copies[1].wait()
    coarse_out[...] = coarse_matrix(rate[...], coup[...])

    @pl.when(first)
    def _():
        given.wait()
        for f in range(count):
            for a in range(starts.shape[1] // DOWN):
                parts = split_columns(chunks_of(initial, f, 8 * a))
                mine = [own_out[f, q, 8 * a : 8 * a + 8, :] for q in range(8)]
                put_blocks(offset_out, f, a, [part - m for part, m in zip(parts, mine)])


def powers_kernel(inner, outer, dec, matrix, total_out, near_out, step_out, far_out, held):
    lat = matrix.shape[0]
    inside = lax.axis_index("cuts") % inner
    coarse = matrix[...]
    powers = [identity(lat), coarse]
    for k in range(2, inner + 1):
        powers.append(dot_full(powers[k // 2], powers[k - k // 2]))
    for k, power in enumerate(powers):
        held[k] = power
    weight = dec[...].T
    decoded = [weight]
    for d in range(1, inner):
        place = inside ^ d
        part = dot_full(weight, held[jnp.maximum(inside - place, 0)])
        decoded.append(jnp.where(place < inside, part, 0.0))
    near_out[...] = jnp.concatenate(decoded, axis=1)
    total_out[...] = jnp.concatenate([held[inner - 1 - (inside ^ d)] for d in range(inner)], axis=1)
    part = dot_full(weight, held[inside + 1])
    decoded, steps, step = [part], [identity(lat), powers[inner]], powers[inner]
    for k in range(1, outer // 2):
        part = dot_full(part, powers[inner])
        decoded.append(part)
        step = dot_full(step, powers[inner])
        steps.append(step)
    far_out[...] = jnp.concatenate(decoded, axis=1)
    step_out[...] = jnp.concatenate(steps, axis=1)


class Padded:
    def __init__(self, ref, reps):
        self.ref = ref
        self.reps = reps

    def put(self, field, r, q, value, rows=True, cols=True):
        ref, reps = self.ref, self.reps
        ref[field, r + 2, q + 2] = value
        if rows and r < 2:
            ref[field, r + reps + 2, q + 2] = pltpu.roll(value, 7, 0)
        if rows and r >= reps - 2:
            ref[field, r - reps + 2, q + 2] = pltpu.roll(value, 1, 0)
        if cols and q < 2:
            ref[field, r + 2, q + 10] = pltpu.roll(value, LANES - 1, 1)
        if cols and q >= 6:
            ref[field, r + 2, q - 6] = pltpu.roll(value, 1, 1)

    def put_cell(self, r, q, height, along_c, along_r):
        self.put(0, r, q, height)
        self.put(1, r, q, along_c)
        self.put(2, r, q, along_r)
        self.put(3, r, q, along_r + height * along_r, cols=False)
        self.put(4, r, q, along_c + height * along_c, rows=False)

    def cell(self, field, r, q):
        return self.ref[field, r + 2, q + 2]

    def along_cols(self, field, r, q):
        at = self.cell
        return 8.0 * (at(field, r, q + 1) - at(field, r, q - 1)) - (at(field, r, q + 2) - at(field, r, q - 2))

    def along_rows(self, field, r, q):
        at = self.cell
        return 8.0 * (at(field, r + 1, q) - at(field, r - 1, q)) - (at(field, r + 2, q) - at(field, r - 2, q))


def stage(base, now, reps, alpha, beta, gamma, put):
    for r in range(reps):
        for q in range(8):
            height, along_c, along_r = (now.cell(f, r, q) for f in range(3))
            scale = gamma / 12.0
            d_height = now.along_cols(4, r, q) + now.along_rows(3, r, q)
            d_colvel = along_c * now.along_cols(1, r, q) + along_r * now.along_rows(1, r, q) + now.along_cols(0, r, q)
            d_rowvel = along_c * now.along_cols(2, r, q) + along_r * now.along_rows(2, r, q) + now.along_rows(0, r, q)
            new = []
            turn = gamma * FCOR
            for f, (mine, d, extra) in enumerate(
                ((height, d_height, None), (along_c, d_colvel, turn * along_r), (along_r, d_rowvel, -turn * along_c))
            ):
                total = beta * mine if beta != 1.0 else mine
                if alpha:
                    total = total + alpha * base.cell(f, r, q)
                if extra is not None:
                    total = total + extra
                new.append(total - scale * d)
            put(r, q, *new)


def fine_kernel(own, other, offset, enc, coarse, finals_out, g_out, t_out, rows_buf, buf_a, buf_b, buf_c):
    local_rows = own.shape[2]
    ext = local_rows + other.shape[1]
    reps = ext // 8
    groups = local_rows // DOWN
    for f in range(3):
        for q in range(8):
            rows_buf[f, q, 0:local_rows, :] = own[f, q, :, :]
        for tile in range(other.shape[1] // 8):
            parts = split_columns(chunks_of(other, f, 8 * tile))
            for q in range(8):
                rows_buf[f, q, local_rows + 8 * tile : local_rows + 8 * tile + 8, :] = parts[q]
    t_part = dot3(coarse[...], dot3(enc[...], side_by_side(offset)))
    t_out[...] = t_part
    state, second, third = Padded(buf_a, reps), Padded(buf_b, reps), Padded(buf_c, reps)
    for r in range(reps):
        for q in range(8):
            state.put_cell(r, q, *(rows_buf[f, q, pl.ds(r, 8, stride=reps), :] for f in range(3)))

    def finish(r, q, *cells):
        for f in range(3):
            rows_buf[f, q, pl.ds(r, 8, stride=reps), :] = cells[f]

    for step in range(FINE_STEPS):
        stage(None, state, reps, 0.0, 1.0, TSTEP, second.put_cell)
        stage(state, second, reps, 0.75, 0.25, 0.25 * TSTEP, third.put_cell)
        last = step + 1 == FINE_STEPS
        stage(state, third, reps, 1.0 / 3.0, 2.0 / 3.0, 2.0 / 3.0 * TSTEP, finish if last else state.put_cell)
    for f in range(3):
        for a in range(groups):
            put_blocks(finals_out, f, a, [rows_buf[f, q, 8 * a : 8 * a + 8, :] for q in range(8)])
    g_out[...] = dot3(enc[...], side_by_side(finals_out)) + t_part


def weighted_kernel(*refs):
    *parts, weights, out = refs
    out[...] = dot3(weights[...], jnp.concatenate([part[...] for part in parts], axis=0))


def base_kernel(finals, *refs):
    *parts, weights, out = refs
    change = dot3(weights[...], jnp.concatenate([part[...] for part in parts], axis=0))
    for a in range(finals.shape[0]):
        out[a] = finals[a] + change[:, LANES * a : LANES * (a + 1)]


def received(plan, inner, parts):
    group = lax.axis_index("cuts") // inner
    sums = {}
    for part, (block, between) in zip(parts, plan):
        taken = jnp.where(group % block == block // 2 + between, part[...], 0.0)
        sums[between] = sums[between] + taken if between in sums else taken
    return [sums[k] for k in sorted(sums)]


def running_kernel(plan, inner, total, *refs):
    *parts, weights, out = refs
    latents = [total[...]] + received(plan, inner, parts)
    width = total.shape[0] * len(latents)
    out[...] = dot3(weights[:, :width], jnp.concatenate(latents, axis=0))


def output_kernel(plan, inner, base, *refs):
    *parts, weights, out_hbm, held, joined_out, sems = refs
    latents = jnp.concatenate(received(plan, inner, parts), axis=0)
    change = dot3(weights[...], latents)
    copies = []
    for a in range(base.shape[0]):
        held[a] = base[a] + change[:, LANES * a : LANES * (a + 1)]
        for f in range(3):
            joined = join_columns([held[a, pl.ds(64 * f + q, 8, stride=8), :] for q in range(8)])
            for j, chunk in enumerate(joined):
                joined_out[f, 8 * a : 8 * a + 8, LANES * j : LANES * (j + 1)] = chunk
            rows = pl.ds(8 * a, 8)
            copy = pltpu.make_async_copy(joined_out.at[f, rows], out_hbm.at[0, f, rows], sems.at[3 * a + f])
            copy.start()
            copies.append(copy)
    for copy in copies:
        copy.wait()


def call(kernel, shapes, inputs, scratch=(), flops=0, inside=VMEM, outside=VMEM):
    return pl.pallas_call(
        kernel,
        out_shape=[jax.ShapeDtypeStruct(s, F32) for s in shapes],
        in_specs=[inside] * len(inputs),
        out_specs=[outside] * len(shapes),
        scratch_shapes=list(scratch),
        compiler_params=pltpu.CompilerParams(vmem_limit_bytes=40 * 1024 * 1024),
        cost_estimate=pl.CostEstimate(
            flops=flops, bytes_accessed=sum(4 * x.size for x in inputs), transcendentals=0
        ),
    )(*inputs)


def neighbour_rows(state):
    count = lax.axis_size("row")
    rows = state.shape[1]
    if count == 1:
        return jnp.concatenate([state[:, :HALO], state[:, rows - HALO :]], axis=1)
    forward = [(i, (i + 1) % count) for i in range(count)]
    backward = [((i + 1) % count, i) for i in range(count)]
    if count == 2 and rows <= 2 * HALO:
        return lax.ppermute(state, "row", forward)
    below = lax.ppermute(state[:, :HALO], "row", backward)
    above = lax.ppermute(state[:, rows - HALO :], "row", forward)
    return jnp.concatenate([below, above], axis=1)


def swapped(value, distance):
    return lax.ppermute(value, "cuts", [(i, i ^ distance) for i in range(lax.axis_size("cuts"))])


def passed_on(value, block, distance, inner):
    groups = lax.axis_size("cuts") // inner
    place = list(range(groups))
    for z in range(block // 2 - 1, groups, block):
        place[z], place[z + distance] = z + distance, z
    return lax.ppermute(value, "cuts", [(inner * z + i, inner * place[z] + i) for z in range(groups) for i in range(inner)])


def local(starts, initial, encode_weight, decode_weight, latent_rate, coupling):
    lat = coupling.shape[0]
    state = starts[0]
    rows = state.shape[1]
    groups = rows // DOWN
    wide = groups * LANES
    size = encode_weight.shape[1]
    slices = lax.axis_size("cuts")
    inner = 1 << (slices.bit_length() // 2)
    outer = slices // inner
    rate = latent_rate.reshape(1, lat)
    other = neighbour_rows(state)
    given = (state, initial, rate, coupling)
    own, offset, coarse = call(
        split_kernel,
        [(3, 8, rows, LANES), (groups, size, LANES), (lat, lat)],
        [pltpu.with_memory_space_constraint(x, pltpu.HBM) for x in given],
        [pltpu.VMEM(x.shape, F32) for x in given] + [pltpu.SemaphoreType.DMA((6,))],
        flops=100_000_000,
        inside=pl.BlockSpec(memory_space=pl.ANY),
    )
    reps = (rows + other.shape[1]) // 8
    pad = pltpu.VMEM((5, reps + 4, 12, 8, LANES), F32)
    finals, g_part, t_part = call(
        fine_kernel,
        [(groups, size, LANES), (lat, wide), (lat, wide)],
        [own, other, offset, encode_weight, coarse],
        [pltpu.VMEM((3, 8, 8 * reps, LANES), F32), pad, pad, pad],
        flops=400_000_000,
    )
    parts = [swapped(g_part, d) for d in range(1, inner)]
    half = outer // 2
    to_total, to_near, to_running, to_far = call(
        functools.partial(powers_kernel, inner, outer),
        [(lat, inner * lat), (size, inner * lat), (lat, (half + 1) * lat), (size, half * lat)],
        [decode_weight.T, coarse],
        [pltpu.VMEM((inner + 1, lat, lat), F32)],
        flops=50_000_000,
    )
    (total,) = call(weighted_kernel, [(lat, wide)], [g_part, *parts, to_total], flops=50_000_000)
    running, come, plan, block = total, [], [], 2
    while block <= outer:
        if come:
            kernel = functools.partial(running_kernel, tuple(plan), inner)
            (running,) = call(kernel, [(lat, wide)], [total, *come, to_running], flops=50_000_000)
        for k in range(block // 2):
            come.append(passed_on(running, block, k + 1, inner))
            plan.append((block, k))
        block *= 2
    (base,) = call(base_kernel, [(groups, size, LANES)], [finals, t_part, *parts, to_near], flops=50_000_000)
    (out,) = call(
        functools.partial(output_kernel, tuple(plan), inner),
        [(1, 3, rows, starts.shape[3])],
        [base, *come, to_far],
        [
            pltpu.VMEM((groups, size, LANES), F32),
            pltpu.VMEM(state.shape, F32),
            pltpu.SemaphoreType.DMA((3 * groups,)),
        ],
        flops=50_000_000,
        outside=pl.BlockSpec(memory_space=pltpu.HBM),
    )
    return out


def solution(mesh):
    return jax.shard_map(
        local,
        mesh=mesh,
        in_specs=(P("cuts", None, "row", None), P(None, "row", None), P(), P(), P(), P()),
        out_specs=P("cuts", None, "row", None),
        check_vma=False,
    )
```

```python
import functools

import jax
import jax.numpy as jnp
from jax import lax
from jax.experimental import pallas as pl
from jax.experimental.pallas import tpu as pltpu
from jax.sharding import PartitionSpec as P

DOWN = 8
FINE_STEPS = 2
FCOR = 0.3
TSTEP = 0.25
HALO = 6 * FINE_STEPS
LANES = 128
F32 = jnp.float32
BF16 = jnp.bfloat16
VMEM = pl.BlockSpec(memory_space=pltpu.VMEM)


def halves(value):
    high = value.astype(BF16)
    return high, (value - high.astype(F32)).astype(BF16)


def dot3(left, right, contract=((1,), (0,))):
    dims = (contract, ((), ()))
    lh, ll = halves(left)
    rh, rl = halves(right)
    one = functools.partial(lax.dot_general, dimension_numbers=dims, preferred_element_type=F32)
    return one(lh, rh) + (one(lh, rl) + one(ll, rh))


def dot_full(left, right):
    return jnp.dot(left, right, precision=lax.Precision.HIGHEST, preferred_element_type=F32)


def lanes_iota():
    return lax.broadcasted_iota(jnp.int32, (8, LANES), 1)


def split_columns(chunks):
    lane = lanes_iota()
    moved = [c if j == 0 else pltpu.roll(c, j, 1) for j, c in enumerate(chunks)]
    phase = lane & 7
    out = []
    for q in range(8):
        merged = moved[0]
        for j in range(1, 8):
            merged = jnp.where(phase == (q + j) % 8, moved[j], merged)
        place = (8 * (lane & 15) + q + (lane >> 4)) & (LANES - 1)
        out.append(jnp.take_along_axis(merged, place, axis=1))
    return out


def join_columns(parts):
    lane = lanes_iota()
    phase = lane & 7
    picked = []
    for q, part in enumerate(parts):
        j = (lane - q) & 7
        place = 16 * j + (((lane - q - j) & (LANES - 1)) >> 3)
        picked.append(jnp.take_along_axis(part, place, axis=1))
    out = []
    for j in range(8):
        merged = picked[(-j) % 8]
        for q in range(8):
            if q != (-j) % 8:
                merged = jnp.where(phase == (q + j) % 8, picked[q], merged)
        out.append(merged if j == 0 else pltpu.roll(merged, LANES - j, 1))
    return out


def chunks_of(ref, field, row):
    return [ref[field, row : row + 8, LANES * j : LANES * (j + 1)] for j in range(8)]


def identity(size):
    rows = lax.broadcasted_iota(jnp.int32, (size, size), 0)
    return (rows == lax.broadcasted_iota(jnp.int32, (size, size), 1)).astype(F32)


def coarse_matrix(rate, coupling):
    return (rate * (identity(coupling.shape[0]) + coupling.T - coupling)).T


def put_blocks(ref, field, group, parts):
    for q, part in enumerate(parts):
        ref[group, pl.ds(64 * field + q, 8, stride=8), :] = part


def side_by_side(ref):
    return jnp.concatenate([ref[a] for a in range(ref.shape[0])], axis=1)


def split_kernel(starts_hbm, initial_hbm, rate_hbm, coup_hbm, own_out, offset_out, coarse_out, *scratch):
    starts, initial, rate, coup, sems = scratch
    count = starts.shape[0]
    pieces = [(rate_hbm, rate), (coup_hbm, coup)] + [(starts_hbm.at[f], starts.at[f]) for f in range(count)]
    copies = [pltpu.make_async_copy(src, dst, sems.at[i]) for i, (src, dst) in enumerate(pieces)]
    for copy in copies[2:] + copies[:2]:
        copy.start()
    first = lax.axis_index("cuts") == 0
    given = pltpu.make_async_copy(initial_hbm, initial, sems.at[len(copies)])

    @pl.when(first)
    def _():
        given.start()

    for f in range(count):
        copies[2 + f].wait()
        for a in range(starts.shape[1] // DOWN):
            parts = split_columns(chunks_of(starts, f, 8 * a))
            for q, part in enumerate(parts):
                own_out[f, q, 8 * a : 8 * a + 8, :] = part
            put_blocks(offset_out, f, a, [-part for part in parts])
    copies[0].wait()
    copies[1].wait()
    coarse_out[...] = coarse_matrix(rate[...], coup[...])

    @pl.when(first)
    def _():
        given.wait()
        for f in range(count):
            for a in range(starts.shape[1] // DOWN):
                parts = split_columns(chunks_of(initial, f, 8 * a))
                mine = [own_out[f, q, 8 * a : 8 * a + 8, :] for q in range(8)]
                put_blocks(offset_out, f, a, [part - m for part, m in zip(parts, mine)])


def powers_kernel(inner, outer, dec, matrix, total_out, near_out, far_out, held, decoded_held):
    lat = matrix.shape[0]
    inside = lax.axis_index("cuts") % inner
    coarse = matrix[...]
    powers = [identity(lat), coarse]
    for k in range(2, inner + 1):
        powers.append(dot_full(powers[k // 2], powers[k - k // 2]))
    for k, power in enumerate(powers):
        held[k] = power
    weight = dec[...].T
    decoded = [weight]
    for d in range(1, inner):
        place = inside ^ d
        part = dot_full(weight, held[jnp.maximum(inside - place, 0)])
        decoded.append(jnp.where(place < inside, part, 0.0))
    near_out[...] = jnp.concatenate(decoded, axis=1)
    total_out[...] = jnp.concatenate([held[inner - 1 - (inside ^ d)] for d in range(inner)], axis=1)
    group = lax.axis_index("cuts") // inner
    far = [dot_full(weight, held[inside + 1])]
    for k in range(2, outer):
        far.append(dot_full(far[-1], powers[inner]))
    for k, part in enumerate(far):
        decoded_held[k] = part
    order = [jnp.maximum(group - 1 - (group ^ d), 0) for d in range(1, outer)]
    far_out[...] = jnp.concatenate([decoded_held[k] for k in order], axis=1)


class Padded:
    def __init__(self, ref, reps):
        self.ref = ref
        self.reps = reps

    def put(self, field, r, q, value, rows=True, cols=True):
        ref, reps = self.ref, self.reps
        ref[field, r + 2, q + 2] = value
        if rows and r < 2:
            ref[field, r + reps + 2, q + 2] = pltpu.roll(value, 7, 0)
        if rows and r >= reps - 2:
            ref[field, r - reps + 2, q + 2] = pltpu.roll(value, 1, 0)
        if cols and q < 2:
            ref[field, r + 2, q + 10] = pltpu.roll(value, LANES - 1, 1)
        if cols and q >= 6:
            ref[field, r + 2, q - 6] = pltpu.roll(value, 1, 1)

    def put_cell(self, r, q, height, along_c, along_r):
        self.put(0, r, q, height)
        self.put(1, r, q, along_c)
        self.put(2, r, q, along_r)
        self.put(3, r, q, along_r + height * along_r, cols=False)
        self.put(4, r, q, along_c + height * along_c, rows=False)

    def cell(self, field, r, q):
        return self.ref[field, r + 2, q + 2]

    def along_cols(self, field, r, q):
        at = self.cell
        return 8.0 * (at(field, r, q + 1) - at(field, r, q - 1)) - (at(field, r, q + 2) - at(field, r, q - 2))

    def along_rows(self, field, r, q):
        at = self.cell
        return 8.0 * (at(field, r + 1, q) - at(field, r - 1, q)) - (at(field, r + 2, q) - at(field, r - 2, q))


def stage(base, now, reps, alpha, beta, gamma, put):
    for r in range(reps):
        for q in range(8):
            height, along_c, along_r = (now.cell(f, r, q) for f in range(3))
            scale = gamma / 12.0
            d_height = now.along_cols(4, r, q) + now.along_rows(3, r, q)
            d_colvel = along_c * now.along_cols(1, r, q) + along_r * now.along_rows(1, r, q) + now.along_cols(0, r, q)
            d_rowvel = along_c * now.along_cols(2, r, q) + along_r * now.along_rows(2, r, q) + now.along_rows(0, r, q)
            new = []
            turn = gamma * FCOR
            for f, (mine, d, extra) in enumerate(
                ((height, d_height, None), (along_c, d_colvel, turn * along_r), (along_r, d_rowvel, -turn * along_c))
            ):
                total = beta * mine if beta != 1.0 else mine
                if alpha:
                    total = total + alpha * base.cell(f, r, q)
                if extra is not None:
                    total = total + extra
                new.append(total - scale * d)
            put(r, q, *new)


def fine_kernel(own, other, offset, enc, coarse, finals_out, g_out, t_out, rows_buf, buf_a, buf_b, buf_c):
    local_rows = own.shape[2]
    ext = local_rows + other.shape[1]
    reps = ext // 8
    groups = local_rows // DOWN
    for f in range(3):
        for q in range(8):
            rows_buf[f, q, 0:local_rows, :] = own[f, q, :, :]
        for tile in range(other.shape[1] // 8):
            parts = split_columns(chunks_of(other, f, 8 * tile))
            for q in range(8):
                rows_buf[f, q, local_rows + 8 * tile : local_rows + 8 * tile + 8, :] = parts[q]
    t_part = dot3(coarse[...], dot3(enc[...], side_by_side(offset)))
    t_out[...] = t_part
    state, second, third = Padded(buf_a, reps), Padded(buf_b, reps), Padded(buf_c, reps)
    for r in range(reps):
        for q in range(8):
            state.put_cell(r, q, *(rows_buf[f, q, pl.ds(r, 8, stride=reps), :] for f in range(3)))

    def finish(r, q, *cells):
        for f in range(3):
            rows_buf[f, q, pl.ds(r, 8, stride=reps), :] = cells[f]

    for step in range(FINE_STEPS):
        stage(None, state, reps, 0.0, 1.0, TSTEP, second.put_cell)
        stage(state, second, reps, 0.75, 0.25, 0.25 * TSTEP, third.put_cell)
        last = step + 1 == FINE_STEPS
        stage(state, third, reps, 1.0 / 3.0, 2.0 / 3.0, 2.0 / 3.0 * TSTEP, finish if last else state.put_cell)
    for f in range(3):
        for a in range(groups):
            put_blocks(finals_out, f, a, [rows_buf[f, q, 8 * a : 8 * a + 8, :] for q in range(8)])
    g_out[...] = dot3(enc[...], side_by_side(finals_out)) + t_part


def weighted_kernel(*refs):
    *parts, weights, out = refs
    out[...] = dot3(weights[...], jnp.concatenate([part[...] for part in parts], axis=0))


def base_kernel(finals, *refs):
    *parts, weights, out_hbm, out, held, sems = refs
    change = dot3(weights[...], jnp.concatenate([part[...] for part in parts], axis=0))
    copies = []
    for a in range(finals.shape[0]):
        held[a] = finals[a] + change[:, LANES * a : LANES * (a + 1)]
        rows = pl.ds(8 * a, 8)
        for f in range(3):
            joined = join_columns([held[a, pl.ds(64 * f + q, 8, stride=8), :] for q in range(8)])
            for j, chunk in enumerate(joined):
                out[f, 8 * a : 8 * a + 8, LANES * j : LANES * (j + 1)] = chunk
            copies.append(pltpu.make_async_copy(out.at[f, rows], out_hbm.at[0, f, rows], sems.at[3 * a + f]))
            copies[-1].start()
    for copy in copies:
        copy.wait()


def output_kernel(inner, base, *refs):
    *totals, weights, _, out_hbm, held, joined_out, sems = refs
    group = lax.axis_index("cuts") // inner

    @pl.when(group > 0)
    def _():
        taken = [jnp.where((group ^ (d + 1)) < group, part[...], 0.0) for d, part in enumerate(totals)]
        change = dot3(weights[...], jnp.concatenate(taken, axis=0))
        copies = []
        for a in range(held.shape[0]):
            held[a] = change[:, LANES * a : LANES * (a + 1)]
            rows = pl.ds(8 * a, 8)
            for f in range(3):
                joined = join_columns([held[a, pl.ds(64 * f + q, 8, stride=8), :] for q in range(8)])
                for j, chunk in enumerate(joined):
                    cells = (f, slice(8 * a, 8 * a + 8), slice(LANES * j, LANES * (j + 1)))
                    joined_out[cells] = base[cells] + chunk
                copies.append(pltpu.make_async_copy(joined_out.at[f, rows], out_hbm.at[0, f, rows], sems.at[3 * a + f]))
                copies[-1].start()
        for copy in copies:
            copy.wait()


def call(kernel, shapes, inputs, scratch=(), flops=0, inside=None, outside=None, aliases={}):
    return pl.pallas_call(
        kernel,
        out_shape=[jax.ShapeDtypeStruct(s, F32) for s in shapes],
        in_specs=inside or [VMEM] * len(inputs),
        out_specs=outside or [VMEM] * len(shapes),
        scratch_shapes=list(scratch),
        input_output_aliases=aliases,
        compiler_params=pltpu.CompilerParams(vmem_limit_bytes=40 * 1024 * 1024),
        cost_estimate=pl.CostEstimate(
            flops=flops, bytes_accessed=sum(4 * x.size for x in inputs), transcendentals=0
        ),
    )(*inputs)


def neighbour_rows(state):
    count = lax.axis_size("row")
    rows = state.shape[1]
    if count == 1:
        return jnp.concatenate([state[:, :HALO], state[:, rows - HALO :]], axis=1)
    forward = [(i, (i + 1) % count) for i in range(count)]
    backward = [((i + 1) % count, i) for i in range(count)]
    if count == 2 and rows <= 2 * HALO:
        return lax.ppermute(state, "row", forward)
    below = lax.ppermute(state[:, :HALO], "row", backward)
    above = lax.ppermute(state[:, rows - HALO :], "row", forward)
    return jnp.concatenate([below, above], axis=1)


def swapped(value, distance):
    return lax.ppermute(value, "cuts", [(i, i ^ distance) for i in range(lax.axis_size("cuts"))])


def local(starts, initial, encode_weight, decode_weight, latent_rate, coupling):
    lat = coupling.shape[0]
    state = starts[0]
    rows = state.shape[1]
    groups = rows // DOWN
    wide = groups * LANES
    size = encode_weight.shape[1]
    slices = lax.axis_size("cuts")
    inner = 1 << (slices.bit_length() // 2)
    outer = slices // inner
    rate = latent_rate.reshape(1, lat)
    other = neighbour_rows(state)
    given = (state, initial, rate, coupling)
    own, offset, coarse = call(
        split_kernel,
        [(3, 8, rows, LANES), (groups, size, LANES), (lat, lat)],
        [pltpu.with_memory_space_constraint(x, pltpu.HBM) for x in given],
        [pltpu.VMEM(x.shape, F32) for x in given] + [pltpu.SemaphoreType.DMA((6,))],
        flops=100_000_000,
        inside=[pl.BlockSpec(memory_space=pl.ANY)] * len(given),
    )
    reps = (rows + other.shape[1]) // 8
    pad = pltpu.VMEM((5, reps + 4, 12, 8, LANES), F32)
    finals, g_part, t_part = call(
        fine_kernel,
        [(groups, size, LANES), (lat, wide), (lat, wide)],
        [own, other, offset, encode_weight, coarse],
        [pltpu.VMEM((3, 8, 8 * reps, LANES), F32), pad, pad, pad],
        flops=400_000_000,
    )
    parts = [swapped(g_part, d) for d in range(1, inner)]
    to_total, to_near, to_far = call(
        functools.partial(powers_kernel, inner, outer),
        [(lat, inner * lat), (size, inner * lat), (size, (outer - 1) * lat)],
        [decode_weight.T, coarse],
        [pltpu.VMEM((inner + 1, lat, lat), F32), pltpu.VMEM((outer - 1, size, lat), F32)],
        flops=50_000_000,
    )
    (total,) = call(weighted_kernel, [(lat, wide)], [g_part, *parts, to_total], flops=50_000_000)
    totals = [swapped(total, inner * d) for d in range(1, outer)]
    hbm = pl.BlockSpec(memory_space=pltpu.HBM)
    blocks = pltpu.VMEM((groups, size, LANES), F32)
    tiles = pltpu.SemaphoreType.DMA((3 * groups,))
    result = (1, *state.shape)
    near_result, base = call(
        base_kernel,
        [result, state.shape],
        [finals, t_part, *parts, to_near],
        [blocks, tiles],
        flops=50_000_000,
        outside=[hbm, VMEM],
    )
    (out,) = call(
        functools.partial(output_kernel, inner),
        [result],
        [base, *totals, to_far, near_result],
        [blocks, pltpu.VMEM(state.shape, F32), tiles],
        flops=50_000_000,
        inside=[VMEM] * (outer + 1) + [hbm],
        outside=[hbm],
        aliases={outer + 1: 0},
    )
    return out


def solution(mesh):
    return jax.shard_map(
        local,
        mesh=mesh,
        in_specs=(P("cuts", None, "row", None), P(None, "row", None), P(), P(), P(), P()),
        out_specs=P("cuts", None, "row", None),
        check_vma=False,
    )
```

```python
import functools

import jax
import jax.numpy as jnp
from jax import lax
from jax.experimental import pallas as pl
from jax.experimental.pallas import tpu as pltpu
from jax.sharding import PartitionSpec as P

DOWN = 8
FINE_STEPS = 2
FCOR = 0.3
TSTEP = 0.25
HALO = 6 * FINE_STEPS
LANES = 128
F32 = jnp.float32
BF16 = jnp.bfloat16
VMEM = pl.BlockSpec(memory_space=pltpu.VMEM)


def halves(value):
    high = value.astype(BF16)
    return high, (value - high.astype(F32)).astype(BF16)


def dot3(left, right, contract=((1,), (0,))):
    dims = (contract, ((), ()))
    lh, ll = halves(left)
    rh, rl = halves(right)
    one = functools.partial(lax.dot_general, dimension_numbers=dims, preferred_element_type=F32)
    return one(lh, rh) + (one(lh, rl) + one(ll, rh))


def dot_full(left, right):
    return jnp.dot(left, right, precision=lax.Precision.HIGHEST, preferred_element_type=F32)


def lanes_iota():
    return lax.broadcasted_iota(jnp.int32, (8, LANES), 1)


def split_columns(chunks):
    lane = lanes_iota()
    moved = [c if j == 0 else pltpu.roll(c, j, 1) for j, c in enumerate(chunks)]
    phase = lane & 7
    out = []
    for q in range(8):
        merged = moved[0]
        for j in range(1, 8):
            merged = jnp.where(phase == (q + j) % 8, moved[j], merged)
        place = (8 * (lane & 15) + q + (lane >> 4)) & (LANES - 1)
        out.append(jnp.take_along_axis(merged, place, axis=1))
    return out


def join_columns(parts):
    lane = lanes_iota()
    phase = lane & 7
    picked = []
    for q, part in enumerate(parts):
        j = (lane - q) & 7
        place = 16 * j + (((lane - q - j) & (LANES - 1)) >> 3)
        picked.append(jnp.take_along_axis(part, place, axis=1))
    out = []
    for j in range(8):
        merged = picked[(-j) % 8]
        for q in range(8):
            if q != (-j) % 8:
                merged = jnp.where(phase == (q + j) % 8, picked[q], merged)
        out.append(merged if j == 0 else pltpu.roll(merged, LANES - j, 1))
    return out


def chunks_of(ref, field, row):
    return [ref[field, row : row + 8, LANES * j : LANES * (j + 1)] for j in range(8)]


def identity(size):
    rows = lax.broadcasted_iota(jnp.int32, (size, size), 0)
    return (rows == lax.broadcasted_iota(jnp.int32, (size, size), 1)).astype(F32)


def coarse_matrix(rate, coupling):
    return (rate * (identity(coupling.shape[0]) + coupling.T - coupling)).T


def put_blocks(ref, field, group, parts):
    for q, part in enumerate(parts):
        ref[group, 64 * field + 8 * q : 64 * field + 8 * q + 8, :] = part


def reordered(weight):
    size = weight.shape[1]
    source = lax.broadcasted_iota(jnp.int32, (size, size), 0)
    target = lax.broadcasted_iota(jnp.int32, (size, size), 1)
    wanted = (target & ~63) | ((target & 7) << 3) | ((target >> 3) & 7)
    return dot_full(weight, (source == wanted).astype(F32))


def side_by_side(ref):
    return jnp.concatenate([ref[a] for a in range(ref.shape[0])], axis=1)


def split_kernel(starts_hbm, initial_hbm, enc_hbm, rate_hbm, coup_hbm, *refs):
    own_out, offset_out, enc_out, coarse_out, starts, initial, enc, rate, coup, sems = refs
    count = starts.shape[0]
    pieces = [(enc_hbm, enc), (rate_hbm, rate), (coup_hbm, coup)] + [(starts_hbm.at[f], starts.at[f]) for f in range(count)]
    copies = [pltpu.make_async_copy(src, dst, sems.at[i]) for i, (src, dst) in enumerate(pieces)]
    for copy in copies:
        copy.start()
    first = lax.axis_index("cuts") == 0
    given = pltpu.make_async_copy(initial_hbm, initial, sems.at[len(copies)])

    @pl.when(first)
    def _():
        given.start()

    for f in range(count):
        copies[3 + f].wait()
        for a in range(starts.shape[1] // DOWN):
            parts = split_columns(chunks_of(starts, f, 8 * a))
            for q, part in enumerate(parts):
                own_out[f, q, 8 * a : 8 * a + 8, :] = part
            put_blocks(offset_out, f, a, [-part for part in parts])
    for copy in copies[:3]:
        copy.wait()
    enc_out[...] = reordered(enc[...])
    coarse_out[...] = coarse_matrix(rate[...], coup[...])

    @pl.when(first)
    def _():
        given.wait()
        for f in range(count):
            for a in range(starts.shape[1] // DOWN):
                parts = split_columns(chunks_of(initial, f, 8 * a))
                mine = [own_out[f, q, 8 * a : 8 * a + 8, :] for q in range(8)]
                put_blocks(offset_out, f, a, [part - m for part, m in zip(parts, mine)])


def powers_kernel(inner, outer, dec, matrix, total_out, near_out, far_out, held, decoded_held):
    lat = matrix.shape[0]
    inside = lax.axis_index("cuts") % inner
    coarse = matrix[...]
    powers = [identity(lat), coarse]
    for k in range(2, inner + 1):
        powers.append(dot_full(powers[k // 2], powers[k - k // 2]))
    for k, power in enumerate(powers):
        held[k] = power
    weight = reordered(dec[...]).T
    decoded = [weight]
    for d in range(1, inner):
        place = inside ^ d
        part = dot_full(weight, held[jnp.maximum(inside - place, 0)])
        decoded.append(jnp.where(place < inside, part, 0.0))
    near_out[...] = jnp.concatenate(decoded, axis=1)
    total_out[...] = jnp.concatenate([held[inner - 1 - (inside ^ d)] for d in range(inner)], axis=1)
    group = lax.axis_index("cuts") // inner
    far = [dot_full(weight, held[inside + 1])]
    for k in range(2, outer):
        far.append(dot_full(far[-1], powers[inner]))
    for k, part in enumerate(far):
        decoded_held[k] = part
    order = [jnp.maximum(group - 1 - (group ^ d), 0) for d in range(1, outer)]
    far_out[...] = jnp.concatenate([decoded_held[k] for k in order], axis=1)


class Padded:
    def __init__(self, ref, reps):
        self.ref = ref
        self.reps = reps

    def put(self, field, r, q, value, rows=True, cols=True):
        ref, reps = self.ref, self.reps
        ref[field, r + 2, q + 2] = value
        if rows and r < 2:
            ref[field, r + reps + 2, q + 2] = pltpu.roll(value, 7, 0)
        if rows and r >= reps - 2:
            ref[field, r - reps + 2, q + 2] = pltpu.roll(value, 1, 0)
        if cols and q < 2:
            ref[field, r + 2, q + 10] = pltpu.roll(value, LANES - 1, 1)
        if cols and q >= 6:
            ref[field, r + 2, q - 6] = pltpu.roll(value, 1, 1)

    def put_cell(self, r, q, height, along_c, along_r):
        self.put(0, r, q, height)
        self.put(1, r, q, along_c)
        self.put(2, r, q, along_r)
        self.put(3, r, q, along_r + height * along_r, cols=False)
        self.put(4, r, q, along_c + height * along_c, rows=False)

    def cell(self, field, r, q):
        return self.ref[field, r + 2, q + 2]

    def along_rows(self, field, r, q):
        at = self.cell
        return 8.0 * (at(field, r + 1, q) - at(field, r - 1, q)) - (at(field, r + 2, q) - at(field, r - 2, q))


def stage(base, now, reps, alpha, beta, gamma, put):
    scale = gamma / 12.0
    turn = gamma * FCOR
    for r in range(reps):
        window = {f: [now.cell(f, r, q) for q in range(-2, 2)] for f in (0, 1, 2, 4)}
        for q in range(8):
            along_cols = {}
            for f, cells in window.items():
                cells.append(now.cell(f, r, q + 2))
                along_cols[f] = 8.0 * (cells[3] - cells[1]) - (cells[4] - cells[0])
            height, along_c, along_r = (window[f][2] for f in range(3))
            d_height = along_cols[4] + now.along_rows(3, r, q)
            d_colvel = along_c * along_cols[1] + along_r * now.along_rows(1, r, q) + along_cols[0]
            d_rowvel = along_c * along_cols[2] + along_r * now.along_rows(2, r, q) + now.along_rows(0, r, q)
            new = []
            for f, (mine, d, extra) in enumerate(
                ((height, d_height, None), (along_c, d_colvel, turn * along_r), (along_r, d_rowvel, -turn * along_c))
            ):
                total = beta * mine if beta != 1.0 else mine
                if alpha:
                    total = total + alpha * base.cell(f, r, q)
                if extra is not None:
                    total = total + extra
                new.append(total - scale * d)
            put(r, q, *new)
            for cells in window.values():
                del cells[0]


def fine_kernel(own, other, offset, enc, coarse, finals_out, g_out, t_out, rows_buf, buf_a, buf_b, buf_c):
    local_rows = own.shape[2]
    ext = local_rows + other.shape[1]
    reps = ext // 8
    groups = local_rows // DOWN
    for f in range(3):
        for q in range(8):
            rows_buf[f, q, 0:local_rows, :] = own[f, q, :, :]
        for tile in range(other.shape[1] // 8):
            parts = split_columns(chunks_of(other, f, 8 * tile))
            for q in range(8):
                rows_buf[f, q, local_rows + 8 * tile : local_rows + 8 * tile + 8, :] = parts[q]
    t_part = dot3(coarse[...], dot3(enc[...], side_by_side(offset)))
    t_out[...] = t_part
    state, second, third = Padded(buf_a, reps), Padded(buf_b, reps), Padded(buf_c, reps)
    for r in range(reps):
        for q in range(8):
            state.put_cell(r, q, *(rows_buf[f, q, pl.ds(r, 8, stride=reps), :] for f in range(3)))

    def finish(r, q, *cells):
        for f in range(3):
            rows_buf[f, q, pl.ds(r, 8, stride=reps), :] = cells[f]

    for step in range(FINE_STEPS):
        stage(None, state, reps, 0.0, 1.0, TSTEP, second.put_cell)
        stage(state, second, reps, 0.75, 0.25, 0.25 * TSTEP, third.put_cell)
        last = step + 1 == FINE_STEPS
        stage(state, third, reps, 1.0 / 3.0, 2.0 / 3.0, 2.0 / 3.0 * TSTEP, finish if last else state.put_cell)
    for f in range(3):
        for a in range(groups):
            put_blocks(finals_out, f, a, [rows_buf[f, q, 8 * a : 8 * a + 8, :] for q in range(8)])
    g_out[...] = dot3(enc[...], side_by_side(finals_out)) + t_part


def weighted_kernel(*refs):
    *parts, weights, out = refs
    out[...] = dot3(weights[...], jnp.concatenate([part[...] for part in parts], axis=0))


def base_kernel(finals, *refs):
    *parts, weights, out_hbm, out, sems = refs
    change = dot3(weights[...], jnp.concatenate([part[...] for part in parts], axis=0))
    copies = []
    for a in range(finals.shape[0]):
        rows = pl.ds(8 * a, 8)
        for f in range(3):
            places = [slice(64 * f + 8 * q, 64 * f + 8 * q + 8) for q in range(8)]
            joined = join_columns([finals[a, k, :] + change[k, LANES * a : LANES * (a + 1)] for k in places])
            for j, chunk in enumerate(joined):
                out[f, 8 * a : 8 * a + 8, LANES * j : LANES * (j + 1)] = chunk
            copies.append(pltpu.make_async_copy(out.at[f, rows], out_hbm.at[0, f, rows], sems.at[3 * a + f]))
            copies[-1].start()
    for copy in copies:
        copy.wait()


def output_kernel(inner, base, *refs):
    *totals, weights, _, out_hbm, joined_out, sems = refs
    group = lax.axis_index("cuts") // inner

    @pl.when(group > 0)
    def _():
        taken = [jnp.where((group ^ (d + 1)) < group, part[...], 0.0) for d, part in enumerate(totals)]
        change = dot3(weights[...], jnp.concatenate(taken, axis=0))
        copies = []
        for a in range(base.shape[1] // DOWN):
            rows = pl.ds(8 * a, 8)
            for f in range(3):
                places = [slice(64 * f + 8 * q, 64 * f + 8 * q + 8) for q in range(8)]
                joined = join_columns([change[k, LANES * a : LANES * (a + 1)] for k in places])
                for j, chunk in enumerate(joined):
                    cells = (f, slice(8 * a, 8 * a + 8), slice(LANES * j, LANES * (j + 1)))
                    joined_out[cells] = base[cells] + chunk
                copies.append(pltpu.make_async_copy(joined_out.at[f, rows], out_hbm.at[0, f, rows], sems.at[3 * a + f]))
                copies[-1].start()
        for copy in copies:
            copy.wait()


def call(kernel, shapes, inputs, scratch=(), flops=0, inside=None, outside=None, aliases={}):
    return pl.pallas_call(
        kernel,
        out_shape=[jax.ShapeDtypeStruct(s, F32) for s in shapes],
        in_specs=inside or [VMEM] * len(inputs),
        out_specs=outside or [VMEM] * len(shapes),
        scratch_shapes=list(scratch),
        input_output_aliases=aliases,
        compiler_params=pltpu.CompilerParams(vmem_limit_bytes=40 * 1024 * 1024),
        cost_estimate=pl.CostEstimate(
            flops=flops, bytes_accessed=sum(4 * x.size for x in inputs), transcendentals=0
        ),
    )(*inputs)


def neighbour_rows(state):
    count = lax.axis_size("row")
    rows = state.shape[1]
    if count == 1:
        return jnp.concatenate([state[:, :HALO], state[:, rows - HALO :]], axis=1)
    forward = [(i, (i + 1) % count) for i in range(count)]
    backward = [((i + 1) % count, i) for i in range(count)]
    if count == 2 and rows <= 2 * HALO:
        return lax.ppermute(state, "row", forward)
    below = lax.ppermute(state[:, :HALO], "row", backward)
    above = lax.ppermute(state[:, rows - HALO :], "row", forward)
    return jnp.concatenate([below, above], axis=1)


def swapped(value, distance):
    return lax.ppermute(value, "cuts", [(i, i ^ distance) for i in range(lax.axis_size("cuts"))])


def local(starts, initial, encode_weight, decode_weight, latent_rate, coupling):
    lat = coupling.shape[0]
    state = starts[0]
    rows = state.shape[1]
    groups = rows // DOWN
    wide = groups * LANES
    size = encode_weight.shape[1]
    slices = lax.axis_size("cuts")
    inner = 1 << (slices.bit_length() // 2)
    outer = slices // inner
    rate = latent_rate.reshape(1, lat)
    other = neighbour_rows(state)
    given = (state, initial, encode_weight, rate, coupling)
    own, offset, enc, coarse = call(
        split_kernel,
        [(3, 8, rows, LANES), (groups, size, LANES), encode_weight.shape, (lat, lat)],
        [pltpu.with_memory_space_constraint(x, pltpu.HBM) for x in given],
        [pltpu.VMEM(x.shape, F32) for x in given] + [pltpu.SemaphoreType.DMA((7,))],
        flops=100_000_000,
        inside=[pl.BlockSpec(memory_space=pl.ANY)] * len(given),
    )
    reps = (rows + other.shape[1]) // 8
    pad = pltpu.VMEM((5, reps + 4, 12, 8, LANES), F32)
    finals, g_part, t_part = call(
        fine_kernel,
        [(groups, size, LANES), (lat, wide), (lat, wide)],
        [own, other, offset, enc, coarse],
        [pltpu.VMEM((3, 8, 8 * reps, LANES), F32), pad, pad, pad],
        flops=400_000_000,
    )
    parts = [swapped(g_part, d) for d in range(1, inner)]
    to_total, to_near, to_far = call(
        functools.partial(powers_kernel, inner, outer),
        [(lat, inner * lat), (size, inner * lat), (size, (outer - 1) * lat)],
        [decode_weight.T, coarse],
        [pltpu.VMEM((inner + 1, lat, lat), F32), pltpu.VMEM((outer - 1, size, lat), F32)],
        flops=50_000_000,
    )
    (total,) = call(weighted_kernel, [(lat, wide)], [g_part, *parts, to_total], flops=50_000_000)
    totals = [swapped(total, inner * d) for d in range(1, outer)]
    hbm = pl.BlockSpec(memory_space=pltpu.HBM)
    tiles = pltpu.SemaphoreType.DMA((3 * groups,))
    result = (1, *state.shape)
    near_result, base = call(
        base_kernel,
        [result, state.shape],
        [finals, t_part, *parts, to_near],
        [tiles],
        flops=50_000_000,
        outside=[hbm, VMEM],
    )
    (out,) = call(
        functools.partial(output_kernel, inner),
        [result],
        [base, *totals, to_far, near_result],
        [pltpu.VMEM(state.shape, F32), tiles],
        flops=50_000_000,
        inside=[VMEM] * (outer + 1) + [hbm],
        outside=[hbm],
        aliases={outer + 1: 0},
    )
    return out


def solution(mesh):
    return jax.shard_map(
        local,
        mesh=mesh,
        in_specs=(P("cuts", None, "row", None), P(None, "row", None), P(), P(), P(), P()),
        out_specs=P("cuts", None, "row", None),
        check_vma=False,
    )
```

```python
import functools

import jax
import jax.numpy as jnp
from jax import lax
from jax.experimental import pallas as pl
from jax.experimental.pallas import tpu as pltpu
from jax.sharding import PartitionSpec as P

DOWN = 8
FINE_STEPS = 2
FCOR = 0.3
TSTEP = 0.25
HALO = 6 * FINE_STEPS
LANES = 128
F32 = jnp.float32
BF16 = jnp.bfloat16
VMEM = pl.BlockSpec(memory_space=pltpu.VMEM)


def halves(value):
    high = value.astype(BF16)
    return high, (value - high.astype(F32)).astype(BF16)


def dot3(left, right, contract=((1,), (0,))):
    dims = (contract, ((), ()))
    lh, ll = halves(left)
    rh, rl = halves(right)
    one = functools.partial(lax.dot_general, dimension_numbers=dims, preferred_element_type=F32)
    return one(lh, rh) + (one(lh, rl) + one(ll, rh))


def dot_full(left, right):
    return jnp.dot(left, right, precision=lax.Precision.HIGHEST, preferred_element_type=F32)


def lanes_iota():
    return lax.broadcasted_iota(jnp.int32, (8, LANES), 1)


def split_columns(chunks):
    lane = lanes_iota()
    moved = [c if j == 0 else pltpu.roll(c, j, 1) for j, c in enumerate(chunks)]
    phase = lane & 7
    out = []
    for q in range(8):
        merged = moved[0]
        for j in range(1, 8):
            merged = jnp.where(phase == (q + j) % 8, moved[j], merged)
        place = (8 * (lane & 15) + q + (lane >> 4)) & (LANES - 1)
        out.append(jnp.take_along_axis(merged, place, axis=1))
    return out


def join_columns(parts):
    lane = lanes_iota()
    phase = lane & 7
    picked = []
    for q, part in enumerate(parts):
        j = (lane - q) & 7
        place = 16 * j + (((lane - q - j) & (LANES - 1)) >> 3)
        picked.append(jnp.take_along_axis(part, place, axis=1))
    out = []
    for j in range(8):
        merged = picked[(-j) % 8]
        for q in range(8):
            if q != (-j) % 8:
                merged = jnp.where(phase == (q + j) % 8, picked[q], merged)
        out.append(merged if j == 0 else pltpu.roll(merged, LANES - j, 1))
    return out


def chunks_of(ref, field, row):
    return [ref[field, row : row + 8, LANES * j : LANES * (j + 1)] for j in range(8)]


def identity(size):
    rows = lax.broadcasted_iota(jnp.int32, (size, size), 0)
    return (rows == lax.broadcasted_iota(jnp.int32, (size, size), 1)).astype(F32)


def coarse_matrix(rate, coupling):
    return (rate * (identity(coupling.shape[0]) + coupling.T - coupling)).T


def put_blocks(ref, field, group, parts):
    for q, part in enumerate(parts):
        ref[group, 64 * field + 8 * q : 64 * field + 8 * q + 8, :] = part


def reordered(weight):
    size = weight.shape[1]
    source = lax.broadcasted_iota(jnp.int32, (size, size), 0)
    target = lax.broadcasted_iota(jnp.int32, (size, size), 1)
    wanted = (target & ~63) | ((target & 7) << 3) | ((target >> 3) & 7)
    return dot_full(weight, (source == wanted).astype(F32))


def side_by_side(ref):
    return jnp.concatenate([ref[a] for a in range(ref.shape[0])], axis=1)


def split_kernel(starts_hbm, initial_hbm, enc_hbm, rate_hbm, coup_hbm, *refs):
    own_out, offset_out, enc_out, coarse_out, starts, initial, enc, rate, coup, sems = refs
    count = starts.shape[0]
    pieces = [(enc_hbm, enc), (rate_hbm, rate), (coup_hbm, coup)] + [(starts_hbm.at[f], starts.at[f]) for f in range(count)]
    copies = [pltpu.make_async_copy(src, dst, sems.at[i]) for i, (src, dst) in enumerate(pieces)]
    for copy in copies[3:] + copies[:3]:
        copy.start()
    first = lax.axis_index("cuts") == 0
    given = pltpu.make_async_copy(initial_hbm, initial, sems.at[len(copies)])

    @pl.when(first)
    def _():
        given.start()

    for copy in copies:
        copy.wait()
    enc_out[...] = reordered(enc[...])
    coarse_out[...] = coarse_matrix(rate[...], coup[...])
    for f in range(count):
        for a in range(starts.shape[1] // DOWN):
            parts = split_columns(chunks_of(starts, f, 8 * a))
            for q, part in enumerate(parts):
                own_out[f, q, 8 * a : 8 * a + 8, :] = part
            put_blocks(offset_out, f, a, [-part for part in parts])

    @pl.when(first)
    def _():
        given.wait()
        for f in range(count):
            for a in range(starts.shape[1] // DOWN):
                parts = split_columns(chunks_of(initial, f, 8 * a))
                mine = [own_out[f, q, 8 * a : 8 * a + 8, :] for q in range(8)]
                put_blocks(offset_out, f, a, [part - m for part, m in zip(parts, mine)])


def powers_kernel(inner, order, dec, matrix, total_out, near_out, far_out, held, decoded_held):
    lat = matrix.shape[0]
    inside = lax.axis_index("cuts") % inner
    coarse = matrix[...]
    powers = [identity(lat), coarse]
    for k in range(2, inner + 1):
        powers.append(dot_full(powers[k // 2], powers[k - k // 2]))
    for k, power in enumerate(powers):
        held[k] = power
    weight = reordered(dec[...]).T
    decoded = [weight]
    for d in range(1, inner):
        place = inside ^ d
        part = dot_full(weight, held[jnp.maximum(inside - place, 0)])
        decoded.append(jnp.where(place < inside, part, 0.0))
    near_out[...] = jnp.concatenate(decoded, axis=1)
    total_out[...] = jnp.concatenate([held[inner - 1 - (inside ^ d)] for d in range(inner)], axis=1)
    group = lax.axis_index("cuts") // inner
    far = [dot_full(weight, held[inside + 1])]
    for k in range(2, len(order) + 1):
        far.append(dot_full(far[-1], powers[inner]))
    for k, part in enumerate(far):
        decoded_held[k] = part
    picked = [decoded_held[jnp.maximum(group - 1 - (group ^ d), 0)] for d in order]
    far_out[...] = jnp.concatenate(picked, axis=1)


class Padded:
    def __init__(self, ref, reps):
        self.ref = ref
        self.reps = reps

    def put(self, field, r, q, value, rows=True, cols=True):
        ref, reps = self.ref, self.reps
        ref[field, r + 2, q + 2] = value
        if rows and r < 2:
            ref[field, r + reps + 2, q + 2] = pltpu.roll(value, 7, 0)
        if rows and r >= reps - 2:
            ref[field, r - reps + 2, q + 2] = pltpu.roll(value, 1, 0)
        if cols and q < 2:
            ref[field, r + 2, q + 10] = pltpu.roll(value, LANES - 1, 1)
        if cols and q >= 6:
            ref[field, r + 2, q - 6] = pltpu.roll(value, 1, 1)

    def put_cell(self, r, q, height, along_c, along_r):
        self.put(0, r, q, height)
        self.put(1, r, q, along_c)
        self.put(2, r, q, along_r)
        self.put(3, r, q, along_r + height * along_r, cols=False)
        self.put(4, r, q, along_c + height * along_c, rows=False)

    def cell(self, field, r, q):
        return self.ref[field, r + 2, q + 2]

    def along_rows(self, field, r, q):
        at = self.cell
        return 8.0 * (at(field, r + 1, q) - at(field, r - 1, q)) - (at(field, r + 2, q) - at(field, r - 2, q))


def stage(base, now, reps, alpha, beta, gamma, put):
    scale = gamma / 12.0
    turn = 12.0 * FCOR
    for r in range(reps):
        window = {f: [now.cell(f, r, q) for q in range(-2, 2)] for f in (0, 1, 2, 4)}
        for q in range(8):
            along_cols = {}
            for f, cells in window.items():
                cells.append(now.cell(f, r, q + 2))
                along_cols[f] = 8.0 * (cells[3] - cells[1]) - (cells[4] - cells[0])
            height, along_c, along_r = (window[f][2] for f in range(3))
            d_height = along_cols[4] + now.along_rows(3, r, q)
            d_colvel = along_c * along_cols[1] + along_r * (now.along_rows(1, r, q) - turn) + along_cols[0]
            d_rowvel = along_c * (along_cols[2] + turn) + along_r * now.along_rows(2, r, q) + now.along_rows(0, r, q)
            new = []
            for f, (mine, d) in enumerate(((height, d_height), (along_c, d_colvel), (along_r, d_rowvel))):
                total = beta * mine if beta != 1.0 else mine
                if alpha:
                    total = total + alpha * base.cell(f, r, q)
                new.append(total - scale * d)
            put(r, q, *new)
            for cells in window.values():
                del cells[0]


def fine_kernel(own, other, offset, enc, coarse, finals_out, g_out, t_out, rows_buf, buf_a, buf_b, buf_c):
    local_rows = own.shape[2]
    ext = local_rows + other.shape[1]
    reps = ext // 8
    groups = local_rows // DOWN
    for f in range(3):
        for q in range(8):
            rows_buf[f, q, 0:local_rows, :] = own[f, q, :, :]
        for tile in range(other.shape[1] // 8):
            parts = split_columns(chunks_of(other, f, 8 * tile))
            for q in range(8):
                rows_buf[f, q, local_rows + 8 * tile : local_rows + 8 * tile + 8, :] = parts[q]
    t_part = dot3(coarse[...], dot3(enc[...], side_by_side(offset)))
    t_out[...] = t_part
    state, second, third = Padded(buf_a, reps), Padded(buf_b, reps), Padded(buf_c, reps)
    for r in range(reps):
        for q in range(8):
            state.put_cell(r, q, *(rows_buf[f, q, pl.ds(r, 8, stride=reps), :] for f in range(3)))

    def finish(r, q, *cells):
        for f in range(3):
            rows_buf[f, q, pl.ds(r, 8, stride=reps), :] = cells[f]

    for step in range(FINE_STEPS):
        stage(None, state, reps, 0.0, 1.0, TSTEP, second.put_cell)
        stage(state, second, reps, 0.75, 0.25, 0.25 * TSTEP, third.put_cell)
        last = step + 1 == FINE_STEPS
        stage(state, third, reps, 1.0 / 3.0, 2.0 / 3.0, 2.0 / 3.0 * TSTEP, finish if last else state.put_cell)
    for f in range(3):
        for a in range(groups):
            put_blocks(finals_out, f, a, [rows_buf[f, q, 8 * a : 8 * a + 8, :] for q in range(8)])
    g_out[...] = dot3(enc[...], side_by_side(finals_out)) + t_part


def weighted_kernel(*refs):
    *parts, weights, out = refs
    out[...] = dot3(weights[...], jnp.concatenate([part[...] for part in parts], axis=0))


def base_kernel(finals, *refs):
    *parts, weights, out_hbm, out, sems = refs
    change = dot3(weights[...], jnp.concatenate([part[...] for part in parts], axis=0))
    copies = []
    for a in range(finals.shape[0]):
        rows = pl.ds(8 * a, 8)
        for f in range(3):
            places = [slice(64 * f + 8 * q, 64 * f + 8 * q + 8) for q in range(8)]
            joined = join_columns([finals[a, k, :] + change[k, LANES * a : LANES * (a + 1)] for k in places])
            for j, chunk in enumerate(joined):
                out[f, 8 * a : 8 * a + 8, LANES * j : LANES * (j + 1)] = chunk
            copies.append(pltpu.make_async_copy(out.at[f, rows], out_hbm.at[0, f, rows], sems.at[3 * a + f]))
            copies[-1].start()
    for copy in copies:
        copy.wait()


def output_kernel(inner, order, base, *refs):
    *totals, weights, _, out_hbm, joined_out, sems = refs
    group = lax.axis_index("cuts") // inner

    @pl.when(group > 0)
    def _():
        taken = [jnp.where((group ^ d) < group, part[...], 0.0) for d, part in zip(order, totals)]
        change = dot3(weights[...], jnp.concatenate(taken, axis=0))
        copies = []
        for a in range(base.shape[1] // DOWN):
            rows = pl.ds(8 * a, 8)
            for f in range(3):
                places = [slice(64 * f + 8 * q, 64 * f + 8 * q + 8) for q in range(8)]
                joined = join_columns([change[k, LANES * a : LANES * (a + 1)] for k in places])
                for j, chunk in enumerate(joined):
                    cells = (f, slice(8 * a, 8 * a + 8), slice(LANES * j, LANES * (j + 1)))
                    joined_out[cells] = base[cells] + chunk
                copies.append(pltpu.make_async_copy(joined_out.at[f, rows], out_hbm.at[0, f, rows], sems.at[3 * a + f]))
                copies[-1].start()
        for copy in copies:
            copy.wait()


def call(kernel, shapes, inputs, scratch=(), flops=0, inside=None, outside=None, aliases={}):
    return pl.pallas_call(
        kernel,
        out_shape=[jax.ShapeDtypeStruct(s, F32) for s in shapes],
        in_specs=inside or [VMEM] * len(inputs),
        out_specs=outside or [VMEM] * len(shapes),
        scratch_shapes=list(scratch),
        input_output_aliases=aliases,
        compiler_params=pltpu.CompilerParams(vmem_limit_bytes=40 * 1024 * 1024),
        cost_estimate=pl.CostEstimate(
            flops=flops, bytes_accessed=sum(4 * x.size for x in inputs), transcendentals=0
        ),
    )(*inputs)


def neighbour_rows(state):
    count = lax.axis_size("row")
    rows = state.shape[1]
    if count == 1:
        return jnp.concatenate([state[:, :HALO], state[:, rows - HALO :]], axis=1)
    forward = [(i, (i + 1) % count) for i in range(count)]
    backward = [((i + 1) % count, i) for i in range(count)]
    if count == 2 and rows <= 2 * HALO:
        return lax.ppermute(state, "row", forward)
    below = lax.ppermute(state[:, :HALO], "row", backward)
    above = lax.ppermute(state[:, rows - HALO :], "row", forward)
    return jnp.concatenate([below, above], axis=1)


def swapped(value, distance):
    return lax.ppermute(value, "cuts", [(i, i ^ distance) for i in range(lax.axis_size("cuts"))])


def local(starts, initial, encode_weight, decode_weight, latent_rate, coupling):
    lat = coupling.shape[0]
    state = starts[0]
    rows = state.shape[1]
    groups = rows // DOWN
    wide = groups * LANES
    size = encode_weight.shape[1]
    slices = lax.axis_size("cuts")
    inner = 1 << (slices.bit_length() // 2)
    outer = slices // inner
    order = (1, *range(outer - 1, 1, -1))
    rate = latent_rate.reshape(1, lat)
    other = neighbour_rows(state)
    given = (state, initial, encode_weight, rate, coupling)
    own, offset, enc, coarse = call(
        split_kernel,
        [(3, 8, rows, LANES), (groups, size, LANES), encode_weight.shape, (lat, lat)],
        [pltpu.with_memory_space_constraint(x, pltpu.HBM) for x in given],
        [pltpu.VMEM(x.shape, F32) for x in given] + [pltpu.SemaphoreType.DMA((7,))],
        flops=100_000_000,
        inside=[pl.BlockSpec(memory_space=pl.ANY)] * len(given),
    )
    reps = (rows + other.shape[1]) // 8
    pad = pltpu.VMEM((5, reps + 4, 12, 8, LANES), F32)
    finals, g_part, t_part = call(
        fine_kernel,
        [(groups, size, LANES), (lat, wide), (lat, wide)],
        [own, other, offset, enc, coarse],
        [pltpu.VMEM((3, 8, 8 * reps, LANES), F32), pad, pad, pad],
        flops=400_000_000,
    )
    parts = [swapped(g_part, d) for d in range(1, inner)]
    to_total, to_near, to_far = call(
        functools.partial(powers_kernel, inner, order),
        [(lat, inner * lat), (size, inner * lat), (size, (outer - 1) * lat)],
        [decode_weight.T, coarse],
        [pltpu.VMEM((inner + 1, lat, lat), F32), pltpu.VMEM((outer - 1, size, lat), F32)],
        flops=50_000_000,
    )
    (total,) = call(weighted_kernel, [(lat, wide)], [g_part, *parts, to_total], flops=50_000_000)
    totals = [swapped(total, inner * d) for d in order]
    hbm = pl.BlockSpec(memory_space=pltpu.HBM)
    tiles = pltpu.SemaphoreType.DMA((3 * groups,))
    result = (1, *state.shape)
    near_result, base = call(
        base_kernel,
        [result, state.shape],
        [finals, t_part, *parts, to_near],
        [tiles],
        flops=50_000_000,
        outside=[hbm, VMEM],
    )
    (out,) = call(
        functools.partial(output_kernel, inner, order),
        [result],
        [base, *totals, to_far, near_result],
        [pltpu.VMEM(state.shape, F32), tiles],
        flops=50_000_000,
        inside=[VMEM] * (outer + 1) + [hbm],
        outside=[hbm],
        aliases={outer + 1: 0},
    )
    return out


def solution(mesh):
    return jax.shard_map(
        local,
        mesh=mesh,
        in_specs=(P("cuts", None, "row", None), P(None, "row", None), P(), P(), P(), P()),
        out_specs=P("cuts", None, "row", None),
        check_vma=False,
    )
```

```python
import functools

import jax
import jax.numpy as jnp
from jax import lax
from jax.experimental import pallas as pl
from jax.experimental.pallas import tpu as pltpu
from jax.sharding import PartitionSpec as P

DOWN = 8
FINE_STEPS = 2
FCOR = 0.3
TSTEP = 0.25
HALO = 6 * FINE_STEPS
LANES = 128
F32 = jnp.float32
BF16 = jnp.bfloat16
VMEM = pl.BlockSpec(memory_space=pltpu.VMEM)


def halves(value):
    high = value.astype(BF16)
    return high, (value - high.astype(F32)).astype(BF16)


def dot3(left, right, contract=((1,), (0,))):
    dims = (contract, ((), ()))
    lh, ll = halves(left)
    rh, rl = halves(right)
    one = functools.partial(lax.dot_general, dimension_numbers=dims, preferred_element_type=F32)
    return one(lh, rh) + (one(lh, rl) + one(ll, rh))


def dot_full(left, right):
    return jnp.dot(left, right, precision=lax.Precision.HIGHEST, preferred_element_type=F32)


def lanes_iota():
    return lax.broadcasted_iota(jnp.int32, (8, LANES), 1)


def split_columns(chunks):
    lane = lanes_iota()
    moved = [c if j == 0 else pltpu.roll(c, j, 1) for j, c in enumerate(chunks)]
    phase = lane & 7
    out = []
    for q in range(8):
        merged = moved[0]
        for j in range(1, 8):
            merged = jnp.where(phase == (q + j) % 8, moved[j], merged)
        place = (8 * (lane & 15) + q + (lane >> 4)) & (LANES - 1)
        out.append(jnp.take_along_axis(merged, place, axis=1))
    return out


def join_columns(parts):
    lane = lanes_iota()
    phase = lane & 7
    picked = []
    for q, part in enumerate(parts):
        j = (lane - q) & 7
        place = 16 * j + (((lane - q - j) & (LANES - 1)) >> 3)
        picked.append(jnp.take_along_axis(part, place, axis=1))
    out = []
    for j in range(8):
        merged = picked[(-j) % 8]
        for q in range(8):
            if q != (-j) % 8:
                merged = jnp.where(phase == (q + j) % 8, picked[q], merged)
        out.append(merged if j == 0 else pltpu.roll(merged, LANES - j, 1))
    return out


def chunks_of(ref, field, row):
    return [ref[field, row : row + 8, LANES * j : LANES * (j + 1)] for j in range(8)]


def identity(size):
    rows = lax.broadcasted_iota(jnp.int32, (size, size), 0)
    return (rows == lax.broadcasted_iota(jnp.int32, (size, size), 1)).astype(F32)


def coarse_matrix(rate, coupling):
    return (rate * (identity(coupling.shape[0]) + coupling.T - coupling)).T


def put_blocks(ref, field, group, parts):
    for q, part in enumerate(parts):
        ref[group, 64 * field + 8 * q : 64 * field + 8 * q + 8, :] = part


def reordered(weight):
    size = weight.shape[1]
    source = lax.broadcasted_iota(jnp.int32, (size, size), 0)
    target = lax.broadcasted_iota(jnp.int32, (size, size), 1)
    wanted = (target & ~63) | ((target & 7) << 3) | ((target >> 3) & 7)
    return dot_full(weight, (source == wanted).astype(F32))


def side_by_side(ref):
    return jnp.concatenate([ref[a] for a in range(ref.shape[0])], axis=1)


def split_kernel(starts_hbm, initial_hbm, enc_hbm, rate_hbm, coup_hbm, *refs):
    own_out, offset_out, enc_out, coarse_out, starts, initial, enc, rate, coup, sems = refs
    count = starts.shape[0]
    pieces = [(enc_hbm, enc), (rate_hbm, rate), (coup_hbm, coup)] + [(starts_hbm.at[f], starts.at[f]) for f in range(count)]
    copies = [pltpu.make_async_copy(src, dst, sems.at[i]) for i, (src, dst) in enumerate(pieces)]
    for copy in copies[3:] + copies[:3]:
        copy.start()
    first = lax.axis_index("cuts") == 0
    given = pltpu.make_async_copy(initial_hbm, initial, sems.at[len(copies)])

    @pl.when(first)
    def _():
        given.start()

    for copy in copies:
        copy.wait()
    enc_out[...] = reordered(enc[...])
    coarse_out[...] = coarse_matrix(rate[...], coup[...])
    for f in range(count):
        for a in range(starts.shape[1] // DOWN):
            parts = split_columns(chunks_of(starts, f, 8 * a))
            for q, part in enumerate(parts):
                own_out[f, q, 8 * a : 8 * a + 8, :] = part
            put_blocks(offset_out, f, a, [-part for part in parts])

    @pl.when(first)
    def _():
        given.wait()
        for f in range(count):
            for a in range(starts.shape[1] // DOWN):
                parts = split_columns(chunks_of(initial, f, 8 * a))
                mine = [own_out[f, q, 8 * a : 8 * a + 8, :] for q in range(8)]
                put_blocks(offset_out, f, a, [part - m for part, m in zip(parts, mine)])


def powers_kernel(inner, near_order, far_order, dec, matrix, total_out, near_out, far_out, held, decoded_held):
    lat = matrix.shape[0]
    inside = lax.axis_index("cuts") % inner
    coarse = matrix[...]
    powers = [identity(lat), coarse]
    for k in range(2, inner + 1):
        powers.append(dot_full(powers[k // 2], powers[k - k // 2]))
    for k, power in enumerate(powers):
        held[k] = power
    weight = reordered(dec[...]).T
    decoded = [weight]
    for d in near_order:
        place = inside ^ d
        part = dot_full(weight, held[jnp.maximum(inside - place, 0)])
        decoded.append(jnp.where(place < inside, part, 0.0))
    near_out[...] = jnp.concatenate(decoded, axis=1)
    total_out[...] = jnp.concatenate([held[inner - 1 - (inside ^ d)] for d in (0, *near_order)], axis=1)
    group = lax.axis_index("cuts") // inner
    far = [dot_full(weight, held[inside + 1])]
    for k in range(2, len(far_order) + 1):
        far.append(dot_full(far[-1], powers[inner]))
    for k, part in enumerate(far):
        decoded_held[k] = part
    picked = [decoded_held[jnp.maximum(group - 1 - (group ^ d), 0)] for d in far_order]
    far_out[...] = jnp.concatenate(picked, axis=1)


class Padded:
    def __init__(self, ref, reps):
        self.ref = ref
        self.reps = reps

    def put(self, field, r, q, value, rows=True, cols=True):
        ref, reps = self.ref, self.reps
        ref[field, r + 2, q + 2] = value
        if rows and r < 2:
            ref[field, r + reps + 2, q + 2] = pltpu.roll(value, 7, 0)
        if rows and r >= reps - 2:
            ref[field, r - reps + 2, q + 2] = pltpu.roll(value, 1, 0)
        if cols and q < 2:
            ref[field, r + 2, q + 10] = pltpu.roll(value, LANES - 1, 1)
        if cols and q >= 6:
            ref[field, r + 2, q - 6] = pltpu.roll(value, 1, 1)

    def put_cell(self, r, q, height, along_c, along_r):
        self.put(0, r, q, height)
        self.put(1, r, q, along_c)
        self.put(2, r, q, along_r)
        self.put(3, r, q, along_r + height * along_r, cols=False)
        self.put(4, r, q, along_c + height * along_c, rows=False)

    def cell(self, field, r, q):
        return self.ref[field, r + 2, q + 2]

    def along_rows(self, field, r, q):
        at = self.cell
        return 8.0 * (at(field, r + 1, q) - at(field, r - 1, q)) - (at(field, r + 2, q) - at(field, r - 2, q))


def stage(base, now, reps, alpha, beta, gamma, put):
    scale = gamma / 12.0
    turn = 12.0 * FCOR
    for r in range(reps):
        window = {f: [now.cell(f, r, q) for q in range(-2, 2)] for f in (0, 1, 2, 4)}
        for q in range(8):
            along_cols = {}
            for f, cells in window.items():
                cells.append(now.cell(f, r, q + 2))
                along_cols[f] = 8.0 * (cells[3] - cells[1]) - (cells[4] - cells[0])
            height, along_c, along_r = (window[f][2] for f in range(3))
            d_height = along_cols[4] + now.along_rows(3, r, q)
            d_colvel = along_c * along_cols[1] + along_r * (now.along_rows(1, r, q) - turn) + along_cols[0]
            d_rowvel = along_c * (along_cols[2] + turn) + along_r * now.along_rows(2, r, q) + now.along_rows(0, r, q)
            new = []
            for f, (mine, d) in enumerate(((height, d_height), (along_c, d_colvel), (along_r, d_rowvel))):
                total = beta * mine if beta != 1.0 else mine
                if alpha:
                    total = total + alpha * base.cell(f, r, q)
                new.append(total - scale * d)
            put(r, q, *new)
            for cells in window.values():
                del cells[0]


def fine_solve(own, other, finals, rows_buf, buf_a, buf_b, buf_c):
    local_rows = own.shape[2]
    ext = local_rows + other.shape[1]
    reps = ext // 8
    for f in range(3):
        for q in range(8):
            rows_buf[f, q, 0:local_rows, :] = own[f, q, :, :]
        for tile in range(other.shape[1] // 8):
            parts = split_columns(chunks_of(other, f, 8 * tile))
            for q in range(8):
                rows_buf[f, q, local_rows + 8 * tile : local_rows + 8 * tile + 8, :] = parts[q]
    state, second, third = Padded(buf_a, reps), Padded(buf_b, reps), Padded(buf_c, reps)
    for r in range(reps):
        for q in range(8):
            state.put_cell(r, q, *(rows_buf[f, q, pl.ds(r, 8, stride=reps), :] for f in range(3)))

    def finish(r, q, *cells):
        for f in range(3):
            rows_buf[f, q, pl.ds(r, 8, stride=reps), :] = cells[f]

    for step in range(FINE_STEPS):
        stage(None, state, reps, 0.0, 1.0, TSTEP, second.put_cell)
        stage(state, second, reps, 0.75, 0.25, 0.25 * TSTEP, third.put_cell)
        last = step + 1 == FINE_STEPS
        stage(state, third, reps, 1.0 / 3.0, 2.0 / 3.0, 2.0 / 3.0 * TSTEP, finish if last else state.put_cell)
    for f in range(3):
        for a in range(local_rows // DOWN):
            put_blocks(finals, f, a, [rows_buf[f, q, 8 * a : 8 * a + 8, :] for q in range(8)])


def last_slice():
    return lax.axis_index("cuts") == lax.axis_size("cuts") - 1


def fine_kernel(own, other, offset, enc, coarse, finals_out, g_out, t_out, *buffers):
    last = last_slice()

    @pl.when(jnp.logical_not(last))
    def _():
        t_part = dot3(coarse[...], dot3(enc[...], side_by_side(offset)))
        t_out[...] = t_part
        fine_solve(own, other, finals_out, *buffers)
        g_out[...] = dot3(enc[...], side_by_side(finals_out)) + t_part

    @pl.when(last)
    def _():
        t_part = dot3(coarse[...], dot3(enc[...], side_by_side(offset)))
        t_out[...] = t_part
        g_out[...] = t_part


def weighted_kernel(*refs):
    *parts, weights, out = refs
    out[...] = dot3(weights[...], jnp.concatenate([part[...] for part in parts], axis=0))


def base_kernel(own, other, given, *refs):
    *parts, weights, out_hbm, out, finals, sems, rows_buf, buf_a, buf_b, buf_c = refs
    last = last_slice()

    @pl.when(last)
    def _():
        fine_solve(own, other, finals, rows_buf, buf_a, buf_b, buf_c)

    @pl.when(jnp.logical_not(last))
    def _():
        finals[...] = given[...]

    change = dot3(weights[...], jnp.concatenate([part[...] for part in parts], axis=0))
    copies = []
    for a in range(finals.shape[0]):
        rows = pl.ds(8 * a, 8)
        for f in range(3):
            places = [slice(64 * f + 8 * q, 64 * f + 8 * q + 8) for q in range(8)]
            joined = join_columns([finals[a, k, :] + change[k, LANES * a : LANES * (a + 1)] for k in places])
            for j, chunk in enumerate(joined):
                out[f, 8 * a : 8 * a + 8, LANES * j : LANES * (j + 1)] = chunk
            copies.append(pltpu.make_async_copy(out.at[f, rows], out_hbm.at[0, f, rows], sems.at[3 * a + f]))
            copies[-1].start()
    for copy in copies:
        copy.wait()


def output_kernel(inner, order, base, *refs):
    *totals, weights, _, out_hbm, joined_out, sems = refs
    group = lax.axis_index("cuts") // inner

    @pl.when(group > 0)
    def _():
        taken = [jnp.where((group ^ d) < group, part[...], 0.0) for d, part in zip(order, totals)]
        change = dot3(weights[...], jnp.concatenate(taken, axis=0))
        copies = []
        for a in range(base.shape[1] // DOWN):
            rows = pl.ds(8 * a, 8)
            for f in range(3):
                places = [slice(64 * f + 8 * q, 64 * f + 8 * q + 8) for q in range(8)]
                joined = join_columns([change[k, LANES * a : LANES * (a + 1)] for k in places])
                for j, chunk in enumerate(joined):
                    cells = (f, slice(8 * a, 8 * a + 8), slice(LANES * j, LANES * (j + 1)))
                    joined_out[cells] = base[cells] + chunk
                copies.append(pltpu.make_async_copy(joined_out.at[f, rows], out_hbm.at[0, f, rows], sems.at[3 * a + f]))
                copies[-1].start()
        for copy in copies:
            copy.wait()


def call(kernel, shapes, inputs, scratch=(), flops=0, inside=None, outside=None, aliases={}):
    return pl.pallas_call(
        kernel,
        out_shape=[jax.ShapeDtypeStruct(s, F32) for s in shapes],
        in_specs=inside or [VMEM] * len(inputs),
        out_specs=outside or [VMEM] * len(shapes),
        scratch_shapes=list(scratch),
        input_output_aliases=aliases,
        compiler_params=pltpu.CompilerParams(vmem_limit_bytes=40 * 1024 * 1024),
        cost_estimate=pl.CostEstimate(
            flops=flops, bytes_accessed=sum(4 * x.size for x in inputs), transcendentals=0
        ),
    )(*inputs)


def neighbour_rows(state):
    count = lax.axis_size("row")
    rows = state.shape[1]
    if count == 1:
        return jnp.concatenate([state[:, :HALO], state[:, rows - HALO :]], axis=1)
    forward = [(i, (i + 1) % count) for i in range(count)]
    backward = [((i + 1) % count, i) for i in range(count)]
    if count == 2 and rows <= 2 * HALO:
        return lax.ppermute(state, "row", forward)
    below = lax.ppermute(state[:, :HALO], "row", backward)
    above = lax.ppermute(state[:, rows - HALO :], "row", forward)
    return jnp.concatenate([below, above], axis=1)


def swapped(value, distance):
    return lax.ppermute(value, "cuts", [(i, i ^ distance) for i in range(lax.axis_size("cuts"))])


def local(starts, initial, encode_weight, decode_weight, latent_rate, coupling):
    lat = coupling.shape[0]
    state = starts[0]
    rows = state.shape[1]
    groups = rows // DOWN
    wide = groups * LANES
    size = encode_weight.shape[1]
    slices = lax.axis_size("cuts")
    inner = 1 << (slices.bit_length() // 2)
    outer = slices // inner
    near_order = (2, 1, *range(3, inner)) if inner > 2 else tuple(range(1, inner))
    far_order = tuple(range(1, outer))
    rate = latent_rate.reshape(1, lat)
    other = neighbour_rows(state)
    given = (state, initial, encode_weight, rate, coupling)
    own, offset, enc, coarse = call(
        split_kernel,
        [(3, 8, rows, LANES), (groups, size, LANES), encode_weight.shape, (lat, lat)],
        [pltpu.with_memory_space_constraint(x, pltpu.HBM) for x in given],
        [pltpu.VMEM(x.shape, F32) for x in given] + [pltpu.SemaphoreType.DMA((7,))],
        flops=100_000_000,
        inside=[pl.BlockSpec(memory_space=pl.ANY)] * len(given),
    )
    reps = (rows + other.shape[1]) // 8
    pad = pltpu.VMEM((5, reps + 4, 12, 8, LANES), F32)
    buffers = [pltpu.VMEM((3, 8, 8 * reps, LANES), F32), pad, pad, pad]
    finals, g_part, t_part = call(
        fine_kernel,
        [(groups, size, LANES), (lat, wide), (lat, wide)],
        [own, other, offset, enc, coarse],
        buffers,
        flops=400_000_000,
    )
    parts = [swapped(g_part, d) for d in near_order]
    to_total, to_near, to_far = call(
        functools.partial(powers_kernel, inner, near_order, far_order),
        [(lat, inner * lat), (size, inner * lat), (size, (outer - 1) * lat)],
        [decode_weight.T, coarse],
        [pltpu.VMEM((inner + 1, lat, lat), F32), pltpu.VMEM((outer - 1, size, lat), F32)],
        flops=50_000_000,
    )
    (total,) = call(weighted_kernel, [(lat, wide)], [g_part, *parts, to_total], flops=50_000_000)
    totals = [swapped(total, inner * d) for d in far_order]
    hbm = pl.BlockSpec(memory_space=pltpu.HBM)
    tiles = pltpu.SemaphoreType.DMA((3 * groups,))
    result = (1, *state.shape)
    near_result, base = call(
        base_kernel,
        [result, state.shape],
        [own, other, finals, t_part, *parts, to_near],
        [pltpu.VMEM((groups, size, LANES), F32), tiles, *buffers],
        flops=50_000_000,
        outside=[hbm, VMEM],
    )
    (out,) = call(
        functools.partial(output_kernel, inner, far_order),
        [result],
        [base, *totals, to_far, near_result],
        [pltpu.VMEM(state.shape, F32), tiles],
        flops=50_000_000,
        inside=[VMEM] * (outer + 1) + [hbm],
        outside=[hbm],
        aliases={outer + 1: 0},
    )
    return out


def solution(mesh):
    return jax.shard_map(
        local,
        mesh=mesh,
        in_specs=(P("cuts", None, "row", None), P(None, "row", None), P(), P(), P(), P()),
        out_specs=P("cuts", None, "row", None),
        check_vma=False,
    )
```

```python
import functools

import jax
import jax.numpy as jnp
from jax import lax
from jax.experimental import pallas as pl
from jax.experimental.pallas import tpu as pltpu
from jax.sharding import PartitionSpec as P

DOWN = 8
FINE_STEPS = 2
FCOR = 0.3
TSTEP = 0.25
HALO = 6 * FINE_STEPS
LANES = 128
F32 = jnp.float32
BF16 = jnp.bfloat16
VMEM = pl.BlockSpec(memory_space=pltpu.VMEM)


def halves(value):
    high = value.astype(BF16)
    return high, (value - high.astype(F32)).astype(BF16)


def dot3(left, right, contract=((1,), (0,))):
    dims = (contract, ((), ()))
    lh, ll = halves(left)
    rh, rl = halves(right)
    one = functools.partial(lax.dot_general, dimension_numbers=dims, preferred_element_type=F32)
    return one(lh, rh) + (one(lh, rl) + one(ll, rh))


def dot_full(left, right):
    return jnp.dot(left, right, precision=lax.Precision.HIGHEST, preferred_element_type=F32)


def lanes_iota():
    return lax.broadcasted_iota(jnp.int32, (8, LANES), 1)


def split_columns(chunks):
    lane = lanes_iota()
    moved = [c if j == 0 else pltpu.roll(c, j, 1) for j, c in enumerate(chunks)]
    phase = lane & 7
    out = []
    for q in range(8):
        merged = moved[0]
        for j in range(1, 8):
            merged = jnp.where(phase == (q + j) % 8, moved[j], merged)
        place = (8 * (lane & 15) + q + (lane >> 4)) & (LANES - 1)
        out.append(jnp.take_along_axis(merged, place, axis=1))
    return out


def join_columns(parts):
    lane = lanes_iota()
    phase = lane & 7
    picked = []
    for q, part in enumerate(parts):
        j = (lane - q) & 7
        place = 16 * j + (((lane - q - j) & (LANES - 1)) >> 3)
        picked.append(jnp.take_along_axis(part, place, axis=1))
    out = []
    for j in range(8):
        merged = picked[(-j) % 8]
        for q in range(8):
            if q != (-j) % 8:
                merged = jnp.where(phase == (q + j) % 8, picked[q], merged)
        out.append(merged if j == 0 else pltpu.roll(merged, LANES - j, 1))
    return out


def chunks_of(ref, field, row):
    return [ref[field, row : row + 8, LANES * j : LANES * (j + 1)] for j in range(8)]


def identity(size):
    rows = lax.broadcasted_iota(jnp.int32, (size, size), 0)
    return (rows == lax.broadcasted_iota(jnp.int32, (size, size), 1)).astype(F32)


def coarse_matrix(rate, coupling):
    return (rate * (identity(coupling.shape[0]) + coupling.T - coupling)).T


def put_blocks(ref, field, group, parts):
    for q, part in enumerate(parts):
        ref[group, 64 * field + 8 * q : 64 * field + 8 * q + 8, :] = part


def reordered(weight):
    size = weight.shape[1]
    source = lax.broadcasted_iota(jnp.int32, (size, size), 0)
    target = lax.broadcasted_iota(jnp.int32, (size, size), 1)
    wanted = (target & ~63) | ((target & 7) << 3) | ((target >> 3) & 7)
    return dot_full(weight, (source == wanted).astype(F32))


def side_by_side(ref):
    return jnp.concatenate([ref[a] for a in range(ref.shape[0])], axis=1)


def split_kernel(starts_hbm, initial_hbm, enc_hbm, rate_hbm, coup_hbm, *refs):
    own_out, offset_out, enc_out, coarse_out, starts, initial, enc, rate, coup, sems = refs
    count = starts.shape[0]
    pieces = [(enc_hbm, enc), (rate_hbm, rate), (coup_hbm, coup)] + [(starts_hbm.at[f], starts.at[f]) for f in range(count)]
    copies = [pltpu.make_async_copy(src, dst, sems.at[i]) for i, (src, dst) in enumerate(pieces)]
    for copy in copies[3:] + copies[:3]:
        copy.start()
    first = lax.axis_index("cuts") == 0
    given = pltpu.make_async_copy(initial_hbm, initial, sems.at[len(copies)])

    @pl.when(first)
    def _():
        given.start()

    for copy in copies:
        copy.wait()
    enc_out[...] = reordered(enc[...])
    coarse_out[...] = coarse_matrix(rate[...], coup[...])
    for f in range(count):
        for a in range(starts.shape[1] // DOWN):
            parts = split_columns(chunks_of(starts, f, 8 * a))
            for q, part in enumerate(parts):
                own_out[f, q, 8 * a : 8 * a + 8, :] = part
            put_blocks(offset_out, f, a, [-part for part in parts])

    @pl.when(first)
    def _():
        given.wait()
        for f in range(count):
            for a in range(starts.shape[1] // DOWN):
                parts = split_columns(chunks_of(initial, f, 8 * a))
                mine = [own_out[f, q, 8 * a : 8 * a + 8, :] for q in range(8)]
                put_blocks(offset_out, f, a, [part - m for part, m in zip(parts, mine)])


def powers_kernel(inner, order, dec, matrix, total_out, near_out, far_out, held, decoded_held):
    lat = matrix.shape[0]
    inside = lax.axis_index("cuts") % inner
    coarse = matrix[...]
    powers = [identity(lat), coarse]
    for k in range(2, inner + 1):
        powers.append(dot_full(powers[k // 2], powers[k - k // 2]))
    for k, power in enumerate(powers):
        held[k] = power
    weight = reordered(dec[...]).T
    decoded = [weight]
    for d in range(1, inner):
        place = inside ^ d
        part = dot_full(weight, held[jnp.maximum(inside - place, 0)])
        decoded.append(jnp.where(place < inside, part, 0.0))
    near_out[...] = jnp.concatenate(decoded, axis=1)
    total_out[...] = jnp.concatenate([held[inner - 1 - (inside ^ d)] for d in range(inner)], axis=1)
    group = lax.axis_index("cuts") // inner
    far = [dot_full(weight, held[inside + 1])]
    for k in range(2, len(order) + 1):
        far.append(dot_full(far[-1], powers[inner]))
    for k, part in enumerate(far):
        decoded_held[k] = part
    picked = [decoded_held[jnp.maximum(group - 1 - (group ^ d), 0)] for d in order]
    far_out[...] = jnp.concatenate(picked, axis=1)


class Padded:
    def __init__(self, ref, reps):
        self.ref = ref
        self.reps = reps

    def put_cell(self, r, q, *cells):
        ref, reps = self.ref, self.reps
        for field, value in enumerate(cells):
            ref[field, r + 2, q + 2] = value
            if r < 2:
                ref[field, r + reps + 2, q + 2] = pltpu.roll(value, 7, 0)
            if r >= reps - 2:
                ref[field, r - reps + 2, q + 2] = pltpu.roll(value, 1, 0)
            if q < 2:
                ref[field, r + 2, q + 10] = pltpu.roll(value, LANES - 1, 1)
            if q >= 6:
                ref[field, r + 2, q - 6] = pltpu.roll(value, 1, 1)

    def cell(self, field, r, q):
        return self.ref[field, r + 2, q + 2]


def slope(before_2, before, after, after_2):
    return 8.0 * (after - before) - (after_2 - before_2)


def stage(base, now, reps, alpha, beta, gamma, put):
    scale = gamma / 12.0
    turn = 12.0 * FCOR

    def column(r, q):
        height, along_c, along_r = (now.cell(f, r, q) for f in range(3))
        return height, along_c, along_r, along_c + height * along_c

    for r in range(reps):
        window = [column(r, q) for q in range(-2, 2)]
        for q in range(8):
            window.append(column(r, q + 2))
            height, along_c, along_r, _ = window[2]
            cols = [slope(*(window[k][f] for k in (0, 1, 3, 4))) for f in range(4)]
            near = [[now.cell(f, r + k, q) for f in range(3)] for k in (-2, -1, 1, 2)]
            for cells in near:
                cells.append(cells[2] + cells[0] * cells[2])
            rows = [slope(*(cells[f] for cells in near)) for f in range(4)]
            d_height = cols[3] + rows[3]
            d_colvel = along_c * cols[1] + along_r * (rows[1] - turn) + cols[0]
            d_rowvel = along_c * (cols[2] + turn) + along_r * rows[2] + rows[0]
            new = []
            for f, (mine, d) in enumerate(((height, d_height), (along_c, d_colvel), (along_r, d_rowvel))):
                total = beta * mine if beta != 1.0 else mine
                if alpha:
                    total = total + alpha * base.cell(f, r, q)
                new.append(total - scale * d)
            put(r, q, *new)
            del window[0]


def fine_kernel(own, other, offset, enc, coarse, finals_out, g_out, t_out, rows_buf, buf_a, buf_b, buf_c):
    local_rows = own.shape[2]
    ext = local_rows + other.shape[1]
    reps = ext // 8
    groups = local_rows // DOWN
    for f in range(3):
        for q in range(8):
            rows_buf[f, q, 0:local_rows, :] = own[f, q, :, :]
        for tile in range(other.shape[1] // 8):
            parts = split_columns(chunks_of(other, f, 8 * tile))
            for q in range(8):
                rows_buf[f, q, local_rows + 8 * tile : local_rows + 8 * tile + 8, :] = parts[q]
    t_part = dot3(coarse[...], dot3(enc[...], side_by_side(offset)))
    t_out[...] = t_part
    state, second, third = Padded(buf_a, reps), Padded(buf_b, reps), Padded(buf_c, reps)
    for r in range(reps):
        for q in range(8):
            state.put_cell(r, q, *(rows_buf[f, q, pl.ds(r, 8, stride=reps), :] for f in range(3)))

    def finish(r, q, *cells):
        for f in range(3):
            rows_buf[f, q, pl.ds(r, 8, stride=reps), :] = cells[f]

    for step in range(FINE_STEPS):
        stage(None, state, reps, 0.0, 1.0, TSTEP, second.put_cell)
        stage(state, second, reps, 0.75, 0.25, 0.25 * TSTEP, third.put_cell)
        last = step + 1 == FINE_STEPS
        stage(state, third, reps, 1.0 / 3.0, 2.0 / 3.0, 2.0 / 3.0 * TSTEP, finish if last else state.put_cell)
    for f in range(3):
        for a in range(groups):
            put_blocks(finals_out, f, a, [rows_buf[f, q, 8 * a : 8 * a + 8, :] for q in range(8)])
    g_out[...] = dot3(enc[...], side_by_side(finals_out)) + t_part


def weighted_kernel(*refs):
    *parts, weights, out = refs
    out[...] = dot3(weights[...], jnp.concatenate([part[...] for part in parts], axis=0))


def base_kernel(finals, *refs):
    *parts, weights, out_hbm, out, sems = refs
    change = dot3(weights[...], jnp.concatenate([part[...] for part in parts], axis=0))
    copies = []
    for a in range(finals.shape[0]):
        rows = pl.ds(8 * a, 8)
        for f in range(3):
            places = [slice(64 * f + 8 * q, 64 * f + 8 * q + 8) for q in range(8)]
            joined = join_columns([finals[a, k, :] + change[k, LANES * a : LANES * (a + 1)] for k in places])
            for j, chunk in enumerate(joined):
                out[f, 8 * a : 8 * a + 8, LANES * j : LANES * (j + 1)] = chunk
            copies.append(pltpu.make_async_copy(out.at[f, rows], out_hbm.at[0, f, rows], sems.at[3 * a + f]))
            copies[-1].start()
    for copy in copies:
        copy.wait()


def output_kernel(inner, order, base, *refs):
    *totals, weights, _, out_hbm, joined_out, sems = refs
    group = lax.axis_index("cuts") // inner

    @pl.when(group > 0)
    def _():
        taken = [jnp.where((group ^ d) < group, part[...], 0.0) for d, part in zip(order, totals)]
        change = dot3(weights[...], jnp.concatenate(taken, axis=0))
        copies = []
        for a in range(base.shape[1] // DOWN):
            rows = pl.ds(8 * a, 8)
            for f in range(3):
                places = [slice(64 * f + 8 * q, 64 * f + 8 * q + 8) for q in range(8)]
                joined = join_columns([change[k, LANES * a : LANES * (a + 1)] for k in places])
                for j, chunk in enumerate(joined):
                    cells = (f, slice(8 * a, 8 * a + 8), slice(LANES * j, LANES * (j + 1)))
                    joined_out[cells] = base[cells] + chunk
                copies.append(pltpu.make_async_copy(joined_out.at[f, rows], out_hbm.at[0, f, rows], sems.at[3 * a + f]))
                copies[-1].start()
        for copy in copies:
            copy.wait()


def call(kernel, shapes, inputs, scratch=(), flops=0, inside=None, outside=None, aliases={}):
    return pl.pallas_call(
        kernel,
        out_shape=[jax.ShapeDtypeStruct(s, F32) for s in shapes],
        in_specs=inside or [VMEM] * len(inputs),
        out_specs=outside or [VMEM] * len(shapes),
        scratch_shapes=list(scratch),
        input_output_aliases=aliases,
        compiler_params=pltpu.CompilerParams(vmem_limit_bytes=40 * 1024 * 1024),
        cost_estimate=pl.CostEstimate(
            flops=flops, bytes_accessed=sum(4 * x.size for x in inputs), transcendentals=0
        ),
    )(*inputs)


def neighbour_rows(state):
    count = lax.axis_size("row")
    rows = state.shape[1]
    if count == 1:
        return jnp.concatenate([state[:, :HALO], state[:, rows - HALO :]], axis=1)
    forward = [(i, (i + 1) % count) for i in range(count)]
    backward = [((i + 1) % count, i) for i in range(count)]
    if count == 2 and rows <= 2 * HALO:
        return lax.ppermute(state, "row", forward)
    below = lax.ppermute(state[:, :HALO], "row", backward)
    above = lax.ppermute(state[:, rows - HALO :], "row", forward)
    return jnp.concatenate([below, above], axis=1)


def swapped(value, distance):
    return lax.ppermute(value, "cuts", [(i, i ^ distance) for i in range(lax.axis_size("cuts"))])


def local(starts, initial, encode_weight, decode_weight, latent_rate, coupling):
    lat = coupling.shape[0]
    state = starts[0]
    rows = state.shape[1]
    groups = rows // DOWN
    wide = groups * LANES
    size = encode_weight.shape[1]
    slices = lax.axis_size("cuts")
    inner = 1 << (slices.bit_length() // 2)
    outer = slices // inner
    order = (1, *range(outer - 1, 1, -1))
    rate = latent_rate.reshape(1, lat)
    other = neighbour_rows(state)
    given = (state, initial, encode_weight, rate, coupling)
    own, offset, enc, coarse = call(
        split_kernel,
        [(3, 8, rows, LANES), (groups, size, LANES), encode_weight.shape, (lat, lat)],
        [pltpu.with_memory_space_constraint(x, pltpu.HBM) for x in given],
        [pltpu.VMEM(x.shape, F32) for x in given] + [pltpu.SemaphoreType.DMA((7,))],
        flops=100_000_000,
        inside=[pl.BlockSpec(memory_space=pl.ANY)] * len(given),
    )
    reps = (rows + other.shape[1]) // 8
    pad = pltpu.VMEM((3, reps + 4, 12, 8, LANES), F32)
    finals, g_part, t_part = call(
        fine_kernel,
        [(groups, size, LANES), (lat, wide), (lat, wide)],
        [own, other, offset, enc, coarse],
        [pltpu.VMEM((3, 8, 8 * reps, LANES), F32), pad, pad, pad],
        flops=400_000_000,
    )
    parts = [swapped(g_part, d) for d in range(1, inner)]
    to_total, to_near, to_far = call(
        functools.partial(powers_kernel, inner, order),
        [(lat, inner * lat), (size, inner * lat), (size, (outer - 1) * lat)],
        [decode_weight.T, coarse],
        [pltpu.VMEM((inner + 1, lat, lat), F32), pltpu.VMEM((outer - 1, size, lat), F32)],
        flops=50_000_000,
    )
    (total,) = call(weighted_kernel, [(lat, wide)], [g_part, *parts, to_total], flops=50_000_000)
    totals = [swapped(total, inner * d) for d in order]
    hbm = pl.BlockSpec(memory_space=pltpu.HBM)
    tiles = pltpu.SemaphoreType.DMA((3 * groups,))
    result = (1, *state.shape)
    near_result, base = call(
        base_kernel,
        [result, state.shape],
        [finals, t_part, *parts, to_near],
        [tiles],
        flops=50_000_000,
        outside=[hbm, VMEM],
    )
    (out,) = call(
        functools.partial(output_kernel, inner, order),
        [result],
        [base, *totals, to_far, near_result],
        [pltpu.VMEM(state.shape, F32), tiles],
        flops=50_000_000,
        inside=[VMEM] * (outer + 1) + [hbm],
        outside=[hbm],
        aliases={outer + 1: 0},
    )
    return out


def solution(mesh):
    return jax.shard_map(
        local,
        mesh=mesh,
        in_specs=(P("cuts", None, "row", None), P(None, "row", None), P(), P(), P(), P()),
        out_specs=P("cuts", None, "row", None),
        check_vma=False,
    )
```

```python
import functools

import jax
import jax.numpy as jnp
from jax import lax
from jax.experimental import pallas as pl
from jax.experimental.pallas import tpu as pltpu
from jax.sharding import PartitionSpec as P

DOWN = 8
FINE_STEPS = 2
FCOR = 0.3
TSTEP = 0.25
HALO = 6 * FINE_STEPS
LANES = 128
F32 = jnp.float32
BF16 = jnp.bfloat16
VMEM = pl.BlockSpec(memory_space=pltpu.VMEM)


def halves(value):
    high = value.astype(BF16)
    return high, (value - high.astype(F32)).astype(BF16)


def dot3(left, right, contract=((1,), (0,))):
    dims = (contract, ((), ()))
    lh, ll = halves(left)
    rh, rl = halves(right)
    one = functools.partial(lax.dot_general, dimension_numbers=dims, preferred_element_type=F32)
    return one(lh, rh) + (one(lh, rl) + one(ll, rh))


def dot_full(left, right):
    return jnp.dot(left, right, precision=lax.Precision.HIGHEST, preferred_element_type=F32)


def lanes_iota():
    return lax.broadcasted_iota(jnp.int32, (8, LANES), 1)


def split_columns(chunks):
    lane = lanes_iota()
    moved = [c if j == 0 else pltpu.roll(c, j, 1) for j, c in enumerate(chunks)]
    phase = lane & 7
    out = []
    for q in range(8):
        merged = moved[0]
        for j in range(1, 8):
            merged = jnp.where(phase == (q + j) % 8, moved[j], merged)
        place = (8 * (lane & 15) + q + (lane >> 4)) & (LANES - 1)
        out.append(jnp.take_along_axis(merged, place, axis=1))
    return out


def join_columns(parts):
    lane = lanes_iota()
    phase = lane & 7
    picked = []
    for q, part in enumerate(parts):
        j = (lane - q) & 7
        place = 16 * j + (((lane - q - j) & (LANES - 1)) >> 3)
        picked.append(jnp.take_along_axis(part, place, axis=1))
    out = []
    for j in range(8):
        merged = picked[(-j) % 8]
        for q in range(8):
            if q != (-j) % 8:
                merged = jnp.where(phase == (q + j) % 8, picked[q], merged)
        out.append(merged if j == 0 else pltpu.roll(merged, LANES - j, 1))
    return out


def chunks_of(ref, field, row):
    return [ref[field, row : row + 8, LANES * j : LANES * (j + 1)] for j in range(8)]


def identity(size):
    rows = lax.broadcasted_iota(jnp.int32, (size, size), 0)
    return (rows == lax.broadcasted_iota(jnp.int32, (size, size), 1)).astype(F32)


def coarse_matrix(rate, coupling):
    return (rate * (identity(coupling.shape[0]) + coupling.T - coupling)).T


def put_blocks(ref, field, group, parts):
    for q, part in enumerate(parts):
        ref[group, 64 * field + 8 * q : 64 * field + 8 * q + 8, :] = part


def reordered(weight):
    size = weight.shape[1]
    source = lax.broadcasted_iota(jnp.int32, (size, size), 0)
    target = lax.broadcasted_iota(jnp.int32, (size, size), 1)
    wanted = (target & ~63) | ((target & 7) << 3) | ((target >> 3) & 7)
    return dot_full(weight, (source == wanted).astype(F32))


def side_by_side(ref):
    return jnp.concatenate([ref[a] for a in range(ref.shape[0])], axis=1)


def split_kernel(starts_hbm, initial_hbm, enc_hbm, rate_hbm, coup_hbm, *refs):
    own_out, offset_out, enc_out, coarse_out, starts, initial, enc, rate, coup, sems = refs
    count = starts.shape[0]
    pieces = [(enc_hbm, enc), (rate_hbm, rate), (coup_hbm, coup)] + [(starts_hbm.at[f], starts.at[f]) for f in range(count)]
    copies = [pltpu.make_async_copy(src, dst, sems.at[i]) for i, (src, dst) in enumerate(pieces)]
    for copy in copies[3:] + copies[:3]:
        copy.start()
    first = lax.axis_index("cuts") == 0
    given = pltpu.make_async_copy(initial_hbm, initial, sems.at[len(copies)])

    @pl.when(first)
    def _():
        given.start()

    for copy in copies:
        copy.wait()
    enc_out[...] = reordered(enc[...])
    coarse_out[...] = coarse_matrix(rate[...], coup[...])
    for f in range(count):
        for a in range(starts.shape[1] // DOWN):
            parts = split_columns(chunks_of(starts, f, 8 * a))
            for q, part in enumerate(parts):
                own_out[f, q, 8 * a : 8 * a + 8, :] = part
            put_blocks(offset_out, f, a, [-part for part in parts])

    @pl.when(first)
    def _():
        given.wait()
        for f in range(count):
            for a in range(starts.shape[1] // DOWN):
                parts = split_columns(chunks_of(initial, f, 8 * a))
                mine = [own_out[f, q, 8 * a : 8 * a + 8, :] for q in range(8)]
                put_blocks(offset_out, f, a, [part - m for part, m in zip(parts, mine)])


def powers_kernel(inner, order, dec, matrix, total_out, near_out, far_out, held, decoded_held):
    lat = matrix.shape[0]
    inside = lax.axis_index("cuts") % inner
    coarse = matrix[...]
    powers = [identity(lat), coarse]
    for k in range(2, inner + 1):
        powers.append(dot_full(powers[k // 2], powers[k - k // 2]))
    for k, power in enumerate(powers):
        held[k] = power
    weight = reordered(dec[...]).T
    decoded = [weight]
    for d in range(1, inner):
        place = inside ^ d
        part = dot_full(weight, held[jnp.maximum(inside - place, 0)])
        decoded.append(jnp.where(place < inside, part, 0.0))
    near_out[...] = jnp.concatenate(decoded, axis=1)
    total_out[...] = jnp.concatenate([held[inner - 1 - (inside ^ d)] for d in range(inner)], axis=1)
    group = lax.axis_index("cuts") // inner
    far = [dot_full(weight, held[inside + 1])]
    for k in range(2, len(order) + 1):
        far.append(dot_full(far[-1], powers[inner]))
    for k, part in enumerate(far):
        decoded_held[k] = part
    picked = [decoded_held[jnp.maximum(group - 1 - (group ^ d), 0)] for d in order]
    far_out[...] = jnp.concatenate(picked, axis=1)


class Padded:
    def __init__(self, ref, reps):
        self.ref = ref
        self.reps = reps

    def put_cell(self, r, q, *cells):
        ref, reps = self.ref, self.reps
        for field, value in enumerate(cells):
            ref[field, r + 2, q + 2] = value
            if r < 2:
                ref[field, r + reps + 2, q + 2] = pltpu.roll(value, 7, 0)
            if r >= reps - 2:
                ref[field, r - reps + 2, q + 2] = pltpu.roll(value, 1, 0)
            if q < 2:
                ref[field, r + 2, q + 10] = pltpu.roll(value, LANES - 1, 1)
            if q >= 6:
                ref[field, r + 2, q - 6] = pltpu.roll(value, 1, 1)

    def cell(self, field, r, q):
        return self.ref[field, r + 2, q + 2]


def slope(before_2, before, after, after_2):
    return 8.0 * (after - before) - (after_2 - before_2)


def stage(base, now, reps, alpha, beta, gamma, put):
    scale = gamma / 12.0
    turn = 12.0 * FCOR

    def column(r, q):
        height, along_c, along_r = (now.cell(f, r, q) for f in range(3))
        return height, along_c, along_r, along_c + height * along_c

    for r in range(reps):
        window = [column(r, q) for q in range(-2, 2)]
        for q in range(8):
            window.append(column(r, q + 2))
            height, along_c, along_r, _ = window[2]
            cols = [slope(*(window[k][f] for k in (0, 1, 3, 4))) for f in range(4)]
            near = [[now.cell(f, r + k, q) for f in range(3)] for k in (-2, -1, 1, 2)]
            for cells in near:
                cells.append(cells[2] + cells[0] * cells[2])
            rows = [slope(*(cells[f] for cells in near)) for f in range(4)]
            d_height = cols[3] + rows[3]
            d_colvel = along_c * cols[1] + along_r * (rows[1] - turn) + cols[0]
            d_rowvel = along_c * (cols[2] + turn) + along_r * rows[2] + rows[0]
            new = []
            for f, (mine, d) in enumerate(((height, d_height), (along_c, d_colvel), (along_r, d_rowvel))):
                total = beta * mine if beta != 1.0 else mine
                if alpha:
                    total = total + alpha * base.cell(f, r, q)
                new.append(total - scale * d)
            put(r, q, *new)
            del window[0]


def fine_solve(own, other, finals, rows_buf, buf_a, buf_b, buf_c):
    local_rows = own.shape[2]
    ext = local_rows + other.shape[1]
    reps = ext // 8
    for f in range(3):
        for q in range(8):
            rows_buf[f, q, 0:local_rows, :] = own[f, q, :, :]
        for tile in range(other.shape[1] // 8):
            parts = split_columns(chunks_of(other, f, 8 * tile))
            for q in range(8):
                rows_buf[f, q, local_rows + 8 * tile : local_rows + 8 * tile + 8, :] = parts[q]
    state, second, third = Padded(buf_a, reps), Padded(buf_b, reps), Padded(buf_c, reps)
    for r in range(reps):
        for q in range(8):
            state.put_cell(r, q, *(rows_buf[f, q, pl.ds(r, 8, stride=reps), :] for f in range(3)))

    def finish(r, q, *cells):
        for f in range(3):
            rows_buf[f, q, pl.ds(r, 8, stride=reps), :] = cells[f]

    for step in range(FINE_STEPS):
        stage(None, state, reps, 0.0, 1.0, TSTEP, second.put_cell)
        stage(state, second, reps, 0.75, 0.25, 0.25 * TSTEP, third.put_cell)
        last = step + 1 == FINE_STEPS
        stage(state, third, reps, 1.0 / 3.0, 2.0 / 3.0, 2.0 / 3.0 * TSTEP, finish if last else state.put_cell)
    for f in range(3):
        for a in range(local_rows // DOWN):
            put_blocks(finals, f, a, [rows_buf[f, q, 8 * a : 8 * a + 8, :] for q in range(8)])


def last_slice():
    return lax.axis_index("cuts") == lax.axis_size("cuts") - 1


def fine_kernel(own, other, offset, enc, coarse, finals_out, g_out, t_out, *buffers):
    last = last_slice()

    @pl.when(jnp.logical_not(last))
    def _():
        t_part = dot3(coarse[...], dot3(enc[...], side_by_side(offset)))
        t_out[...] = t_part
        fine_solve(own, other, finals_out, *buffers)
        g_out[...] = dot3(enc[...], side_by_side(finals_out)) + t_part

    @pl.when(last)
    def _():
        t_part = dot3(coarse[...], dot3(enc[...], side_by_side(offset)))
        t_out[...] = t_part
        g_out[...] = t_part


def weighted_kernel(*refs):
    *parts, weights, out = refs
    out[...] = dot3(weights[...], jnp.concatenate([part[...] for part in parts], axis=0))


def base_kernel(own, other, given, *refs):
    *parts, weights, out_hbm, out, finals, sems, rows_buf, buf_a, buf_b, buf_c = refs
    last = last_slice()

    @pl.when(last)
    def _():
        fine_solve(own, other, finals, rows_buf, buf_a, buf_b, buf_c)

    @pl.when(jnp.logical_not(last))
    def _():
        finals[...] = given[...]

    change = dot3(weights[...], jnp.concatenate([part[...] for part in parts], axis=0))
    copies = []
    for a in range(finals.shape[0]):
        rows = pl.ds(8 * a, 8)
        for f in range(3):
            places = [slice(64 * f + 8 * q, 64 * f + 8 * q + 8) for q in range(8)]
            joined = join_columns([finals[a, k, :] + change[k, LANES * a : LANES * (a + 1)] for k in places])
            for j, chunk in enumerate(joined):
                out[f, 8 * a : 8 * a + 8, LANES * j : LANES * (j + 1)] = chunk
            copies.append(pltpu.make_async_copy(out.at[f, rows], out_hbm.at[0, f, rows], sems.at[3 * a + f]))
            copies[-1].start()
    for copy in copies:
        copy.wait()


def output_kernel(inner, order, base, *refs):
    *totals, weights, _, out_hbm, joined_out, sems = refs
    group = lax.axis_index("cuts") // inner

    @pl.when(group > 0)
    def _():
        taken = [jnp.where((group ^ d) < group, part[...], 0.0) for d, part in zip(order, totals)]
        change = dot3(weights[...], jnp.concatenate(taken, axis=0))
        copies = []
        for a in range(base.shape[1] // DOWN):
            rows = pl.ds(8 * a, 8)
            for f in range(3):
                places = [slice(64 * f + 8 * q, 64 * f + 8 * q + 8) for q in range(8)]
                joined = join_columns([change[k, LANES * a : LANES * (a + 1)] for k in places])
                for j, chunk in enumerate(joined):
                    cells = (f, slice(8 * a, 8 * a + 8), slice(LANES * j, LANES * (j + 1)))
                    joined_out[cells] = base[cells] + chunk
                copies.append(pltpu.make_async_copy(joined_out.at[f, rows], out_hbm.at[0, f, rows], sems.at[3 * a + f]))
                copies[-1].start()
        for copy in copies:
            copy.wait()


def call(kernel, shapes, inputs, scratch=(), flops=0, inside=None, outside=None, aliases={}):
    return pl.pallas_call(
        kernel,
        out_shape=[jax.ShapeDtypeStruct(s, F32) for s in shapes],
        in_specs=inside or [VMEM] * len(inputs),
        out_specs=outside or [VMEM] * len(shapes),
        scratch_shapes=list(scratch),
        input_output_aliases=aliases,
        compiler_params=pltpu.CompilerParams(vmem_limit_bytes=40 * 1024 * 1024),
        cost_estimate=pl.CostEstimate(
            flops=flops, bytes_accessed=sum(4 * x.size for x in inputs), transcendentals=0
        ),
    )(*inputs)


def neighbour_rows(state):
    count = lax.axis_size("row")
    rows = state.shape[1]
    if count == 1:
        return jnp.concatenate([state[:, :HALO], state[:, rows - HALO :]], axis=1)
    forward = [(i, (i + 1) % count) for i in range(count)]
    backward = [((i + 1) % count, i) for i in range(count)]
    if count == 2 and rows <= 2 * HALO:
        return lax.ppermute(state, "row", forward)
    below = lax.ppermute(state[:, :HALO], "row", backward)
    above = lax.ppermute(state[:, rows - HALO :], "row", forward)
    return jnp.concatenate([below, above], axis=1)


def swapped(value, distance):
    return lax.ppermute(value, "cuts", [(i, i ^ distance) for i in range(lax.axis_size("cuts"))])


def local(starts, initial, encode_weight, decode_weight, latent_rate, coupling):
    lat = coupling.shape[0]
    state = starts[0]
    rows = state.shape[1]
    groups = rows // DOWN
    wide = groups * LANES
    size = encode_weight.shape[1]
    slices = lax.axis_size("cuts")
    inner = 1 << (slices.bit_length() // 2)
    outer = slices // inner
    order = (1, *range(outer - 1, 1, -1))
    rate = latent_rate.reshape(1, lat)
    other = neighbour_rows(state)
    given = (state, initial, encode_weight, rate, coupling)
    own, offset, enc, coarse = call(
        split_kernel,
        [(3, 8, rows, LANES), (groups, size, LANES), encode_weight.shape, (lat, lat)],
        [pltpu.with_memory_space_constraint(x, pltpu.HBM) for x in given],
        [pltpu.VMEM(x.shape, F32) for x in given] + [pltpu.SemaphoreType.DMA((7,))],
        flops=100_000_000,
        inside=[pl.BlockSpec(memory_space=pl.ANY)] * len(given),
    )
    reps = (rows + other.shape[1]) // 8
    pad = pltpu.VMEM((3, reps + 4, 12, 8, LANES), F32)
    buffers = [pltpu.VMEM((3, 8, 8 * reps, LANES), F32), pad, pad, pad]
    finals, g_part, t_part = call(
        fine_kernel,
        [(groups, size, LANES), (lat, wide), (lat, wide)],
        [own, other, offset, enc, coarse],
        buffers,
        flops=400_000_000,
    )
    parts = [swapped(g_part, d) for d in range(1, inner)]
    to_total, to_near, to_far = call(
        functools.partial(powers_kernel, inner, order),
        [(lat, inner * lat), (size, inner * lat), (size, (outer - 1) * lat)],
        [decode_weight.T, coarse],
        [pltpu.VMEM((inner + 1, lat, lat), F32), pltpu.VMEM((outer - 1, size, lat), F32)],
        flops=50_000_000,
    )
    (total,) = call(weighted_kernel, [(lat, wide)], [g_part, *parts, to_total], flops=50_000_000)
    totals = [swapped(total, inner * d) for d in order]
    hbm = pl.BlockSpec(memory_space=pltpu.HBM)
    tiles = pltpu.SemaphoreType.DMA((3 * groups,))
    result = (1, *state.shape)
    near_result, base = call(
        base_kernel,
        [result, state.shape],
        [own, other, finals, t_part, *parts, to_near],
        [pltpu.VMEM((groups, size, LANES), F32), tiles, *buffers],
        flops=50_000_000,
        outside=[hbm, VMEM],
    )
    (out,) = call(
        functools.partial(output_kernel, inner, order),
        [result],
        [base, *totals, to_far, near_result],
        [pltpu.VMEM(state.shape, F32), tiles],
        flops=50_000_000,
        inside=[VMEM] * (outer + 1) + [hbm],
        outside=[hbm],
        aliases={outer + 1: 0},
    )
    return out


def solution(mesh):
    return jax.shard_map(
        local,
        mesh=mesh,
        in_specs=(P("cuts", None, "row", None), P(None, "row", None), P(), P(), P(), P()),
        out_specs=P("cuts", None, "row", None),
        check_vma=False,
    )
```

```python
import functools

import jax
import jax.numpy as jnp
from jax import lax
from jax.experimental import pallas as pl
from jax.experimental.pallas import tpu as pltpu
from jax.sharding import PartitionSpec as P

DOWN = 8
FINE_STEPS = 2
FCOR = 0.3
TSTEP = 0.25
HALO = 6 * FINE_STEPS
LANES = 128
F32 = jnp.float32
BF16 = jnp.bfloat16
VMEM = pl.BlockSpec(memory_space=pltpu.VMEM)


def halves(value):
    high = value.astype(BF16)
    return high, (value - high.astype(F32)).astype(BF16)


def dot3(left, right, contract=((1,), (0,))):
    dims = (contract, ((), ()))
    lh, ll = halves(left)
    rh, rl = halves(right)
    one = functools.partial(lax.dot_general, dimension_numbers=dims, preferred_element_type=F32)
    return one(lh, rh) + (one(lh, rl) + one(ll, rh))


def dot_full(left, right):
    return jnp.dot(left, right, precision=lax.Precision.HIGHEST, preferred_element_type=F32)


def lanes_iota():
    return lax.broadcasted_iota(jnp.int32, (8, LANES), 1)


def split_columns(chunks):
    lane = lanes_iota()
    moved = [c if j == 0 else pltpu.roll(c, j, 1) for j, c in enumerate(chunks)]
    phase = lane & 7
    out = []
    for q in range(8):
        merged = moved[0]
        for j in range(1, 8):
            merged = jnp.where(phase == (q + j) % 8, moved[j], merged)
        place = (8 * (lane & 15) + q + (lane >> 4)) & (LANES - 1)
        out.append(jnp.take_along_axis(merged, place, axis=1))
    return out


def join_columns(parts):
    lane = lanes_iota()
    phase = lane & 7
    picked = []
    for q, part in enumerate(parts):
        j = (lane - q) & 7
        place = 16 * j + (((lane - q - j) & (LANES - 1)) >> 3)
        picked.append(jnp.take_along_axis(part, place, axis=1))
    out = []
    for j in range(8):
        merged = picked[(-j) % 8]
        for q in range(8):
            if q != (-j) % 8:
                merged = jnp.where(phase == (q + j) % 8, picked[q], merged)
        out.append(merged if j == 0 else pltpu.roll(merged, LANES - j, 1))
    return out


def chunks_of(ref, field, row):
    return [ref[field, row : row + 8, LANES * j : LANES * (j + 1)] for j in range(8)]


def identity(size):
    rows = lax.broadcasted_iota(jnp.int32, (size, size), 0)
    return (rows == lax.broadcasted_iota(jnp.int32, (size, size), 1)).astype(F32)


def coarse_matrix(rate, coupling):
    return (rate * (identity(coupling.shape[0]) + coupling.T - coupling)).T


def put_blocks(ref, field, group, parts):
    for q, part in enumerate(parts):
        ref[group, 64 * field + 8 * q : 64 * field + 8 * q + 8, :] = part


def reordered(weight):
    size = weight.shape[1]
    source = lax.broadcasted_iota(jnp.int32, (size, size), 0)
    target = lax.broadcasted_iota(jnp.int32, (size, size), 1)
    wanted = (target & ~63) | ((target & 7) << 3) | ((target >> 3) & 7)
    return dot_full(weight, (source == wanted).astype(F32))


def side_by_side(ref):
    return jnp.concatenate([ref[a] for a in range(ref.shape[0])], axis=1)


def split_kernel(starts_hbm, initial_hbm, enc_hbm, rate_hbm, coup_hbm, *refs):
    own_out, offset_out, enc_out, coarse_out, starts, initial, enc, rate, coup, sems = refs
    count = starts.shape[0]
    pieces = [(enc_hbm, enc), (rate_hbm, rate), (coup_hbm, coup)] + [(starts_hbm.at[f], starts.at[f]) for f in range(count)]
    copies = [pltpu.make_async_copy(src, dst, sems.at[i]) for i, (src, dst) in enumerate(pieces)]
    for copy in copies[3:] + copies[:3]:
        copy.start()
    first = lax.axis_index("cuts") == 0
    given = pltpu.make_async_copy(initial_hbm, initial, sems.at[len(copies)])

    @pl.when(first)
    def _():
        given.start()

    for copy in copies:
        copy.wait()
    enc_out[...] = reordered(enc[...])
    coarse_out[...] = coarse_matrix(rate[...], coup[...])
    for f in range(count):
        for a in range(starts.shape[1] // DOWN):
            parts = split_columns(chunks_of(starts, f, 8 * a))
            for q, part in enumerate(parts):
                own_out[f, q, 8 * a : 8 * a + 8, :] = part
            put_blocks(offset_out, f, a, [-part for part in parts])

    @pl.when(first)
    def _():
        given.wait()
        for f in range(count):
            for a in range(starts.shape[1] // DOWN):
                parts = split_columns(chunks_of(initial, f, 8 * a))
                mine = [own_out[f, q, 8 * a : 8 * a + 8, :] for q in range(8)]
                put_blocks(offset_out, f, a, [part - m for part, m in zip(parts, mine)])


def powers_kernel(inner, near_order, far_order, dec, matrix, total_out, near_out, far_out, held, decoded_held):
    lat = matrix.shape[0]
    inside = lax.axis_index("cuts") % inner
    coarse = matrix[...]
    powers = [identity(lat), coarse]
    for k in range(2, inner + 1):
        powers.append(dot_full(powers[k // 2], powers[k - k // 2]))
    for k, power in enumerate(powers):
        held[k] = power
    weight = reordered(dec[...]).T
    decoded = [weight]
    for d in near_order:
        place = inside ^ d
        part = dot_full(weight, held[jnp.maximum(inside - place, 0)])
        decoded.append(jnp.where(place < inside, part, 0.0))
    near_out[...] = jnp.concatenate(decoded, axis=1)
    total_out[...] = jnp.concatenate([held[inner - 1 - (inside ^ d)] for d in (0, *near_order)], axis=1)
    group = lax.axis_index("cuts") // inner
    far = [dot_full(weight, held[inside + 1])]
    for k in range(2, len(far_order) + 1):
        far.append(dot_full(far[-1], powers[inner]))
    for k, part in enumerate(far):
        decoded_held[k] = part
    picked = [decoded_held[jnp.maximum(group - 1 - (group ^ d), 0)] for d in far_order]
    far_out[...] = jnp.concatenate(picked, axis=1)


class Padded:
    def __init__(self, ref, reps):
        self.ref = ref
        self.reps = reps

    def put_cell(self, r, q, *cells):
        ref, reps = self.ref, self.reps
        for field, value in enumerate(cells):
            ref[field, r + 2, q + 2] = value
            if r < 2:
                ref[field, r + reps + 2, q + 2] = pltpu.roll(value, 7, 0)
            if r >= reps - 2:
                ref[field, r - reps + 2, q + 2] = pltpu.roll(value, 1, 0)
            if q < 2:
                ref[field, r + 2, q + 10] = pltpu.roll(value, LANES - 1, 1)
            if q >= 6:
                ref[field, r + 2, q - 6] = pltpu.roll(value, 1, 1)

    def cell(self, field, r, q):
        return self.ref[field, r + 2, q + 2]


def slope(before_2, before, after, after_2):
    return 8.0 * (after - before) - (after_2 - before_2)


def stage(base, now, reps, alpha, beta, gamma, put):
    scale = gamma / 12.0
    turn = 12.0 * FCOR

    def column(r, q):
        height, along_c, along_r = (now.cell(f, r, q) for f in range(3))
        return height, along_c, along_r, along_c + height * along_c

    for r in range(reps):
        window = [column(r, q) for q in range(-2, 2)]
        for q in range(8):
            window.append(column(r, q + 2))
            height, along_c, along_r, _ = window[2]
            cols = [slope(*(window[k][f] for k in (0, 1, 3, 4))) for f in range(4)]
            near = [[now.cell(f, r + k, q) for f in range(3)] for k in (-2, -1, 1, 2)]
            for cells in near:
                cells.append(cells[2] + cells[0] * cells[2])
            rows = [slope(*(cells[f] for cells in near)) for f in range(4)]
            d_height = cols[3] + rows[3]
            d_colvel = along_c * cols[1] + along_r * (rows[1] - turn) + cols[0]
            d_rowvel = along_c * (cols[2] + turn) + along_r * rows[2] + rows[0]
            new = []
            for f, (mine, d) in enumerate(((height, d_height), (along_c, d_colvel), (along_r, d_rowvel))):
                total = beta * mine if beta != 1.0 else mine
                if alpha:
                    total = total + alpha * base.cell(f, r, q)
                new.append(total - scale * d)
            put(r, q, *new)
            del window[0]


def fine_kernel(own, other, offset, enc, coarse, finals_out, g_out, t_out, rows_buf, buf_a, buf_b, buf_c):
    local_rows = own.shape[2]
    ext = local_rows + other.shape[1]
    reps = ext // 8
    groups = local_rows // DOWN
    for f in range(3):
        for q in range(8):
            rows_buf[f, q, 0:local_rows, :] = own[f, q, :, :]
        for tile in range(other.shape[1] // 8):
            parts = split_columns(chunks_of(other, f, 8 * tile))
            for q in range(8):
                rows_buf[f, q, local_rows + 8 * tile : local_rows + 8 * tile + 8, :] = parts[q]
    t_part = dot3(coarse[...], dot3(enc[...], side_by_side(offset)))
    t_out[...] = t_part
    state, second, third = Padded(buf_a, reps), Padded(buf_b, reps), Padded(buf_c, reps)
    for r in range(reps):
        for q in range(8):
            state.put_cell(r, q, *(rows_buf[f, q, pl.ds(r, 8, stride=reps), :] for f in range(3)))

    def finish(r, q, *cells):
        for f in range(3):
            rows_buf[f, q, pl.ds(r, 8, stride=reps), :] = cells[f]

    for step in range(FINE_STEPS):
        stage(None, state, reps, 0.0, 1.0, TSTEP, second.put_cell)
        stage(state, second, reps, 0.75, 0.25, 0.25 * TSTEP, third.put_cell)
        last = step + 1 == FINE_STEPS
        stage(state, third, reps, 1.0 / 3.0, 2.0 / 3.0, 2.0 / 3.0 * TSTEP, finish if last else state.put_cell)
    for f in range(3):
        for a in range(groups):
            put_blocks(finals_out, f, a, [rows_buf[f, q, 8 * a : 8 * a + 8, :] for q in range(8)])
    g_out[...] = dot3(enc[...], side_by_side(finals_out)) + t_part


def weighted_kernel(*refs):
    *parts, weights, out = refs
    out[...] = dot3(weights[...], jnp.concatenate([part[...] for part in parts], axis=0))


def base_kernel(finals, *refs):
    *parts, weights, out_hbm, out, sems = refs
    change = dot3(weights[...], jnp.concatenate([part[...] for part in parts], axis=0))
    copies = []
    for a in range(finals.shape[0]):
        rows = pl.ds(8 * a, 8)
        for f in range(3):
            places = [slice(64 * f + 8 * q, 64 * f + 8 * q + 8) for q in range(8)]
            joined = join_columns([finals[a, k, :] + change[k, LANES * a : LANES * (a + 1)] for k in places])
            for j, chunk in enumerate(joined):
                out[f, 8 * a : 8 * a + 8, LANES * j : LANES * (j + 1)] = chunk
            copies.append(pltpu.make_async_copy(out.at[f, rows], out_hbm.at[0, f, rows], sems.at[3 * a + f]))
            copies[-1].start()
    for copy in copies:
        copy.wait()


def output_kernel(inner, order, base, *refs):
    *totals, weights, _, out_hbm, joined_out, sems = refs
    group = lax.axis_index("cuts") // inner

    @pl.when(group > 0)
    def _():
        taken = [jnp.where((group ^ d) < group, part[...], 0.0) for d, part in zip(order, totals)]
        change = dot3(weights[...], jnp.concatenate(taken, axis=0))
        copies = []
        for a in range(base.shape[1] // DOWN):
            rows = pl.ds(8 * a, 8)
            for f in range(3):
                places = [slice(64 * f + 8 * q, 64 * f + 8 * q + 8) for q in range(8)]
                joined = join_columns([change[k, LANES * a : LANES * (a + 1)] for k in places])
                for j, chunk in enumerate(joined):
                    cells = (f, slice(8 * a, 8 * a + 8), slice(LANES * j, LANES * (j + 1)))
                    joined_out[cells] = base[cells] + chunk
                copies.append(pltpu.make_async_copy(joined_out.at[f, rows], out_hbm.at[0, f, rows], sems.at[3 * a + f]))
                copies[-1].start()
        for copy in copies:
            copy.wait()


def call(kernel, shapes, inputs, scratch=(), flops=0, inside=None, outside=None, aliases={}):
    return pl.pallas_call(
        kernel,
        out_shape=[jax.ShapeDtypeStruct(s, F32) for s in shapes],
        in_specs=inside or [VMEM] * len(inputs),
        out_specs=outside or [VMEM] * len(shapes),
        scratch_shapes=list(scratch),
        input_output_aliases=aliases,
        compiler_params=pltpu.CompilerParams(vmem_limit_bytes=40 * 1024 * 1024),
        cost_estimate=pl.CostEstimate(
            flops=flops, bytes_accessed=sum(4 * x.size for x in inputs), transcendentals=0
        ),
    )(*inputs)


def neighbour_rows(state):
    count = lax.axis_size("row")
    rows = state.shape[1]
    if count == 1:
        return jnp.concatenate([state[:, :HALO], state[:, rows - HALO :]], axis=1)
    forward = [(i, (i + 1) % count) for i in range(count)]
    backward = [((i + 1) % count, i) for i in range(count)]
    if count == 2 and rows <= 2 * HALO:
        return lax.ppermute(state, "row", forward)
    below = lax.ppermute(state[:, :HALO], "row", backward)
    above = lax.ppermute(state[:, rows - HALO :], "row", forward)
    return jnp.concatenate([below, above], axis=1)


def swapped(value, distance):
    return lax.ppermute(value, "cuts", [(i, i ^ distance) for i in range(lax.axis_size("cuts"))])


def local(starts, initial, encode_weight, decode_weight, latent_rate, coupling):
    lat = coupling.shape[0]
    state = starts[0]
    rows = state.shape[1]
    groups = rows // DOWN
    wide = groups * LANES
    size = encode_weight.shape[1]
    slices = lax.axis_size("cuts")
    inner = 1 << (slices.bit_length() // 2)
    outer = slices // inner
    near_order = (2, 1, *range(3, inner)) if inner > 2 else tuple(range(1, inner))
    far_order = (2, 1, *range(3, outer)) if outer > 2 else tuple(range(1, outer))
    rate = latent_rate.reshape(1, lat)
    other = neighbour_rows(state)
    given = (state, initial, encode_weight, rate, coupling)
    own, offset, enc, coarse = call(
        split_kernel,
        [(3, 8, rows, LANES), (groups, size, LANES), encode_weight.shape, (lat, lat)],
        [pltpu.with_memory_space_constraint(x, pltpu.HBM) for x in given],
        [pltpu.VMEM(x.shape, F32) for x in given] + [pltpu.SemaphoreType.DMA((7,))],
        flops=100_000_000,
        inside=[pl.BlockSpec(memory_space=pl.ANY)] * len(given),
    )
    reps = (rows + other.shape[1]) // 8
    pad = pltpu.VMEM((3, reps + 4, 12, 8, LANES), F32)
    finals, g_part, t_part = call(
        fine_kernel,
        [(groups, size, LANES), (lat, wide), (lat, wide)],
        [own, other, offset, enc, coarse],
        [pltpu.VMEM((3, 8, 8 * reps, LANES), F32), pad, pad, pad],
        flops=400_000_000,
    )
    parts = [swapped(g_part, d) for d in near_order]
    to_total, to_near, to_far = call(
        functools.partial(powers_kernel, inner, near_order, far_order),
        [(lat, inner * lat), (size, inner * lat), (size, (outer - 1) * lat)],
        [decode_weight.T, coarse],
        [pltpu.VMEM((inner + 1, lat, lat), F32), pltpu.VMEM((outer - 1, size, lat), F32)],
        flops=50_000_000,
    )
    (total,) = call(weighted_kernel, [(lat, wide)], [g_part, *parts, to_total], flops=50_000_000)
    totals = [swapped(total, inner * d) for d in far_order]
    hbm = pl.BlockSpec(memory_space=pltpu.HBM)
    tiles = pltpu.SemaphoreType.DMA((3 * groups,))
    result = (1, *state.shape)
    near_result, base = call(
        base_kernel,
        [result, state.shape],
        [finals, t_part, *parts, to_near],
        [tiles],
        flops=50_000_000,
        outside=[hbm, VMEM],
    )
    (out,) = call(
        functools.partial(output_kernel, inner, far_order),
        [result],
        [base, *totals, to_far, near_result],
        [pltpu.VMEM(state.shape, F32), tiles],
        flops=50_000_000,
        inside=[VMEM] * (outer + 1) + [hbm],
        outside=[hbm],
        aliases={outer + 1: 0},
    )
    return out


def solution(mesh):
    return jax.shard_map(
        local,
        mesh=mesh,
        in_specs=(P("cuts", None, "row", None), P(None, "row", None), P(), P(), P(), P()),
        out_specs=P("cuts", None, "row", None),
        check_vma=False,
    )
```

```python
import functools

import jax
import jax.numpy as jnp
from jax import lax
from jax.experimental import pallas as pl
from jax.experimental.pallas import tpu as pltpu
from jax.sharding import PartitionSpec as P

DOWN = 8
FINE_STEPS = 2
FCOR = 0.3
TSTEP = 0.25
HALO = 6 * FINE_STEPS
LANES = 128
F32 = jnp.float32
BF16 = jnp.bfloat16
VMEM = pl.BlockSpec(memory_space=pltpu.VMEM)


def halves(value):
    high = value.astype(BF16)
    return high, (value - high.astype(F32)).astype(BF16)


def dot3(left, right, contract=((1,), (0,))):
    dims = (contract, ((), ()))
    lh, ll = halves(left)
    rh, rl = halves(right)
    one = functools.partial(lax.dot_general, dimension_numbers=dims, preferred_element_type=F32)
    return one(lh, rh) + (one(lh, rl) + one(ll, rh))


def dot_full(left, right):
    return jnp.dot(left, right, precision=lax.Precision.HIGHEST, preferred_element_type=F32)


def lanes_iota():
    return lax.broadcasted_iota(jnp.int32, (8, LANES), 1)


def split_columns(chunks):
    lane = lanes_iota()
    moved = [c if j == 0 else pltpu.roll(c, j, 1) for j, c in enumerate(chunks)]
    phase = lane & 7
    out = []
    for q in range(8):
        merged = moved[0]
        for j in range(1, 8):
            merged = jnp.where(phase == (q + j) % 8, moved[j], merged)
        place = (8 * (lane & 15) + q + (lane >> 4)) & (LANES - 1)
        out.append(jnp.take_along_axis(merged, place, axis=1))
    return out


def join_columns(parts):
    lane = lanes_iota()
    phase = lane & 7
    picked = []
    for q, part in enumerate(parts):
        j = (lane - q) & 7
        place = 16 * j + (((lane - q - j) & (LANES - 1)) >> 3)
        picked.append(jnp.take_along_axis(part, place, axis=1))
    out = []
    for j in range(8):
        merged = picked[(-j) % 8]
        for q in range(8):
            if q != (-j) % 8:
                merged = jnp.where(phase == (q + j) % 8, picked[q], merged)
        out.append(merged if j == 0 else pltpu.roll(merged, LANES - j, 1))
    return out


def chunks_of(ref, field, row):
    return [ref[field, row : row + 8, LANES * j : LANES * (j + 1)] for j in range(8)]


def identity(size):
    rows = lax.broadcasted_iota(jnp.int32, (size, size), 0)
    return (rows == lax.broadcasted_iota(jnp.int32, (size, size), 1)).astype(F32)


def coarse_matrix(rate, coupling):
    return (rate * (identity(coupling.shape[0]) + coupling.T - coupling)).T


def put_blocks(ref, field, group, parts):
    for q, part in enumerate(parts):
        ref[group, 64 * field + 8 * q : 64 * field + 8 * q + 8, :] = part


def reordered(weight):
    size = weight.shape[1]
    source = lax.broadcasted_iota(jnp.int32, (size, size), 0)
    target = lax.broadcasted_iota(jnp.int32, (size, size), 1)
    wanted = (target & ~63) | ((target & 7) << 3) | ((target >> 3) & 7)
    return dot_full(weight, (source == wanted).astype(F32))


def side_by_side(ref):
    return jnp.concatenate([ref[a] for a in range(ref.shape[0])], axis=1)


def split_kernel(starts_hbm, initial_hbm, enc_hbm, rate_hbm, coup_hbm, *refs):
    own_out, offset_out, enc_out, coarse_out, starts, initial, enc, rate, coup, sems = refs
    count = starts.shape[0]
    pieces = [(enc_hbm, enc), (rate_hbm, rate), (coup_hbm, coup)] + [(starts_hbm.at[f], starts.at[f]) for f in range(count)]
    copies = [pltpu.make_async_copy(src, dst, sems.at[i]) for i, (src, dst) in enumerate(pieces)]
    for copy in copies[3:] + copies[:3]:
        copy.start()
    first = lax.axis_index("cuts") == 0
    given = pltpu.make_async_copy(initial_hbm, initial, sems.at[len(copies)])

    @pl.when(first)
    def _():
        given.start()

    for copy in copies:
        copy.wait()
    enc_out[...] = reordered(enc[...])
    coarse_out[...] = coarse_matrix(rate[...], coup[...])
    for f in range(count):
        for a in range(starts.shape[1] // DOWN):
            parts = split_columns(chunks_of(starts, f, 8 * a))
            for q, part in enumerate(parts):
                own_out[f, q, 8 * a : 8 * a + 8, :] = part
            put_blocks(offset_out, f, a, [-part for part in parts])

    @pl.when(first)
    def _():
        given.wait()
        for f in range(count):
            for a in range(starts.shape[1] // DOWN):
                parts = split_columns(chunks_of(initial, f, 8 * a))
                mine = [own_out[f, q, 8 * a : 8 * a + 8, :] for q in range(8)]
                put_blocks(offset_out, f, a, [part - m for part, m in zip(parts, mine)])


def powers_kernel(inner, order, dec, matrix, carry_out, step_out, base_out, near_out, held, far_held):
    lat = matrix.shape[0]
    inside = lax.axis_index("cuts") % inner
    group = lax.axis_index("cuts") // inner
    powers = [identity(lat), matrix[...]]
    for k in range(2, inner + 1):
        powers.append(dot_full(powers[k // 2], powers[k - k // 2]))
    step = powers[inner]
    step_out[...] = step
    lifted = powers[0]
    for k in range(len(order)):
        far_held[k] = lifted
        if k + 1 < len(order):
            lifted = dot_full(lifted, step)
    picked = [far_held[jnp.maximum(group - 1 - (group ^ d), 0)] for d in order]
    carry_out[...] = jnp.concatenate(picked, axis=1)
    weight = reordered(dec[...]).T
    base_out[...] = jnp.concatenate([weight, dot_full(weight, step)], axis=1)
    for k in range(inner):
        held[k] = dot_full(weight, powers[k])
    near_out[...] = jnp.concatenate([held[(inside - (inside ^ d) + inner) % inner] for d in range(1, inner)], axis=1)


class Padded:
    def __init__(self, ref, reps):
        self.ref = ref
        self.reps = reps

    def put_cell(self, r, q, *cells):
        ref, reps = self.ref, self.reps
        for field, value in enumerate(cells):
            ref[field, r + 2, q + 2] = value
            if r < 2:
                ref[field, r + reps + 2, q + 2] = pltpu.roll(value, 7, 0)
            if r >= reps - 2:
                ref[field, r - reps + 2, q + 2] = pltpu.roll(value, 1, 0)
            if q < 2:
                ref[field, r + 2, q + 10] = pltpu.roll(value, LANES - 1, 1)
            if q >= 6:
                ref[field, r + 2, q - 6] = pltpu.roll(value, 1, 1)

    def cell(self, field, r, q):
        return self.ref[field, r + 2, q + 2]


def slope(before_2, before, after, after_2):
    return 8.0 * (after - before) - (after_2 - before_2)


def stage(base, now, reps, alpha, beta, gamma, put):
    scale = gamma / 12.0
    turn = 12.0 * FCOR

    def column(r, q):
        height, along_c, along_r = (now.cell(f, r, q) for f in range(3))
        return height, along_c, along_r, along_c + height * along_c

    for r in range(reps):
        window = [column(r, q) for q in range(-2, 2)]
        for q in range(8):
            window.append(column(r, q + 2))
            height, along_c, along_r, _ = window[2]
            cols = [slope(*(window[k][f] for k in (0, 1, 3, 4))) for f in range(4)]
            near = [[now.cell(f, r + k, q) for f in range(3)] for k in (-2, -1, 1, 2)]
            for cells in near:
                cells.append(cells[2] + cells[0] * cells[2])
            rows = [slope(*(cells[f] for cells in near)) for f in range(4)]
            d_height = cols[3] + rows[3]
            d_colvel = along_c * cols[1] + along_r * (rows[1] - turn) + cols[0]
            d_rowvel = along_c * (cols[2] + turn) + along_r * rows[2] + rows[0]
            new = []
            for f, (mine, d) in enumerate(((height, d_height), (along_c, d_colvel), (along_r, d_rowvel))):
                total = beta * mine if beta != 1.0 else mine
                if alpha:
                    total = total + alpha * base.cell(f, r, q)
                new.append(total - scale * d)
            put(r, q, *new)
            del window[0]


def fine_solve(own, other, finals, rows_buf, buf_a, buf_b, buf_c):
    local_rows = own.shape[2]
    ext = local_rows + other.shape[1]
    reps = ext // 8
    for f in range(3):
        for q in range(8):
            rows_buf[f, q, 0:local_rows, :] = own[f, q, :, :]
        for tile in range(other.shape[1] // 8):
            parts = split_columns(chunks_of(other, f, 8 * tile))
            for q in range(8):
                rows_buf[f, q, local_rows + 8 * tile : local_rows + 8 * tile + 8, :] = parts[q]
    state, second, third = Padded(buf_a, reps), Padded(buf_b, reps), Padded(buf_c, reps)
    for r in range(reps):
        for q in range(8):
            state.put_cell(r, q, *(rows_buf[f, q, pl.ds(r, 8, stride=reps), :] for f in range(3)))

    def finish(r, q, *cells):
        for f in range(3):
            rows_buf[f, q, pl.ds(r, 8, stride=reps), :] = cells[f]

    for step in range(FINE_STEPS):
        stage(None, state, reps, 0.0, 1.0, TSTEP, second.put_cell)
        stage(state, second, reps, 0.75, 0.25, 0.25 * TSTEP, third.put_cell)
        last = step + 1 == FINE_STEPS
        stage(state, third, reps, 1.0 / 3.0, 2.0 / 3.0, 2.0 / 3.0 * TSTEP, finish if last else state.put_cell)
    for f in range(3):
        for a in range(local_rows // DOWN):
            put_blocks(finals, f, a, [rows_buf[f, q, 8 * a : 8 * a + 8, :] for q in range(8)])


def fine_kernel(last, own, other, offset, enc, coarse, finals_out, g_out, t_out, *buffers):
    group_is_last = lax.axis_index("cuts") >= last

    @pl.when(jnp.logical_not(group_is_last))
    def _():
        t_part = dot3(coarse[...], dot3(enc[...], side_by_side(offset)))
        t_out[...] = t_part
        fine_solve(own, other, finals_out, *buffers)
        g_out[...] = dot3(enc[...], side_by_side(finals_out)) + t_part

    @pl.when(group_is_last)
    def _():
        t_part = dot3(coarse[...], dot3(enc[...], side_by_side(offset)))
        t_out[...] = t_part
        g_out[...] = t_part


def late_kernel(last, own, other, finals, g_in, enc, finals_out, g_out, *buffers):
    group_is_last = lax.axis_index("cuts") >= last

    @pl.when(group_is_last)
    def _():
        fine_solve(own, other, finals_out, *buffers)
        g_out[...] = dot3(enc[...], side_by_side(finals_out)) + g_in[...]

    @pl.when(jnp.logical_not(group_is_last))
    def _():
        finals_out[...] = finals[...]
        g_out[...] = g_in[...]


def carry_kernel(inner, order, g_in, *refs):
    parts, (weights, step, q_out), outs = refs[: len(order)], refs[len(order) : len(order) + 3], refs[len(order) + 3 :]
    inside = lax.axis_index("cuts") % inner
    group = lax.axis_index("cuts") // inner
    taken = [jnp.where((group ^ d) < group, part[...], 0.0) for d, part in zip(order, parts)]
    carried = dot3(weights[...], jnp.concatenate(taken, axis=0))
    q_out[...] = carried
    whole = g_in[...] + dot3(step[...], carried)
    for d, out in enumerate(outs, 1):
        out[...] = jnp.where((inside ^ d) > inside, whole, carried)


def base_kernel(finals, *refs):
    *parts, weights, out_hbm, out, sems = refs
    change = dot3(weights[...], jnp.concatenate([part[...] for part in parts], axis=0))
    copies = []
    for a in range(finals.shape[0]):
        rows = pl.ds(8 * a, 8)
        for f in range(3):
            places = [slice(64 * f + 8 * q, 64 * f + 8 * q + 8) for q in range(8)]
            joined = join_columns([finals[a, k, :] + change[k, LANES * a : LANES * (a + 1)] for k in places])
            for j, chunk in enumerate(joined):
                out[f, 8 * a : 8 * a + 8, LANES * j : LANES * (j + 1)] = chunk
            copies.append(pltpu.make_async_copy(out.at[f, rows], out_hbm.at[0, f, rows], sems.at[3 * a + f]))
            copies[-1].start()
    for copy in copies:
        copy.wait()


def output_kernel(base, *refs):
    *parts, weights, _, out_hbm, joined_out, sems = refs

    @pl.when(lax.axis_index("cuts") > 0)
    def _():
        change = dot3(weights[...], jnp.concatenate([part[...] for part in parts], axis=0))
        copies = []
        for a in range(base.shape[1] // DOWN):
            rows = pl.ds(8 * a, 8)
            for f in range(3):
                places = [slice(64 * f + 8 * q, 64 * f + 8 * q + 8) for q in range(8)]
                joined = join_columns([change[k, LANES * a : LANES * (a + 1)] for k in places])
                for j, chunk in enumerate(joined):
                    cells = (f, slice(8 * a, 8 * a + 8), slice(LANES * j, LANES * (j + 1)))
                    joined_out[cells] = base[cells] + chunk
                copies.append(pltpu.make_async_copy(joined_out.at[f, rows], out_hbm.at[0, f, rows], sems.at[3 * a + f]))
                copies[-1].start()
        for copy in copies:
            copy.wait()


def call(kernel, shapes, inputs, scratch=(), flops=0, inside=None, outside=None, aliases={}):
    return pl.pallas_call(
        kernel,
        out_shape=[jax.ShapeDtypeStruct(s, F32) for s in shapes],
        in_specs=inside or [VMEM] * len(inputs),
        out_specs=outside or [VMEM] * len(shapes),
        scratch_shapes=list(scratch),
        input_output_aliases=aliases,
        compiler_params=pltpu.CompilerParams(vmem_limit_bytes=40 * 1024 * 1024),
        cost_estimate=pl.CostEstimate(
            flops=flops, bytes_accessed=sum(4 * x.size for x in inputs), transcendentals=0
        ),
    )(*inputs)


def neighbour_rows(state):
    count = lax.axis_size("row")
    rows = state.shape[1]
    if count == 1:
        return jnp.concatenate([state[:, :HALO], state[:, rows - HALO :]], axis=1)
    forward = [(i, (i + 1) % count) for i in range(count)]
    backward = [((i + 1) % count, i) for i in range(count)]
    if count == 2 and rows <= 2 * HALO:
        return lax.ppermute(state, "row", forward)
    below = lax.ppermute(state[:, :HALO], "row", backward)
    above = lax.ppermute(state[:, rows - HALO :], "row", forward)
    return jnp.concatenate([below, above], axis=1)


def swapped(value, distance):
    return lax.ppermute(value, "cuts", [(i, i ^ distance) for i in range(lax.axis_size("cuts"))])


def local(starts, initial, encode_weight, decode_weight, latent_rate, coupling):
    lat = coupling.shape[0]
    state = starts[0]
    rows = state.shape[1]
    groups = rows // DOWN
    wide = groups * LANES
    size = encode_weight.shape[1]
    slices = lax.axis_size("cuts")
    inner = 1 << (slices.bit_length() // 2)
    outer = slices // inner
    order = (1, *range(outer - 1, 1, -1))
    rate = latent_rate.reshape(1, lat)
    other = neighbour_rows(state)
    given = (state, initial, encode_weight, rate, coupling)
    own, offset, enc, coarse = call(
        split_kernel,
        [(3, 8, rows, LANES), (groups, size, LANES), encode_weight.shape, (lat, lat)],
        [pltpu.with_memory_space_constraint(x, pltpu.HBM) for x in given],
        [pltpu.VMEM(x.shape, F32) for x in given] + [pltpu.SemaphoreType.DMA((7,))],
        flops=100_000_000,
        inside=[pl.BlockSpec(memory_space=pl.ANY)] * len(given),
    )
    reps = (rows + other.shape[1]) // 8
    pad = pltpu.VMEM((3, reps + 4, 12, 8, LANES), F32)
    buffers = [pltpu.VMEM((3, 8, 8 * reps, LANES), F32), pad, pad, pad]
    last = inner * (outer - 1)
    blocks = (groups, size, LANES)
    early, g_early, t_part = call(
        functools.partial(fine_kernel, last),
        [blocks, (lat, wide), (lat, wide)],
        [own, other, offset, enc, coarse],
        buffers,
        flops=400_000_000,
    )
    parts = [swapped(g_early, inner * d) for d in order]
    finals, g_part = call(
        functools.partial(late_kernel, last),
        [blocks, (lat, wide)],
        [own, other, early, g_early, enc],
        buffers,
        flops=200_000_000,
    )
    to_carry, step, to_base, to_near = call(
        functools.partial(powers_kernel, inner, order),
        [(lat, (outer - 1) * lat), (lat, lat), (size, 2 * lat), (size, (inner - 1) * lat)],
        [decode_weight.T, coarse],
        [pltpu.VMEM((inner, size, lat), F32), pltpu.VMEM((outer - 1, lat, lat), F32)],
        flops=50_000_000,
    )
    carried, *sent = call(
        functools.partial(carry_kernel, inner, order),
        [(lat, wide)] * inner,
        [g_part, *parts, to_carry, step],
        flops=50_000_000,
    )
    near = [swapped(part, d) for d, part in enumerate(sent, 1)]
    hbm = pl.BlockSpec(memory_space=pltpu.HBM)
    tiles = pltpu.SemaphoreType.DMA((3 * groups,))
    result = (1, *state.shape)
    near_result, base = call(
        base_kernel,
        [result, state.shape],
        [finals, t_part, carried, to_base],
        [tiles],
        flops=50_000_000,
        outside=[hbm, VMEM],
    )
    (out,) = call(
        output_kernel,
        [result],
        [base, *near, to_near, near_result],
        [pltpu.VMEM(state.shape, F32), tiles],
        flops=50_000_000,
        inside=[VMEM] * (inner + 1) + [hbm],
        outside=[hbm],
        aliases={inner + 1: 0},
    )
    return out


def solution(mesh):
    return jax.shard_map(
        local,
        mesh=mesh,
        in_specs=(P("cuts", None, "row", None), P(None, "row", None), P(), P(), P(), P()),
        out_specs=P("cuts", None, "row", None),
        check_vma=False,
    )
```

```python
import functools

import jax
import jax.numpy as jnp
from jax import lax
from jax.experimental import pallas as pl
from jax.experimental.pallas import tpu as pltpu
from jax.sharding import PartitionSpec as P

DOWN = 8
FINE_STEPS = 2
FCOR = 0.3
TSTEP = 0.25
HALO = 6 * FINE_STEPS
LANES = 128
F32 = jnp.float32
BF16 = jnp.bfloat16
VMEM = pl.BlockSpec(memory_space=pltpu.VMEM)


def halves(value):
    high = value.astype(BF16)
    return high, (value - high.astype(F32)).astype(BF16)


def dot3(left, right, contract=((1,), (0,))):
    dims = (contract, ((), ()))
    lh, ll = halves(left)
    rh, rl = halves(right)
    one = functools.partial(lax.dot_general, dimension_numbers=dims, preferred_element_type=F32)
    return one(lh, rh) + (one(lh, rl) + one(ll, rh))


def dot_full(left, right):
    return jnp.dot(left, right, precision=lax.Precision.HIGHEST, preferred_element_type=F32)


def lanes_iota():
    return lax.broadcasted_iota(jnp.int32, (8, LANES), 1)


def split_columns(chunks):
    lane = lanes_iota()
    moved = [c if j == 0 else pltpu.roll(c, j, 1) for j, c in enumerate(chunks)]
    phase = lane & 7
    out = []
    for q in range(8):
        merged = moved[0]
        for j in range(1, 8):
            merged = jnp.where(phase == (q + j) % 8, moved[j], merged)
        place = (8 * (lane & 15) + q + (lane >> 4)) & (LANES - 1)
        out.append(jnp.take_along_axis(merged, place, axis=1))
    return out


def join_columns(parts):
    lane = lanes_iota()
    phase = lane & 7
    picked = []
    for q, part in enumerate(parts):
        j = (lane - q) & 7
        place = 16 * j + (((lane - q - j) & (LANES - 1)) >> 3)
        picked.append(jnp.take_along_axis(part, place, axis=1))
    out = []
    for j in range(8):
        merged = picked[(-j) % 8]
        for q in range(8):
            if q != (-j) % 8:
                merged = jnp.where(phase == (q + j) % 8, picked[q], merged)
        out.append(merged if j == 0 else pltpu.roll(merged, LANES - j, 1))
    return out


def chunks_of(ref, field, row):
    return [ref[field, row : row + 8, LANES * j : LANES * (j + 1)] for j in range(8)]


def identity(size):
    rows = lax.broadcasted_iota(jnp.int32, (size, size), 0)
    return (rows == lax.broadcasted_iota(jnp.int32, (size, size), 1)).astype(F32)


def coarse_matrix(rate, coupling):
    return (rate * (identity(coupling.shape[0]) + coupling.T - coupling)).T


def put_blocks(ref, field, group, parts):
    for q, part in enumerate(parts):
        ref[group, 64 * field + 8 * q : 64 * field + 8 * q + 8, :] = part


def reordered(weight):
    size = weight.shape[1]
    source = lax.broadcasted_iota(jnp.int32, (size, size), 0)
    target = lax.broadcasted_iota(jnp.int32, (size, size), 1)
    wanted = (target & ~63) | ((target & 7) << 3) | ((target >> 3) & 7)
    return dot_full(weight, (source == wanted).astype(F32))


def side_by_side(ref):
    return jnp.concatenate([ref[a] for a in range(ref.shape[0])], axis=1)


def split_kernel(starts_hbm, initial_hbm, enc_hbm, rate_hbm, coup_hbm, *refs):
    own_out, offset_out, enc_out, coarse_out, starts, initial, enc, rate, coup, sems = refs
    count = starts.shape[0]
    pieces = [(enc_hbm, enc), (rate_hbm, rate), (coup_hbm, coup)] + [(starts_hbm.at[f], starts.at[f]) for f in range(count)]
    copies = [pltpu.make_async_copy(src, dst, sems.at[i]) for i, (src, dst) in enumerate(pieces)]
    for copy in copies[3:] + copies[:3]:
        copy.start()
    first = lax.axis_index("cuts") == 0
    given = pltpu.make_async_copy(initial_hbm, initial, sems.at[len(copies)])

    @pl.when(first)
    def _():
        given.start()

    for copy in copies:
        copy.wait()
    enc_out[...] = reordered(enc[...])
    coarse_out[...] = coarse_matrix(rate[...], coup[...])
    for f in range(count):
        for a in range(starts.shape[1] // DOWN):
            parts = split_columns(chunks_of(starts, f, 8 * a))
            for q, part in enumerate(parts):
                own_out[f, q, 8 * a : 8 * a + 8, :] = part
            put_blocks(offset_out, f, a, [-part for part in parts])

    @pl.when(first)
    def _():
        given.wait()
        for f in range(count):
            for a in range(starts.shape[1] // DOWN):
                parts = split_columns(chunks_of(initial, f, 8 * a))
                mine = [own_out[f, q, 8 * a : 8 * a + 8, :] for q in range(8)]
                put_blocks(offset_out, f, a, [part - m for part, m in zip(parts, mine)])


def powers_kernel(inner, order, dec, matrix, carry_out, base_out, near_out, held, far_held):
    lat = matrix.shape[0]
    inside = lax.axis_index("cuts") % inner
    group = lax.axis_index("cuts") // inner
    powers = [identity(lat), matrix[...]]
    for k in range(2, inner + 1):
        powers.append(dot_full(powers[k // 2], powers[k - k // 2]))
    step = powers[inner]
    lifted = powers[0]
    for k in range(len(order)):
        far_held[k] = lifted
        if k + 1 < len(order):
            lifted = dot_full(lifted, step)
    far_held[len(order)] = dot_full(lifted, step)
    places = [jnp.maximum(group - 1 - (group ^ d), 0) for d in order]
    rows = [jnp.concatenate([far_held[k + more] for k in places], axis=1) for more in (0, 1)]
    carry_out[...] = jnp.concatenate(rows, axis=0)
    weight = reordered(dec[...]).T
    base_out[...] = jnp.concatenate([weight, dot_full(weight, step)], axis=1)
    for k in range(inner):
        held[k] = dot_full(weight, powers[k])
    near_out[...] = jnp.concatenate([held[(inside - (inside ^ d) + inner) % inner] for d in range(inner - 1, 0, -1)], axis=1)


class Padded:
    def __init__(self, ref, reps):
        self.ref = ref
        self.reps = reps

    def put_cell(self, r, q, *cells):
        ref, reps = self.ref, self.reps
        for field, value in enumerate(cells):
            ref[field, r + 2, q + 2] = value
            if r < 2:
                ref[field, r + reps + 2, q + 2] = pltpu.roll(value, 7, 0)
            if r >= reps - 2:
                ref[field, r - reps + 2, q + 2] = pltpu.roll(value, 1, 0)
            if q < 2:
                ref[field, r + 2, q + 10] = pltpu.roll(value, LANES - 1, 1)
            if q >= 6:
                ref[field, r + 2, q - 6] = pltpu.roll(value, 1, 1)

    def cell(self, field, r, q):
        return self.ref[field, r + 2, q + 2]


def slope(before_2, before, after, after_2):
    return 8.0 * (after - before) - (after_2 - before_2)


def stage(base, now, reps, alpha, beta, gamma, put):
    scale = gamma / 12.0
    turn = 12.0 * FCOR

    def column(r, q):
        height, along_c, along_r = (now.cell(f, r, q) for f in range(3))
        return height, along_c, along_r, along_c + height * along_c

    for r in range(reps):
        window = [column(r, q) for q in range(-2, 2)]
        for q in range(8):
            window.append(column(r, q + 2))
            height, along_c, along_r, _ = window[2]
            cols = [slope(*(window[k][f] for k in (0, 1, 3, 4))) for f in range(4)]
            near = [[now.cell(f, r + k, q) for f in range(3)] for k in (-2, -1, 1, 2)]
            for cells in near:
                cells.append(cells[2] + cells[0] * cells[2])
            rows = [slope(*(cells[f] for cells in near)) for f in range(4)]
            d_height = cols[3] + rows[3]
            d_colvel = along_c * cols[1] + along_r * (rows[1] - turn) + cols[0]
            d_rowvel = along_c * (cols[2] + turn) + along_r * rows[2] + rows[0]
            new = []
            for f, (mine, d) in enumerate(((height, d_height), (along_c, d_colvel), (along_r, d_rowvel))):
                total = beta * mine if beta != 1.0 else mine
                if alpha:
                    total = total + alpha * base.cell(f, r, q)
                new.append(total - scale * d)
            put(r, q, *new)
            del window[0]


def fine_solve(own, other, finals, rows_buf, buf_a, buf_b, buf_c):
    local_rows = own.shape[2]
    ext = local_rows + other.shape[1]
    reps = ext // 8
    for f in range(3):
        for q in range(8):
            rows_buf[f, q, 0:local_rows, :] = own[f, q, :, :]
        for tile in range(other.shape[1] // 8):
            parts = split_columns(chunks_of(other, f, 8 * tile))
            for q in range(8):
                rows_buf[f, q, local_rows + 8 * tile : local_rows + 8 * tile + 8, :] = parts[q]
    state, second, third = Padded(buf_a, reps), Padded(buf_b, reps), Padded(buf_c, reps)
    for r in range(reps):
        for q in range(8):
            state.put_cell(r, q, *(rows_buf[f, q, pl.ds(r, 8, stride=reps), :] for f in range(3)))

    def finish(r, q, *cells):
        for f in range(3):
            rows_buf[f, q, pl.ds(r, 8, stride=reps), :] = cells[f]

    for step in range(FINE_STEPS):
        stage(None, state, reps, 0.0, 1.0, TSTEP, second.put_cell)
        stage(state, second, reps, 0.75, 0.25, 0.25 * TSTEP, third.put_cell)
        last = step + 1 == FINE_STEPS
        stage(state, third, reps, 1.0 / 3.0, 2.0 / 3.0, 2.0 / 3.0 * TSTEP, finish if last else state.put_cell)
    for f in range(3):
        for a in range(local_rows // DOWN):
            put_blocks(finals, f, a, [rows_buf[f, q, 8 * a : 8 * a + 8, :] for q in range(8)])


def fine_kernel(last, own, other, offset, enc, coarse, finals_out, g_out, t_out, *buffers):
    group_is_last = lax.axis_index("cuts") >= last

    @pl.when(jnp.logical_not(group_is_last))
    def _():
        t_part = dot3(coarse[...], dot3(enc[...], side_by_side(offset)))
        t_out[...] = t_part
        fine_solve(own, other, finals_out, *buffers)
        g_out[...] = dot3(enc[...], side_by_side(finals_out)) + t_part

    @pl.when(group_is_last)
    def _():
        t_part = dot3(coarse[...], dot3(enc[...], side_by_side(offset)))
        t_out[...] = t_part
        g_out[...] = t_part


def late_kernel(last, own, other, finals, g_in, enc, finals_out, g_out, *buffers):
    group_is_last = lax.axis_index("cuts") >= last

    @pl.when(group_is_last)
    def _():
        fine_solve(own, other, finals_out, *buffers)
        g_out[...] = dot3(enc[...], side_by_side(finals_out)) + g_in[...]

    @pl.when(jnp.logical_not(group_is_last))
    def _():
        finals_out[...] = finals[...]
        g_out[...] = g_in[...]


def carry_kernel(inner, order, g_in, *refs):
    parts, (weights, q_out), outs = refs[: len(order)], refs[len(order) : len(order) + 2], refs[len(order) + 2 :]
    inside = lax.axis_index("cuts") % inner
    group = lax.axis_index("cuts") // inner
    taken = [jnp.where((group ^ d) < group, part[...], 0.0) for d, part in zip(order, parts)]
    both = dot3(weights[...], jnp.concatenate(taken, axis=0))
    lat = g_in.shape[0]
    carried = both[:lat]
    q_out[...] = carried
    whole = g_in[...] + both[lat:]
    for d, out in enumerate(outs, 1):
        out[...] = jnp.where((inside ^ d) > inside, whole, carried)


def base_kernel(finals, *refs):
    *parts, weights, out_hbm, out, sems = refs
    change = dot3(weights[...], jnp.concatenate([part[...] for part in parts], axis=0))
    copies = []
    for a in range(finals.shape[0]):
        rows = pl.ds(8 * a, 8)
        for f in range(3):
            places = [slice(64 * f + 8 * q, 64 * f + 8 * q + 8) for q in range(8)]
            joined = join_columns([finals[a, k, :] + change[k, LANES * a : LANES * (a + 1)] for k in places])
            for j, chunk in enumerate(joined):
                out[f, 8 * a : 8 * a + 8, LANES * j : LANES * (j + 1)] = chunk
            copies.append(pltpu.make_async_copy(out.at[f, rows], out_hbm.at[0, f, rows], sems.at[3 * a + f]))
            copies[-1].start()
    for copy in copies:
        copy.wait()


def output_kernel(base, *refs):
    *parts, weights, _, out_hbm, joined_out, sems = refs

    @pl.when(lax.axis_index("cuts") > 0)
    def _():
        change = dot3(weights[...], jnp.concatenate([part[...] for part in parts], axis=0))
        copies = []
        for a in range(base.shape[1] // DOWN):
            rows = pl.ds(8 * a, 8)
            for f in range(3):
                places = [slice(64 * f + 8 * q, 64 * f + 8 * q + 8) for q in range(8)]
                joined = join_columns([change[k, LANES * a : LANES * (a + 1)] for k in places])
                for j, chunk in enumerate(joined):
                    cells = (f, slice(8 * a, 8 * a + 8), slice(LANES * j, LANES * (j + 1)))
                    joined_out[cells] = base[cells] + chunk
                copies.append(pltpu.make_async_copy(joined_out.at[f, rows], out_hbm.at[0, f, rows], sems.at[3 * a + f]))
                copies[-1].start()
        for copy in copies:
            copy.wait()


def call(kernel, shapes, inputs, scratch=(), flops=0, inside=None, outside=None, aliases={}):
    return pl.pallas_call(
        kernel,
        out_shape=[jax.ShapeDtypeStruct(s, F32) for s in shapes],
        in_specs=inside or [VMEM] * len(inputs),
        out_specs=outside or [VMEM] * len(shapes),
        scratch_shapes=list(scratch),
        input_output_aliases=aliases,
        compiler_params=pltpu.CompilerParams(vmem_limit_bytes=40 * 1024 * 1024),
        cost_estimate=pl.CostEstimate(
            flops=flops, bytes_accessed=sum(4 * x.size for x in inputs), transcendentals=0
        ),
    )(*inputs)


def neighbour_rows(state):
    count = lax.axis_size("row")
    rows = state.shape[1]
    if count == 1:
        return jnp.concatenate([state[:, :HALO], state[:, rows - HALO :]], axis=1)
    forward = [(i, (i + 1) % count) for i in range(count)]
    backward = [((i + 1) % count, i) for i in range(count)]
    if count == 2 and rows <= 2 * HALO:
        return lax.ppermute(state, "row", forward)
    below = lax.ppermute(state[:, :HALO], "row", backward)
    above = lax.ppermute(state[:, rows - HALO :], "row", forward)
    return jnp.concatenate([below, above], axis=1)


def swapped(value, distance):
    return lax.ppermute(value, "cuts", [(i, i ^ distance) for i in range(lax.axis_size("cuts"))])


def local(starts, initial, encode_weight, decode_weight, latent_rate, coupling):
    lat = coupling.shape[0]
    state = starts[0]
    rows = state.shape[1]
    groups = rows // DOWN
    wide = groups * LANES
    size = encode_weight.shape[1]
    slices = lax.axis_size("cuts")
    inner = 1 << (slices.bit_length() // 2)
    outer = slices // inner
    order = (1, *range(outer - 1, 1, -1))
    rate = latent_rate.reshape(1, lat)
    other = neighbour_rows(state)
    given = (state, initial, encode_weight, rate, coupling)
    own, offset, enc, coarse = call(
        split_kernel,
        [(3, 8, rows, LANES), (groups, size, LANES), encode_weight.shape, (lat, lat)],
        [pltpu.with_memory_space_constraint(x, pltpu.HBM) for x in given],
        [pltpu.VMEM(x.shape, F32) for x in given] + [pltpu.SemaphoreType.DMA((7,))],
        flops=100_000_000,
        inside=[pl.BlockSpec(memory_space=pl.ANY)] * len(given),
    )
    reps = (rows + other.shape[1]) // 8
    pad = pltpu.VMEM((3, reps + 4, 12, 8, LANES), F32)
    buffers = [pltpu.VMEM((3, 8, 8 * reps, LANES), F32), pad, pad, pad]
    last = inner * (outer - 1)
    blocks = (groups, size, LANES)
    early, g_early, t_part = call(
        functools.partial(fine_kernel, last),
        [blocks, (lat, wide), (lat, wide)],
        [own, other, offset, enc, coarse],
        buffers,
        flops=400_000_000,
    )
    parts = [swapped(g_early, inner * d) for d in order]
    finals, g_part = call(
        functools.partial(late_kernel, last),
        [blocks, (lat, wide)],
        [own, other, early, g_early, enc],
        buffers,
        flops=200_000_000,
    )
    to_carry, to_base, to_near = call(
        functools.partial(powers_kernel, inner, order),
        [(2 * lat, (outer - 1) * lat), (size, 2 * lat), (size, (inner - 1) * lat)],
        [decode_weight.T, coarse],
        [pltpu.VMEM((inner, size, lat), F32), pltpu.VMEM((outer, lat, lat), F32)],
        flops=50_000_000,
    )
    carried, *sent = call(
        functools.partial(carry_kernel, inner, order),
        [(lat, wide)] * inner,
        [g_part, *parts, to_carry],
        flops=50_000_000,
    )
    near = [swapped(sent[d - 1], d) for d in range(inner - 1, 0, -1)]
    hbm = pl.BlockSpec(memory_space=pltpu.HBM)
    tiles = pltpu.SemaphoreType.DMA((3 * groups,))
    result = (1, *state.shape)
    near_result, base = call(
        base_kernel,
        [result, state.shape],
        [finals, t_part, carried, to_base],
        [tiles],
        flops=50_000_000,
        outside=[hbm, VMEM],
    )
    (out,) = call(
        output_kernel,
        [result],
        [base, *near, to_near, near_result],
        [pltpu.VMEM(state.shape, F32), tiles],
        flops=50_000_000,
        inside=[VMEM] * (inner + 1) + [hbm],
        outside=[hbm],
        aliases={inner + 1: 0},
    )
    return out


def solution(mesh):
    return jax.shard_map(
        local,
        mesh=mesh,
        in_specs=(P("cuts", None, "row", None), P(None, "row", None), P(), P(), P(), P()),
        out_specs=P("cuts", None, "row", None),
        check_vma=False,
    )
```

```python
import functools

import jax
import jax.numpy as jnp
from jax import lax
from jax.experimental import pallas as pl
from jax.experimental.pallas import tpu as pltpu
from jax.sharding import PartitionSpec as P

DOWN = 8
FINE_STEPS = 2
FCOR = 0.3
TSTEP = 0.25
HALO = 6 * FINE_STEPS
LANES = 128
F32 = jnp.float32
BF16 = jnp.bfloat16
VMEM = pl.BlockSpec(memory_space=pltpu.VMEM)


def halves(value):
    high = value.astype(BF16)
    return high, (value - high.astype(F32)).astype(BF16)


def dot3(left, right):
    lh, ll = halves(left)
    rh, rl = halves(right)
    one = functools.partial(jnp.dot, preferred_element_type=F32)
    both = one(jnp.concatenate([lh, ll], axis=0), rh)
    rows = left.shape[0]
    return both[:rows] + (one(lh, rl) + both[rows:])


def dot_full(left, right):
    return jnp.dot(left, right, precision=lax.Precision.HIGHEST, preferred_element_type=F32)


def lanes_iota():
    return lax.broadcasted_iota(jnp.int32, (8, LANES), 1)


def split_columns(chunks):
    lane = lanes_iota()
    moved = [c if j == 0 else pltpu.roll(c, j, 1) for j, c in enumerate(chunks)]
    phase = lane & 7
    out = []
    for q in range(8):
        merged = moved[0]
        for j in range(1, 8):
            merged = jnp.where(phase == (q + j) % 8, moved[j], merged)
        place = (8 * (lane & 15) + q + (lane >> 4)) & (LANES - 1)
        out.append(jnp.take_along_axis(merged, place, axis=1))
    return out


def join_columns(parts):
    lane = lanes_iota()
    phase = lane & 7
    picked = []
    for q, part in enumerate(parts):
        j = (lane - q) & 7
        place = 16 * j + (((lane - q - j) & (LANES - 1)) >> 3)
        picked.append(jnp.take_along_axis(part, place, axis=1))
    out = []
    for j in range(8):
        merged = picked[(-j) % 8]
        for q in range(8):
            if q != (-j) % 8:
                merged = jnp.where(phase == (q + j) % 8, picked[q], merged)
        out.append(merged if j == 0 else pltpu.roll(merged, LANES - j, 1))
    return out


def chunks_of(ref, field, row):
    return [ref[field, row : row + 8, LANES * j : LANES * (j + 1)] for j in range(8)]


def identity(size):
    rows = lax.broadcasted_iota(jnp.int32, (size, size), 0)
    return (rows == lax.broadcasted_iota(jnp.int32, (size, size), 1)).astype(F32)


def coarse_matrix(rate, coupling):
    return (rate * (identity(coupling.shape[0]) + coupling.T - coupling)).T


def put_blocks(ref, field, group, parts):
    for q, part in enumerate(parts):
        ref[group, 64 * field + 8 * q : 64 * field + 8 * q + 8, :] = part


def reordered(weight):
    size = weight.shape[1]
    source = lax.broadcasted_iota(jnp.int32, (size, size), 0)
    target = lax.broadcasted_iota(jnp.int32, (size, size), 1)
    wanted = (target & ~63) | ((target & 7) << 3) | ((target >> 3) & 7)
    return dot_full(weight, (source == wanted).astype(F32))


def side_by_side(ref):
    return jnp.concatenate([ref[a] for a in range(ref.shape[0])], axis=1)


def split_kernel(starts_hbm, initial_hbm, enc_hbm, rate_hbm, coup_hbm, *refs):
    own_out, offset_out, enc_out, coarse_out, starts, initial, enc, rate, coup, sems = refs
    count = starts.shape[0]
    pieces = [(enc_hbm, enc), (rate_hbm, rate), (coup_hbm, coup)] + [(starts_hbm.at[f], starts.at[f]) for f in range(count)]
    copies = [pltpu.make_async_copy(src, dst, sems.at[i]) for i, (src, dst) in enumerate(pieces)]
    for copy in copies[3:] + copies[:3]:
        copy.start()
    first = lax.axis_index("cuts") == 0
    given = pltpu.make_async_copy(initial_hbm, initial, sems.at[len(copies)])

    @pl.when(first)
    def _():
        given.start()

    for copy in copies:
        copy.wait()
    enc_out[...] = reordered(enc[...])
    coarse_out[...] = coarse_matrix(rate[...], coup[...])
    for f in range(count):
        for a in range(starts.shape[1] // DOWN):
            parts = split_columns(chunks_of(starts, f, 8 * a))
            for q, part in enumerate(parts):
                own_out[f, q, 8 * a : 8 * a + 8, :] = part
            put_blocks(offset_out, f, a, [-part for part in parts])

    @pl.when(first)
    def _():
        given.wait()
        for f in range(count):
            for a in range(starts.shape[1] // DOWN):
                parts = split_columns(chunks_of(initial, f, 8 * a))
                mine = [own_out[f, q, 8 * a : 8 * a + 8, :] for q in range(8)]
                put_blocks(offset_out, f, a, [part - m for part, m in zip(parts, mine)])


def powers_kernel(inner, order, dec, matrix, total_out, near_out, far_out, held, decoded_held):
    lat = matrix.shape[0]
    inside = lax.axis_index("cuts") % inner
    coarse = matrix[...]
    powers = [identity(lat), coarse]
    for k in range(2, inner + 1):
        powers.append(dot_full(powers[k // 2], powers[k - k // 2]))
    for k, power in enumerate(powers):
        held[k] = power
    weight = reordered(dec[...]).T
    decoded = [weight]
    for d in range(1, inner):
        place = inside ^ d
        part = dot_full(weight, held[jnp.maximum(inside - place, 0)])
        decoded.append(jnp.where(place < inside, part, 0.0))
    near_out[...] = jnp.concatenate(decoded, axis=1)
    total_out[...] = jnp.concatenate([held[inner - 1 - (inside ^ d)] for d in range(inner)], axis=1)
    group = lax.axis_index("cuts") // inner
    far = [dot_full(weight, held[inside + 1])]
    for k in range(2, len(order) + 1):
        far.append(dot_full(far[-1], powers[inner]))
    for k, part in enumerate(far):
        decoded_held[k] = part
    picked = [decoded_held[jnp.maximum(group - 1 - (group ^ d), 0)] for d in order]
    far_out[...] = jnp.concatenate(picked, axis=1)


class Padded:
    def __init__(self, ref, reps):
        self.ref = ref
        self.reps = reps

    def put_cell(self, r, q, *cells):
        ref, reps = self.ref, self.reps
        for field, value in enumerate(cells):
            ref[field, r + 2, q + 2] = value
            if r < 2:
                ref[field, r + reps + 2, q + 2] = pltpu.roll(value, 7, 0)
            if r >= reps - 2:
                ref[field, r - reps + 2, q + 2] = pltpu.roll(value, 1, 0)
            if q < 2:
                ref[field, r + 2, q + 10] = pltpu.roll(value, LANES - 1, 1)
            if q >= 6:
                ref[field, r + 2, q - 6] = pltpu.roll(value, 1, 1)

    def cell(self, field, r, q):
        return self.ref[field, r + 2, q + 2]


def slope(before_2, before, after, after_2):
    return 8.0 * (after - before) - (after_2 - before_2)


def stage(base, now, reps, alpha, beta, gamma, put):
    scale = gamma / 12.0
    turn = 12.0 * FCOR

    def column(r, q):
        height, along_c, along_r = (now.cell(f, r, q) for f in range(3))
        return height, along_c, along_r, along_c + height * along_c

    for r in range(reps):
        window = [column(r, q) for q in range(-2, 2)]
        for q in range(8):
            window.append(column(r, q + 2))
            height, along_c, along_r, _ = window[2]
            cols = [slope(*(window[k][f] for k in (0, 1, 3, 4))) for f in range(4)]
            near = [[now.cell(f, r + k, q) for f in range(3)] for k in (-2, -1, 1, 2)]
            for cells in near:
                cells.append(cells[2] + cells[0] * cells[2])
            rows = [slope(*(cells[f] for cells in near)) for f in range(4)]
            d_height = cols[3] + rows[3]
            d_colvel = along_c * cols[1] + along_r * (rows[1] - turn) + cols[0]
            d_rowvel = along_c * (cols[2] + turn) + along_r * rows[2] + rows[0]
            new = []
            for f, (mine, d) in enumerate(((height, d_height), (along_c, d_colvel), (along_r, d_rowvel))):
                total = beta * mine if beta != 1.0 else mine
                if alpha:
                    total = total + alpha * base.cell(f, r, q)
                new.append(total - scale * d)
            put(r, q, *new)
            del window[0]


def fine_kernel(own, other, offset, enc, coarse, finals_out, g_out, t_out, rows_buf, buf_a, buf_b, buf_c):
    local_rows = own.shape[2]
    ext = local_rows + other.shape[1]
    reps = ext // 8
    groups = local_rows // DOWN
    for f in range(3):
        for q in range(8):
            rows_buf[f, q, 0:local_rows, :] = own[f, q, :, :]
        for tile in range(other.shape[1] // 8):
            parts = split_columns(chunks_of(other, f, 8 * tile))
            for q in range(8):
                rows_buf[f, q, local_rows + 8 * tile : local_rows + 8 * tile + 8, :] = parts[q]
    t_part = dot3(coarse[...], dot3(enc[...], side_by_side(offset)))
    t_out[...] = t_part
    state, second, third = Padded(buf_a, reps), Padded(buf_b, reps), Padded(buf_c, reps)
    for r in range(reps):
        for q in range(8):
            state.put_cell(r, q, *(rows_buf[f, q, pl.ds(r, 8, stride=reps), :] for f in range(3)))

    def finish(r, q, *cells):
        for f in range(3):
            rows_buf[f, q, pl.ds(r, 8, stride=reps), :] = cells[f]

    for step in range(FINE_STEPS):
        stage(None, state, reps, 0.0, 1.0, TSTEP, second.put_cell)
        stage(state, second, reps, 0.75, 0.25, 0.25 * TSTEP, third.put_cell)
        last = step + 1 == FINE_STEPS
        stage(state, third, reps, 1.0 / 3.0, 2.0 / 3.0, 2.0 / 3.0 * TSTEP, finish if last else state.put_cell)
    ends = []
    for a in range(groups):
        parts = [rows_buf[f, q, 8 * a : 8 * a + 8, :] for f in range(3) for q in range(8)]
        ends.append(jnp.concatenate(parts, axis=0))
        finals_out[a] = ends[a]
    g_out[...] = dot3(enc[...], jnp.concatenate(ends, axis=1)) + t_part


def weighted_kernel(*refs):
    *parts, weights, out = refs
    out[...] = dot3(weights[...], jnp.concatenate([part[...] for part in parts], axis=0))


def base_kernel(finals, *refs):
    *parts, weights, out_hbm, out, sems = refs
    change = dot3(weights[...], jnp.concatenate([part[...] for part in parts], axis=0))
    copies = []
    for a in range(finals.shape[0]):
        rows = pl.ds(8 * a, 8)
        for f in range(3):
            places = [slice(64 * f + 8 * q, 64 * f + 8 * q + 8) for q in range(8)]
            joined = join_columns([finals[a, k, :] + change[k, LANES * a : LANES * (a + 1)] for k in places])
            for j, chunk in enumerate(joined):
                out[f, 8 * a : 8 * a + 8, LANES * j : LANES * (j + 1)] = chunk
            copies.append(pltpu.make_async_copy(out.at[f, rows], out_hbm.at[0, f, rows], sems.at[3 * a + f]))
            copies[-1].start()
    for copy in copies:
        copy.wait()


def output_kernel(inner, order, base, *refs):
    *totals, weights, _, out_hbm, joined_out, sems = refs
    group = lax.axis_index("cuts") // inner

    @pl.when(group > 0)
    def _():
        taken = [jnp.where((group ^ d) < group, part[...], 0.0) for d, part in zip(order, totals)]
        change = dot3(weights[...], jnp.concatenate(taken, axis=0))
        copies = []
        for a in range(base.shape[1] // DOWN):
            rows = pl.ds(8 * a, 8)
            for f in range(3):
                places = [slice(64 * f + 8 * q, 64 * f + 8 * q + 8) for q in range(8)]
                joined = join_columns([change[k, LANES * a : LANES * (a + 1)] for k in places])
                for j, chunk in enumerate(joined):
                    cells = (f, slice(8 * a, 8 * a + 8), slice(LANES * j, LANES * (j + 1)))
                    joined_out[cells] = base[cells] + chunk
                copies.append(pltpu.make_async_copy(joined_out.at[f, rows], out_hbm.at[0, f, rows], sems.at[3 * a + f]))
                copies[-1].start()
        for copy in copies:
            copy.wait()


def call(kernel, shapes, inputs, scratch=(), flops=0, inside=None, outside=None, aliases={}):
    return pl.pallas_call(
        kernel,
        out_shape=[jax.ShapeDtypeStruct(s, F32) for s in shapes],
        in_specs=inside or [VMEM] * len(inputs),
        out_specs=outside or [VMEM] * len(shapes),
        scratch_shapes=list(scratch),
        input_output_aliases=aliases,
        compiler_params=pltpu.CompilerParams(vmem_limit_bytes=40 * 1024 * 1024),
        cost_estimate=pl.CostEstimate(
            flops=flops, bytes_accessed=sum(4 * x.size for x in inputs), transcendentals=0
        ),
    )(*inputs)


def neighbour_rows(state):
    count = lax.axis_size("row")
    rows = state.shape[1]
    if count == 1:
        return jnp.concatenate([state[:, :HALO], state[:, rows - HALO :]], axis=1)
    forward = [(i, (i + 1) % count) for i in range(count)]
    backward = [((i + 1) % count, i) for i in range(count)]
    if count == 2 and rows <= 2 * HALO:
        return lax.ppermute(state, "row", forward)
    below = lax.ppermute(state[:, :HALO], "row", backward)
    above = lax.ppermute(state[:, rows - HALO :], "row", forward)
    return jnp.concatenate([below, above], axis=1)


def swapped(value, distance):
    return lax.ppermute(value, "cuts", [(i, i ^ distance) for i in range(lax.axis_size("cuts"))])


def local(starts, initial, encode_weight, decode_weight, latent_rate, coupling):
    lat = coupling.shape[0]
    state = starts[0]
    rows = state.shape[1]
    groups = rows // DOWN
    wide = groups * LANES
    size = encode_weight.shape[1]
    slices = lax.axis_size("cuts")
    inner = 1 << (slices.bit_length() // 2)
    outer = slices // inner
    order = (1, *range(outer - 1, 1, -1))
    rate = latent_rate.reshape(1, lat)
    other = neighbour_rows(state)
    given = (state, initial, encode_weight, rate, coupling)
    own, offset, enc, coarse = call(
        split_kernel,
        [(3, 8, rows, LANES), (groups, size, LANES), encode_weight.shape, (lat, lat)],
        [pltpu.with_memory_space_constraint(x, pltpu.HBM) for x in given],
        [pltpu.VMEM(x.shape, F32) for x in given] + [pltpu.SemaphoreType.DMA((7,))],
        flops=100_000_000,
        inside=[pl.BlockSpec(memory_space=pl.ANY)] * len(given),
    )
    reps = (rows + other.shape[1]) // 8
    pad = pltpu.VMEM((3, reps + 4, 12, 8, LANES), F32)
    finals, g_part, t_part = call(
        fine_kernel,
        [(groups, size, LANES), (lat, wide), (lat, wide)],
        [own, other, offset, enc, coarse],
        [pltpu.VMEM((3, 8, 8 * reps, LANES), F32), pad, pad, pad],
        flops=400_000_000,
    )
    parts = [swapped(g_part, d) for d in range(1, inner)]
    to_total, to_near, to_far = call(
        functools.partial(powers_kernel, inner, order),
        [(lat, inner * lat), (size, inner * lat), (size, (outer - 1) * lat)],
        [decode_weight.T, coarse],
        [pltpu.VMEM((inner + 1, lat, lat), F32), pltpu.VMEM((outer - 1, size, lat), F32)],
        flops=50_000_000,
    )
    (total,) = call(weighted_kernel, [(lat, wide)], [g_part, *parts, to_total], flops=50_000_000)
    totals = [swapped(total, inner * d) for d in order]
    hbm = pl.BlockSpec(memory_space=pltpu.HBM)
    tiles = pltpu.SemaphoreType.DMA((3 * groups,))
    result = (1, *state.shape)
    near_result, base = call(
        base_kernel,
        [result, state.shape],
        [finals, t_part, *parts, to_near],
        [tiles],
        flops=50_000_000,
        outside=[hbm, VMEM],
    )
    (out,) = call(
        functools.partial(output_kernel, inner, order),
        [result],
        [base, *totals, to_far, near_result],
        [pltpu.VMEM(state.shape, F32), tiles],
        flops=50_000_000,
        inside=[VMEM] * (outer + 1) + [hbm],
        outside=[hbm],
        aliases={outer + 1: 0},
    )
    return out


def solution(mesh):
    return jax.shard_map(
        local,
        mesh=mesh,
        in_specs=(P("cuts", None, "row", None), P(None, "row", None), P(), P(), P(), P()),
        out_specs=P("cuts", None, "row", None),
        check_vma=False,
    )
```

```python
import functools

import jax
import jax.numpy as jnp
from jax import lax
from jax.experimental import pallas as pl
from jax.experimental.pallas import tpu as pltpu
from jax.sharding import PartitionSpec as P

DOWN = 8
FINE_STEPS = 2
FCOR = 0.3
TSTEP = 0.25
HALO = 6 * FINE_STEPS
LANES = 128
F32 = jnp.float32
BF16 = jnp.bfloat16
VMEM = pl.BlockSpec(memory_space=pltpu.VMEM)


def halves(value):
    high = value.astype(BF16)
    return high, (value - high.astype(F32)).astype(BF16)


def dot3(left, right):
    lh, ll = halves(left)
    rh, rl = halves(right)
    one = functools.partial(jnp.dot, preferred_element_type=F32)
    both = one(jnp.concatenate([lh, ll], axis=0), rh)
    rows = left.shape[0]
    return both[:rows] + (one(lh, rl) + both[rows:])


def dot_full(left, right):
    return jnp.dot(left, right, precision=lax.Precision.HIGHEST, preferred_element_type=F32)


def lanes_iota():
    return lax.broadcasted_iota(jnp.int32, (8, LANES), 1)


def split_columns(chunks):
    lane = lanes_iota()
    moved = [c if j == 0 else pltpu.roll(c, j, 1) for j, c in enumerate(chunks)]
    phase = lane & 7
    out = []
    for q in range(8):
        merged = moved[0]
        for j in range(1, 8):
            merged = jnp.where(phase == (q + j) % 8, moved[j], merged)
        place = (8 * (lane & 15) + q + (lane >> 4)) & (LANES - 1)
        out.append(jnp.take_along_axis(merged, place, axis=1))
    return out


def join_columns(parts):
    lane = lanes_iota()
    phase = lane & 7
    picked = []
    for q, part in enumerate(parts):
        j = (lane - q) & 7
        place = 16 * j + (((lane - q - j) & (LANES - 1)) >> 3)
        picked.append(jnp.take_along_axis(part, place, axis=1))
    out = []
    for j in range(8):
        merged = picked[(-j) % 8]
        for q in range(8):
            if q != (-j) % 8:
                merged = jnp.where(phase == (q + j) % 8, picked[q], merged)
        out.append(merged if j == 0 else pltpu.roll(merged, LANES - j, 1))
    return out


def chunks_of(ref, field, row):
    return [ref[field, row : row + 8, LANES * j : LANES * (j + 1)] for j in range(8)]


def identity(size):
    rows = lax.broadcasted_iota(jnp.int32, (size, size), 0)
    return (rows == lax.broadcasted_iota(jnp.int32, (size, size), 1)).astype(F32)


def coarse_matrix(rate, coupling):
    return (rate * (identity(coupling.shape[0]) + coupling.T - coupling)).T


def put_blocks(ref, field, group, parts):
    for q, part in enumerate(parts):
        ref[group, 64 * field + 8 * q : 64 * field + 8 * q + 8, :] = part


def reordered(weight):
    size = weight.shape[1]
    source = lax.broadcasted_iota(jnp.int32, (size, size), 0)
    target = lax.broadcasted_iota(jnp.int32, (size, size), 1)
    wanted = (target & ~63) | ((target & 7) << 3) | ((target >> 3) & 7)
    return dot_full(weight, (source == wanted).astype(F32))


def side_by_side(ref):
    return jnp.concatenate([ref[a] for a in range(ref.shape[0])], axis=1)


def split_kernel(starts_hbm, initial_hbm, enc_hbm, rate_hbm, coup_hbm, *refs):
    own_out, offset_out, enc_out, coarse_out, starts, initial, enc, rate, coup, sems = refs
    count = starts.shape[0]
    pieces = [(enc_hbm, enc), (rate_hbm, rate), (coup_hbm, coup)] + [(starts_hbm.at[f], starts.at[f]) for f in range(count)]
    copies = [pltpu.make_async_copy(src, dst, sems.at[i]) for i, (src, dst) in enumerate(pieces)]
    for copy in copies[3:] + copies[:3]:
        copy.start()
    first = lax.axis_index("cuts") == 0
    given = pltpu.make_async_copy(initial_hbm, initial, sems.at[len(copies)])

    @pl.when(first)
    def _():
        given.start()

    for copy in copies:
        copy.wait()
    enc_out[...] = reordered(enc[...])
    coarse_out[...] = coarse_matrix(rate[...], coup[...])
    for f in range(count):
        for a in range(starts.shape[1] // DOWN):
            parts = split_columns(chunks_of(starts, f, 8 * a))
            for q, part in enumerate(parts):
                own_out[f, q, 8 * a : 8 * a + 8, :] = part
            put_blocks(offset_out, f, a, [-part for part in parts])

    @pl.when(first)
    def _():
        given.wait()
        for f in range(count):
            for a in range(starts.shape[1] // DOWN):
                parts = split_columns(chunks_of(initial, f, 8 * a))
                mine = [own_out[f, q, 8 * a : 8 * a + 8, :] for q in range(8)]
                put_blocks(offset_out, f, a, [part - m for part, m in zip(parts, mine)])


def powers_kernel(inner, order, dec, matrix, total_out, near_out, far_out, held, decoded_held):
    lat = matrix.shape[0]
    inside = lax.axis_index("cuts") % inner
    coarse = matrix[...]
    powers = [identity(lat), coarse]
    for k in range(2, inner + 1):
        powers.append(dot_full(powers[k // 2], powers[k - k // 2]))
    for k, power in enumerate(powers):
        held[k] = power
    weight = reordered(dec[...]).T
    decoded = [weight]
    for d in range(1, inner):
        place = inside ^ d
        part = dot_full(weight, held[jnp.maximum(inside - place, 0)])
        decoded.append(jnp.where(place < inside, part, 0.0))
    near_out[...] = jnp.concatenate(decoded, axis=1)
    total_out[...] = jnp.concatenate([held[inner - 1 - (inside ^ d)] for d in range(inner)], axis=1)
    group = lax.axis_index("cuts") // inner
    far = [dot_full(weight, held[inside + 1])]
    for k in range(2, len(order) + 1):
        far.append(dot_full(far[-1], powers[inner]))
    for k, part in enumerate(far):
        decoded_held[k] = part
    picked = [decoded_held[jnp.maximum(group - 1 - (group ^ d), 0)] for d in order]
    far_out[...] = jnp.concatenate(picked, axis=1)


class Padded:
    def __init__(self, ref, reps):
        self.ref = ref
        self.reps = reps

    def put_cell(self, r, q, *cells):
        ref, reps = self.ref, self.reps
        height, _, along_r = cells
        for field, value in enumerate((*cells, along_r + height * along_r)):
            ref[field, r + 2, q + 2] = value
            if r < 2:
                ref[field, r + reps + 2, q + 2] = pltpu.roll(value, 7, 0)
            if r >= reps - 2:
                ref[field, r - reps + 2, q + 2] = pltpu.roll(value, 1, 0)
            if q < 2 and field < 3:
                ref[field, r + 2, q + 10] = pltpu.roll(value, LANES - 1, 1)
            if q >= 6 and field < 3:
                ref[field, r + 2, q - 6] = pltpu.roll(value, 1, 1)

    def cell(self, field, r, q):
        return self.ref[field, r + 2, q + 2]


def slope(before_2, before, after, after_2):
    return 8.0 * (after - before) - (after_2 - before_2)


def stage(base, now, reps, alpha, beta, gamma, put):
    scale = gamma / 12.0
    turn = 12.0 * FCOR

    def column(r, q):
        height, along_c, along_r = (now.cell(f, r, q) for f in range(3))
        return height, along_c, along_r, along_c + height * along_c

    for r in range(reps):
        window = [column(r, q) for q in range(-2, 2)]
        for q in range(8):
            window.append(column(r, q + 2))
            height, along_c, along_r, _ = window[2]
            cols = [slope(*(window[k][f] for k in (0, 1, 3, 4))) for f in range(4)]
            near = [[now.cell(f, r + k, q) for f in range(4)] for k in (-2, -1, 1, 2)]
            rows = [slope(*(cells[f] for cells in near)) for f in range(4)]
            d_height = cols[3] + rows[3]
            d_colvel = along_c * cols[1] + along_r * (rows[1] - turn) + cols[0]
            d_rowvel = along_c * (cols[2] + turn) + along_r * rows[2] + rows[0]
            new = []
            for f, (mine, d) in enumerate(((height, d_height), (along_c, d_colvel), (along_r, d_rowvel))):
                total = beta * mine if beta != 1.0 else mine
                if alpha:
                    total = total + alpha * base.cell(f, r, q)
                new.append(total - scale * d)
            put(r, q, *new)
            del window[0]


def fine_kernel(own, other, offset, enc, coarse, finals_out, g_out, t_out, rows_buf, buf_a, buf_b, buf_c):
    local_rows = own.shape[2]
    ext = local_rows + other.shape[1]
    reps = ext // 8
    groups = local_rows // DOWN
    for f in range(3):
        for q in range(8):
            rows_buf[f, q, 0:local_rows, :] = own[f, q, :, :]
        for tile in range(other.shape[1] // 8):
            parts = split_columns(chunks_of(other, f, 8 * tile))
            for q in range(8):
                rows_buf[f, q, local_rows + 8 * tile : local_rows + 8 * tile + 8, :] = parts[q]
    t_part = dot3(coarse[...], dot3(enc[...], side_by_side(offset)))
    t_out[...] = t_part
    state, second, third = Padded(buf_a, reps), Padded(buf_b, reps), Padded(buf_c, reps)
    for r in range(reps):
        for q in range(8):
            state.put_cell(r, q, *(rows_buf[f, q, pl.ds(r, 8, stride=reps), :] for f in range(3)))

    def finish(r, q, *cells):
        for f in range(3):
            rows_buf[f, q, pl.ds(r, 8, stride=reps), :] = cells[f]

    for step in range(FINE_STEPS):
        stage(None, state, reps, 0.0, 1.0, TSTEP, second.put_cell)
        stage(state, second, reps, 0.75, 0.25, 0.25 * TSTEP, third.put_cell)
        last = step + 1 == FINE_STEPS
        stage(state, third, reps, 1.0 / 3.0, 2.0 / 3.0, 2.0 / 3.0 * TSTEP, finish if last else state.put_cell)
    ends = []
    for a in range(groups):
        parts = [rows_buf[f, q, 8 * a : 8 * a + 8, :] for f in range(3) for q in range(8)]
        ends.append(jnp.concatenate(parts, axis=0))
        finals_out[a] = ends[a]
    g_out[...] = dot3(enc[...], jnp.concatenate(ends, axis=1)) + t_part


def weighted_kernel(*refs):
    *parts, weights, out = refs
    out[...] = dot3(weights[...], jnp.concatenate([part[...] for part in parts], axis=0))


def base_kernel(finals, *refs):
    *parts, weights, out_hbm, out, sems = refs
    change = dot3(weights[...], jnp.concatenate([part[...] for part in parts], axis=0))
    copies = []
    for a in range(finals.shape[0]):
        rows = pl.ds(8 * a, 8)
        for f in range(3):
            places = [slice(64 * f + 8 * q, 64 * f + 8 * q + 8) for q in range(8)]
            joined = join_columns([finals[a, k, :] + change[k, LANES * a : LANES * (a + 1)] for k in places])
            for j, chunk in enumerate(joined):
                out[f, 8 * a : 8 * a + 8, LANES * j : LANES * (j + 1)] = chunk
            copies.append(pltpu.make_async_copy(out.at[f, rows], out_hbm.at[0, f, rows], sems.at[3 * a + f]))
            copies[-1].start()
    for copy in copies:
        copy.wait()


def output_kernel(inner, order, base, *refs):
    *totals, weights, _, out_hbm, joined_out, sems = refs
    group = lax.axis_index("cuts") // inner

    @pl.when(group > 0)
    def _():
        taken = [jnp.where((group ^ d) < group, part[...], 0.0) for d, part in zip(order, totals)]
        change = dot3(weights[...], jnp.concatenate(taken, axis=0))
        copies = []
        for a in range(base.shape[1] // DOWN):
            rows = pl.ds(8 * a, 8)
            for f in range(3):
                places = [slice(64 * f + 8 * q, 64 * f + 8 * q + 8) for q in range(8)]
                joined = join_columns([change[k, LANES * a : LANES * (a + 1)] for k in places])
                for j, chunk in enumerate(joined):
                    cells = (f, slice(8 * a, 8 * a + 8), slice(LANES * j, LANES * (j + 1)))
                    joined_out[cells] = base[cells] + chunk
                copies.append(pltpu.make_async_copy(joined_out.at[f, rows], out_hbm.at[0, f, rows], sems.at[3 * a + f]))
                copies[-1].start()
        for copy in copies:
            copy.wait()


def call(kernel, shapes, inputs, scratch=(), flops=0, inside=None, outside=None, aliases={}):
    return pl.pallas_call(
        kernel,
        out_shape=[jax.ShapeDtypeStruct(s, F32) for s in shapes],
        in_specs=inside or [VMEM] * len(inputs),
        out_specs=outside or [VMEM] * len(shapes),
        scratch_shapes=list(scratch),
        input_output_aliases=aliases,
        compiler_params=pltpu.CompilerParams(vmem_limit_bytes=40 * 1024 * 1024),
        cost_estimate=pl.CostEstimate(
            flops=flops, bytes_accessed=sum(4 * x.size for x in inputs), transcendentals=0
        ),
    )(*inputs)


def neighbour_rows(state):
    count = lax.axis_size("row")
    rows = state.shape[1]
    if count == 1:
        return jnp.concatenate([state[:, :HALO], state[:, rows - HALO :]], axis=1)
    forward = [(i, (i + 1) % count) for i in range(count)]
    backward = [((i + 1) % count, i) for i in range(count)]
    if count == 2 and rows <= 2 * HALO:
        return lax.ppermute(state, "row", forward)
    below = lax.ppermute(state[:, :HALO], "row", backward)
    above = lax.ppermute(state[:, rows - HALO :], "row", forward)
    return jnp.concatenate([below, above], axis=1)


def swapped(value, distance):
    return lax.ppermute(value, "cuts", [(i, i ^ distance) for i in range(lax.axis_size("cuts"))])


def local(starts, initial, encode_weight, decode_weight, latent_rate, coupling):
    lat = coupling.shape[0]
    state = starts[0]
    rows = state.shape[1]
    groups = rows // DOWN
    wide = groups * LANES
    size = encode_weight.shape[1]
    slices = lax.axis_size("cuts")
    inner = 1 << (slices.bit_length() // 2)
    outer = slices // inner
    order = (1, *range(outer - 1, 1, -1))
    rate = latent_rate.reshape(1, lat)
    other = neighbour_rows(state)
    given = (state, initial, encode_weight, rate, coupling)
    own, offset, enc, coarse = call(
        split_kernel,
        [(3, 8, rows, LANES), (groups, size, LANES), encode_weight.shape, (lat, lat)],
        [pltpu.with_memory_space_constraint(x, pltpu.HBM) for x in given],
        [pltpu.VMEM(x.shape, F32) for x in given] + [pltpu.SemaphoreType.DMA((7,))],
        flops=100_000_000,
        inside=[pl.BlockSpec(memory_space=pl.ANY)] * len(given),
    )
    reps = (rows + other.shape[1]) // 8
    pad = pltpu.VMEM((4, reps + 4, 12, 8, LANES), F32)
    finals, g_part, t_part = call(
        fine_kernel,
        [(groups, size, LANES), (lat, wide), (lat, wide)],
        [own, other, offset, enc, coarse],
        [pltpu.VMEM((3, 8, 8 * reps, LANES), F32), pad, pad, pad],
        flops=400_000_000,
    )
    parts = [swapped(g_part, d) for d in range(1, inner)]
    to_total, to_near, to_far = call(
        functools.partial(powers_kernel, inner, order),
        [(lat, inner * lat), (size, inner * lat), (size, (outer - 1) * lat)],
        [decode_weight.T, coarse],
        [pltpu.VMEM((inner + 1, lat, lat), F32), pltpu.VMEM((outer - 1, size, lat), F32)],
        flops=50_000_000,
    )
    (total,) = call(weighted_kernel, [(lat, wide)], [g_part, *parts, to_total], flops=50_000_000)
    totals = [swapped(total, inner * d) for d in order]
    hbm = pl.BlockSpec(memory_space=pltpu.HBM)
    tiles = pltpu.SemaphoreType.DMA((3 * groups,))
    result = (1, *state.shape)
    near_result, base = call(
        base_kernel,
        [result, state.shape],
        [finals, t_part, *parts, to_near],
        [tiles],
        flops=50_000_000,
        outside=[hbm, VMEM],
    )
    (out,) = call(
        functools.partial(output_kernel, inner, order),
        [result],
        [base, *totals, to_far, near_result],
        [pltpu.VMEM(state.shape, F32), tiles],
        flops=50_000_000,
        inside=[VMEM] * (outer + 1) + [hbm],
        outside=[hbm],
        aliases={outer + 1: 0},
    )
    return out


def solution(mesh):
    return jax.shard_map(
        local,
        mesh=mesh,
        in_specs=(P("cuts", None, "row", None), P(None, "row", None), P(), P(), P(), P()),
        out_specs=P("cuts", None, "row", None),
        check_vma=False,
    )
```

```python
import functools

import jax
import jax.numpy as jnp
from jax import lax
from jax.experimental import pallas as pl
from jax.experimental.pallas import tpu as pltpu
from jax.sharding import PartitionSpec as P

DOWN = 8
FINE_STEPS = 2
FCOR = 0.3
TSTEP = 0.25
HALO = 6 * FINE_STEPS
LANES = 128
F32 = jnp.float32
BF16 = jnp.bfloat16
VMEM = pl.BlockSpec(memory_space=pltpu.VMEM)


def halves(value):
    high = value.astype(BF16)
    return high, (value - high.astype(F32)).astype(BF16)


def dot3(left, right):
    lh, ll = halves(left)
    rh, rl = halves(right)
    one = functools.partial(jnp.dot, preferred_element_type=F32)
    both = one(jnp.concatenate([lh, ll], axis=0), rh)
    rows = left.shape[0]
    return both[:rows] + (one(lh, rl) + both[rows:])


def dot_full(left, right):
    return jnp.dot(left, right, precision=lax.Precision.HIGHEST, preferred_element_type=F32)


def lanes_iota():
    return lax.broadcasted_iota(jnp.int32, (8, LANES), 1)


def split_columns(chunks):
    lane = lanes_iota()
    moved = [c if j == 0 else pltpu.roll(c, j, 1) for j, c in enumerate(chunks)]
    phase = lane & 7
    out = []
    for q in range(8):
        merged = moved[0]
        for j in range(1, 8):
            merged = jnp.where(phase == (q + j) % 8, moved[j], merged)
        place = (8 * (lane & 15) + q + (lane >> 4)) & (LANES - 1)
        out.append(jnp.take_along_axis(merged, place, axis=1))
    return out


def join_columns(parts):
    lane = lanes_iota()
    phase = lane & 7
    picked = []
    for q, part in enumerate(parts):
        j = (lane - q) & 7
        place = 16 * j + (((lane - q - j) & (LANES - 1)) >> 3)
        picked.append(jnp.take_along_axis(part, place, axis=1))
    out = []
    for j in range(8):
        merged = picked[(-j) % 8]
        for q in range(8):
            if q != (-j) % 8:
                merged = jnp.where(phase == (q + j) % 8, picked[q], merged)
        out.append(merged if j == 0 else pltpu.roll(merged, LANES - j, 1))
    return out


def chunks_of(ref, field, row):
    return [ref[field, row : row + 8, LANES * j : LANES * (j + 1)] for j in range(8)]


def identity(size):
    rows = lax.broadcasted_iota(jnp.int32, (size, size), 0)
    return (rows == lax.broadcasted_iota(jnp.int32, (size, size), 1)).astype(F32)


def coarse_matrix(rate, coupling):
    return (rate * (identity(coupling.shape[0]) + coupling.T - coupling)).T


def put_blocks(ref, field, group, parts):
    for q, part in enumerate(parts):
        ref[group, 64 * field + 8 * q : 64 * field + 8 * q + 8, :] = part


def reordered(weight):
    size = weight.shape[1]
    source = lax.broadcasted_iota(jnp.int32, (size, size), 0)
    target = lax.broadcasted_iota(jnp.int32, (size, size), 1)
    wanted = (target & ~63) | ((target & 7) << 3) | ((target >> 3) & 7)
    return dot_full(weight, (source == wanted).astype(F32))


def side_by_side(ref):
    return jnp.concatenate([ref[a] for a in range(ref.shape[0])], axis=1)


def split_kernel(starts_hbm, initial_hbm, enc_hbm, rate_hbm, coup_hbm, *refs):
    own_out, offset_out, enc_out, coarse_out, starts, initial, enc, rate, coup, sems = refs
    count = starts.shape[0]
    pieces = [(enc_hbm, enc), (rate_hbm, rate), (coup_hbm, coup)] + [(starts_hbm.at[f], starts.at[f]) for f in range(count)]
    copies = [pltpu.make_async_copy(src, dst, sems.at[i]) for i, (src, dst) in enumerate(pieces)]
    for copy in copies[3:] + copies[:3]:
        copy.start()
    first = lax.axis_index("cuts") == 0
    given = pltpu.make_async_copy(initial_hbm, initial, sems.at[len(copies)])

    @pl.when(first)
    def _():
        given.start()

    for copy in copies:
        copy.wait()
    enc_out[...] = reordered(enc[...])
    coarse_out[...] = coarse_matrix(rate[...], coup[...])
    for f in range(count):
        for a in range(starts.shape[1] // DOWN):
            parts = split_columns(chunks_of(starts, f, 8 * a))
            for q, part in enumerate(parts):
                own_out[f, q, 8 * a : 8 * a + 8, :] = part
            put_blocks(offset_out, f, a, [-part for part in parts])

    @pl.when(first)
    def _():
        given.wait()
        for f in range(count):
            for a in range(starts.shape[1] // DOWN):
                parts = split_columns(chunks_of(initial, f, 8 * a))
                mine = [own_out[f, q, 8 * a : 8 * a + 8, :] for q in range(8)]
                put_blocks(offset_out, f, a, [part - m for part, m in zip(parts, mine)])


def powers_kernel(inner, order, dec, matrix, total_out, near_out, far_out, held, decoded_held):
    lat = matrix.shape[0]
    inside = lax.axis_index("cuts") % inner
    coarse = matrix[...]
    powers = [identity(lat), coarse]
    for k in range(2, inner + 1):
        powers.append(dot_full(powers[k // 2], powers[k - k // 2]))
    for k, power in enumerate(powers):
        held[k] = power
    weight = reordered(dec[...]).T
    decoded = [weight]
    for d in range(1, inner):
        place = inside ^ d
        part = dot_full(weight, held[jnp.maximum(inside - place, 0)])
        decoded.append(jnp.where(place < inside, part, 0.0))
    near_out[...] = jnp.concatenate(decoded, axis=1)
    total_out[...] = jnp.concatenate([held[inner - 1 - (inside ^ d)] for d in range(inner)], axis=1)
    group = lax.axis_index("cuts") // inner
    far = [dot_full(weight, held[inside + 1])]
    for k in range(2, len(order) + 1):
        far.append(dot_full(far[-1], powers[inner]))
    for k, part in enumerate(far):
        decoded_held[k] = part
    picked = [decoded_held[jnp.maximum(group - 1 - (group ^ d), 0)] for d in order]
    far_out[...] = jnp.concatenate(picked, axis=1)


class Padded:
    def __init__(self, ref, reps):
        self.ref = ref
        self.reps = reps

    def put_cell(self, r, q, *cells):
        ref, reps = self.ref, self.reps
        for field, value in enumerate(cells):
            ref[field, r + 2, q + 2] = value
            if r < 2:
                ref[field, r + reps + 2, q + 2] = pltpu.roll(value, 7, 0)
            if r >= reps - 2:
                ref[field, r - reps + 2, q + 2] = pltpu.roll(value, 1, 0)
            if q < 2:
                ref[field, r + 2, q + 10] = pltpu.roll(value, LANES - 1, 1)
            if q >= 6:
                ref[field, r + 2, q - 6] = pltpu.roll(value, 1, 1)

    def cell(self, field, r, q):
        return self.ref[field, r + 2, q + 2]


def slope(before_2, before, after, after_2):
    return 8.0 * (after - before) - (after_2 - before_2)


def stage(base, now, reps, alpha, beta, gamma, put):
    scale = gamma / 12.0
    turn = 12.0 * FCOR

    def column(r, q):
        height, along_c, along_r = (now.cell(f, r, q) for f in range(3))
        return height, along_c, along_r, along_c + height * along_c

    for r in range(reps):
        window = [column(r, q) for q in range(-2, 2)]
        for q in range(8):
            window.append(column(r, q + 2))
            height, along_c, along_r, _ = window[2]
            cols = [slope(*(window[k][f] for k in (0, 1, 3, 4))) for f in range(4)]
            near = [[now.cell(f, r + k, q) for f in range(3)] for k in (-2, -1, 1, 2)]
            for cells in near:
                cells.append(cells[2] + cells[0] * cells[2])
            rows = [slope(*(cells[f] for cells in near)) for f in range(4)]
            d_height = cols[3] + rows[3]
            d_colvel = along_c * cols[1] + along_r * (rows[1] - turn) + cols[0]
            d_rowvel = along_c * (cols[2] + turn) + along_r * rows[2] + rows[0]
            new = []
            for f, (mine, d) in enumerate(((height, d_height), (along_c, d_colvel), (along_r, d_rowvel))):
                total = beta * mine if beta != 1.0 else mine
                if alpha:
                    total = total + alpha * base.cell(f, r, q)
                new.append(total - scale * d)
            put(r, q, *new)
            del window[0]


def fine_kernel(own, other, offset, enc, coarse, finals_out, g_out, t_out, rows_buf, buf_a, buf_b, buf_c):
    local_rows = own.shape[2]
    ext = local_rows + other.shape[1]
    reps = ext // 8
    groups = local_rows // DOWN
    for f in range(3):
        for q in range(8):
            rows_buf[f, q, 0:local_rows, :] = own[f, q, :, :]
        for tile in range(other.shape[1] // 8):
            parts = split_columns(chunks_of(other, f, 8 * tile))
            for q in range(8):
                rows_buf[f, q, local_rows + 8 * tile : local_rows + 8 * tile + 8, :] = parts[q]
    t_part = dot3(coarse[...], dot3(enc[...], side_by_side(offset)))
    t_out[...] = t_part
    state, second, third = Padded(buf_a, reps), Padded(buf_b, reps), Padded(buf_c, reps)
    for r in range(reps):
        for q in range(8):
            state.put_cell(r, q, *(rows_buf[f, q, pl.ds(r, 8, stride=reps), :] for f in range(3)))

    def finish(r, q, *cells):
        for f in range(3):
            rows_buf[f, q, pl.ds(r, 8, stride=reps), :] = cells[f]

    for step in range(FINE_STEPS):
        stage(None, state, reps, 0.0, 1.0, TSTEP, second.put_cell)
        stage(state, second, reps, 0.75, 0.25, 0.25 * TSTEP, third.put_cell)
        last = step + 1 == FINE_STEPS
        stage(state, third, reps, 1.0 / 3.0, 2.0 / 3.0, 2.0 / 3.0 * TSTEP, finish if last else state.put_cell)
    ends = []
    for a in range(groups):
        parts = [rows_buf[f, q, 8 * a : 8 * a + 8, :] for f in range(3) for q in range(8)]
        ends.append(jnp.concatenate(parts, axis=0))
        finals_out[a] = ends[a]
    g_out[...] = dot3(enc[...], jnp.concatenate(ends, axis=1)) + t_part


def weighted_kernel(*refs):
    *parts, weights, out = refs
    out[...] = dot3(weights[...], jnp.concatenate([part[...] for part in parts], axis=0))


def base_kernel(finals, *refs):
    *parts, weights, out_hbm, out, sems = refs
    change = dot3(weights[...], jnp.concatenate([part[...] for part in parts], axis=0))
    copies = []
    for a in range(finals.shape[0]):
        rows = pl.ds(8 * a, 8)
        for f in range(3):
            places = [slice(64 * f + 8 * q, 64 * f + 8 * q + 8) for q in range(8)]
            joined = join_columns([finals[a, k, :] + change[k, LANES * a : LANES * (a + 1)] for k in places])
            for j, chunk in enumerate(joined):
                out[f, 8 * a : 8 * a + 8, LANES * j : LANES * (j + 1)] = chunk
            copies.append(pltpu.make_async_copy(out.at[f, rows], out_hbm.at[0, f, rows], sems.at[3 * a + f]))
            copies[-1].start()
    for copy in copies:
        copy.wait()


def output_kernel(inner, order, base, *refs):
    *totals, weights, _, out_hbm, joined_out, sems = refs
    group = lax.axis_index("cuts") // inner

    @pl.when(group > 0)
    def _():
        taken = [jnp.where((group ^ d) < group, part[...], 0.0) for d, part in zip(order, totals)]
        change = dot3(weights[...], jnp.concatenate(taken, axis=0))
        copies = []
        for a in range(base.shape[1] // DOWN):
            rows = pl.ds(8 * a, 8)
            for f in range(3):
                places = [slice(64 * f + 8 * q, 64 * f + 8 * q + 8) for q in range(8)]
                joined = join_columns([change[k, LANES * a : LANES * (a + 1)] for k in places])
                for j, chunk in enumerate(joined):
                    cells = (f, slice(8 * a, 8 * a + 8), slice(LANES * j, LANES * (j + 1)))
                    joined_out[cells] = base[cells] + chunk
                copies.append(pltpu.make_async_copy(joined_out.at[f, rows], out_hbm.at[0, f, rows], sems.at[3 * a + f]))
                copies[-1].start()
        for copy in copies:
            copy.wait()


def call(kernel, shapes, inputs, scratch=(), flops=0, inside=None, outside=None, aliases={}):
    return pl.pallas_call(
        kernel,
        out_shape=[jax.ShapeDtypeStruct(s, F32) for s in shapes],
        in_specs=inside or [VMEM] * len(inputs),
        out_specs=outside or [VMEM] * len(shapes),
        scratch_shapes=list(scratch),
        input_output_aliases=aliases,
        compiler_params=pltpu.CompilerParams(vmem_limit_bytes=40 * 1024 * 1024),
        cost_estimate=pl.CostEstimate(
            flops=flops, bytes_accessed=sum(4 * x.size for x in inputs), transcendentals=0
        ),
    )(*inputs)


def neighbour_rows(state):
    count = lax.axis_size("row")
    rows = state.shape[1]
    if count == 1:
        return jnp.concatenate([state[:, :HALO], state[:, rows - HALO :]], axis=1)
    forward = [(i, (i + 1) % count) for i in range(count)]
    backward = [((i + 1) % count, i) for i in range(count)]
    if count == 2 and rows <= 2 * HALO:
        return lax.ppermute(state, "row", forward)
    below = lax.ppermute(state[:, :HALO], "row", backward)
    above = lax.ppermute(state[:, rows - HALO :], "row", forward)
    return jnp.concatenate([below, above], axis=1)


def swapped(value, distance):
    return lax.ppermute(value, "cuts", [(i, i ^ distance) for i in range(lax.axis_size("cuts"))])


def local(starts, initial, encode_weight, decode_weight, latent_rate, coupling):
    lat = coupling.shape[0]
    state = starts[0]
    rows = state.shape[1]
    groups = rows // DOWN
    wide = groups * LANES
    size = encode_weight.shape[1]
    slices = lax.axis_size("cuts")
    inner = 1 << (slices.bit_length() // 2)
    outer = slices // inner
    order = tuple(range(1, outer))
    rate = latent_rate.reshape(1, lat)
    other = neighbour_rows(state)
    given = (state, initial, encode_weight, rate, coupling)
    own, offset, enc, coarse = call(
        split_kernel,
        [(3, 8, rows, LANES), (groups, size, LANES), encode_weight.shape, (lat, lat)],
        [pltpu.with_memory_space_constraint(x, pltpu.HBM) for x in given],
        [pltpu.VMEM(x.shape, F32) for x in given] + [pltpu.SemaphoreType.DMA((7,))],
        flops=100_000_000,
        inside=[pl.BlockSpec(memory_space=pl.ANY)] * len(given),
    )
    reps = (rows + other.shape[1]) // 8
    pad = pltpu.VMEM((3, reps + 4, 12, 8, LANES), F32)
    finals, g_part, t_part = call(
        fine_kernel,
        [(groups, size, LANES), (lat, wide), (lat, wide)],
        [own, other, offset, enc, coarse],
        [pltpu.VMEM((3, 8, 8 * reps, LANES), F32), pad, pad, pad],
        flops=400_000_000,
    )
    parts = [swapped(g_part, d) for d in range(1, inner)]
    to_total, to_near, to_far = call(
        functools.partial(powers_kernel, inner, order),
        [(lat, inner * lat), (size, inner * lat), (size, (outer - 1) * lat)],
        [decode_weight.T, coarse],
        [pltpu.VMEM((inner + 1, lat, lat), F32), pltpu.VMEM((outer - 1, size, lat), F32)],
        flops=50_000_000,
    )
    (total,) = call(weighted_kernel, [(lat, wide)], [g_part, *parts, to_total], flops=50_000_000)
    totals = [swapped(total, inner * d) for d in order]
    hbm = pl.BlockSpec(memory_space=pltpu.HBM)
    tiles = pltpu.SemaphoreType.DMA((3 * groups,))
    result = (1, *state.shape)
    near_result, base = call(
        base_kernel,
        [result, state.shape],
        [finals, t_part, *parts, to_near],
        [tiles],
        flops=50_000_000,
        outside=[hbm, VMEM],
    )
    (out,) = call(
        functools.partial(output_kernel, inner, order),
        [result],
        [base, *totals, to_far, near_result],
        [pltpu.VMEM(state.shape, F32), tiles],
        flops=50_000_000,
        inside=[VMEM] * (outer + 1) + [hbm],
        outside=[hbm],
        aliases={outer + 1: 0},
    )
    return out


def solution(mesh):
    return jax.shard_map(
        local,
        mesh=mesh,
        in_specs=(P("cuts", None, "row", None), P(None, "row", None), P(), P(), P(), P()),
        out_specs=P("cuts", None, "row", None),
        check_vma=False,
    )
```
